512 devices in a mesh: lat: 16 (over x_hi, y, core), lon: 32 (over z, x_lo).
Axes of the slice: x: 4 (x_hi: 2, x_lo: 2; x = x_hi * 2 + x_lo), y: 4, z: 16, core: 2. Of those that a mesh axis runs over, the one named last changes fastest.
Arguments:
- tokens: bfloat16 [2, 192, 384, 1024], P(None, 'lat', 'lon'), may hold values from -96 to 96
- qkv_weight: bfloat16 [1024, 1536], P('lon'), may hold values from -0.1875 to 0.1875
- out_weight: bfloat16 [512, 1024], P('lon'), may hold values from -1 to 1
- norm_gain: float32 [1024], replicated, may hold values from 0.1 to 1.9
- norm_bias: float32 [1024], replicated, may hold values from -3 to 3
- mixed_grad: bfloat16 [2, 192, 384, 1024], P(None, 'lat', 'lon'), may hold values from -6 to 6
Outputs:
- mixed: bfloat16 [2, 192, 384, 1024], P(None, 'lat', 'lon')
- token_grad: bfloat16 [2, 192, 384, 1024], P(None, 'lat', 'lon')
The draws below stay inside these ranges and needn't reach their ends.
All inputs are finite; a program needn't handle non-finite values.
Results may differ from the reference program's by a relative error of at most 0.014.
The reference program's roundings to bfloat16 on the way count: a program that leaves them out, or rounds other values in their place, can miss the bound.
Values may be sent and summed in bfloat16 or wider, within the bound.
A program may use at most 64 MiB of HBM per device.

```python
import math
from functools import partial
import jax
import jax.numpy as jnp
from jax import lax

D = 1024
HEADS = 8
HEAD_DIM = 64
LEV = 2
WIN = 12
INNER = 512
HALF = 6
NLAT = 192
NLON = 384


def draw_tokens(key, part):
    key = jax.random.fold_in(key, 11)
    subkeys = jax.random.split(key, 2)
    shape = (LEV, NLAT, NLON, D)
    token_scale = jnp.exp(jax.random.uniform(subkeys[0], (LEV, NLAT, NLON, 1), jnp.float32, math.log(0.4), math.log(4.0)))
    field_values = jax.random.normal(subkeys[1], shape, jnp.float32) * token_scale
    return jnp.clip(field_values, -96.0, 96.0).astype(jnp.bfloat16)


def draw_out_weight(key, part):
    key = jax.random.fold_in(key, 23)
    subkeys = jax.random.split(key, 2)
    column_scale = jnp.exp(jax.random.uniform(subkeys[0], (1, D), jnp.float32, math.log(0.3), math.log(3.0)))
    values = jnp.clip(jax.random.normal(subkeys[1], (INNER, D), jnp.float32), -6.0, 6.0)
    return jnp.clip(values * column_scale * INNER ** (-0.5), -1.0, 1.0).astype(jnp.bfloat16)


def block_levels(own_key, shape, pieces, least, largest):
    def one(dim, parts):
        heights = jax.random.uniform(jax.random.fold_in(jax.random.fold_in(own_key, 6), dim), (parts,), jnp.float32, least / len(pieces), largest / len(pieces))
        return jnp.repeat(jnp.exp(heights), shape[dim] // parts).reshape((-1,) + (1,) * (len(shape) - dim - 1))

    gain = one(*pieces[0])
    for cut in pieces[1:]:
        gain = gain * one(*cut)
    return gain


def bell_draw(rng, dims, scale, reach, cuts=(), kind=jnp.bfloat16):
    level = block_levels(rng, dims, cuts, -0.22, 0.18) if cuts else 1.0
    drawn = jax.random.normal(rng, dims, jnp.float32) * scale * level
    return jnp.minimum(jnp.maximum(drawn, -reach), reach).astype(kind)


def setup_inputs(seed: int = 0) -> dict:
    keys = jax.random.split(jax.random.key(seed), 7)
    tokens = draw_tokens(jax.random.fold_in(keys[6], 71), 0)
    qkv_weight = bell_draw(keys[1], (D, 3 * INNER), D ** -0.5, 0.1875, ((0, 32),))
    out_weight = draw_out_weight(jax.random.fold_in(keys[6], 71), 0)
    norm_gain = jnp.clip(1.0 + 0.18 * jax.random.normal(keys[3], (D,), jnp.float32), 0.1, 1.9)
    norm_bias = bell_draw(keys[4], (D,), 0.5, 3.0, (), jnp.float32)
    mixed_grad = bell_draw(keys[5], (LEV, NLAT, NLON, D), 1.0, 6.0, ((1, 16), (2, 32)))
    return dict(tokens=tokens, qkv_weight=qkv_weight, out_weight=out_weight, norm_gain=norm_gain, norm_bias=norm_bias, mixed_grad=mixed_grad)


norm_eps = 1e-05

def split_windows(grid_field):
    levels, lat_total, lon_total, feature = grid_field.shape
    blocks = grid_field.reshape(levels, lat_total // WIN, WIN, lon_total // WIN, WIN, feature)
    blocks = blocks.transpose(1, 3, 0, 2, 4, 5)
    return blocks.reshape(lat_total // WIN, lon_total // WIN, levels * WIN * WIN, feature)

def join_windows(blocks):
    band_count, window_count, window_size, feature = blocks.shape
    grid_field = blocks.reshape(band_count, window_count, LEV, WIN, WIN, feature).transpose(2, 0, 3, 1, 4, 5)
    return grid_field.reshape(LEV, band_count * WIN, window_count * WIN, feature)

def band_pass(weights, inputs):
    qkv_weight, out_weight, norm_gain, norm_bias = weights
    windows, grads, band_index = inputs
    window_count, window_size, width = windows.shape
    factor = HEAD_DIM ** (-0.5)
    lat_rows = band_index * WIN + jnp.arange(WIN, dtype=jnp.int32)
    wrapped = lat_rows >= NLAT - HALF
    wrapped = jnp.broadcast_to(wrapped[None, :, None], (LEV, WIN, WIN)).reshape(window_size)
    same_side = wrapped[:, None] == wrapped[None, :]
    packed = jnp.dot(windows.reshape(-1, width), qkv_weight, preferred_element_type=jnp.float32)
    packed = packed.astype(jnp.bfloat16).reshape(window_count, window_size, 3, HEADS, HEAD_DIM)
    query_heads = packed[:, :, 0].astype(jnp.float32)
    key_heads = packed[:, :, 1].astype(jnp.float32)
    value_heads = packed[:, :, 2].astype(jnp.float32)
    scores = jnp.einsum('wqhe,wkhe->whqk', query_heads, key_heads) * factor
    scores = jnp.where(same_side, scores, -jnp.inf)
    highest = lax.optimization_barrier(jnp.max(scores, axis=-1, keepdims=True))
    raised = jnp.exp(scores - highest)
    probs = (raised / lax.optimization_barrier(jnp.sum(raised, axis=-1, keepdims=True))).astype(jnp.bfloat16)
    probs_f = probs.astype(jnp.float32)
    heads = jnp.einsum('whqk,wkhe->wqhe', probs_f, value_heads).astype(jnp.bfloat16)
    attn = jnp.dot(heads.reshape(-1, INNER), out_weight, preferred_element_type=jnp.float32).astype(jnp.bfloat16)
    attn_f = attn.astype(jnp.float32)
    centered = attn_f - lax.optimization_barrier(jnp.mean(attn_f, axis=-1, keepdims=True))
    inverse = lax.rsqrt(lax.optimization_barrier(jnp.mean(centered * centered, axis=-1, keepdims=True)) + norm_eps)
    normed = centered * inverse
    flat_tokens = windows.reshape(-1, width).astype(jnp.float32)
    mixed = (flat_tokens + normed * norm_gain + norm_bias).astype(jnp.bfloat16)
    scaled = grads.reshape(-1, width).astype(jnp.float32) * norm_gain
    attn_grad = (scaled - lax.optimization_barrier(jnp.mean(scaled, axis=-1, keepdims=True)) - normed * lax.optimization_barrier(jnp.mean(scaled * normed, axis=-1, keepdims=True))) * inverse
    attn_grad = attn_grad.astype(jnp.bfloat16)
    heads_grad = jnp.dot(attn_grad, out_weight.T, preferred_element_type=jnp.float32).astype(jnp.bfloat16)
    heads_grad = heads_grad.reshape(window_count, window_size, HEADS, HEAD_DIM).astype(jnp.float32)
    prob_grad = jnp.einsum('wqhe,wkhe->whqk', heads_grad, value_heads)
    value_grad = jnp.einsum('whqk,wqhe->wkhe', probs_f, heads_grad).astype(jnp.bfloat16)
    score_grad = probs_f * (prob_grad - lax.optimization_barrier(jnp.sum(probs_f * prob_grad, axis=-1, keepdims=True))) * factor
    score_grad = score_grad.astype(jnp.bfloat16).astype(jnp.float32)
    query_grad = jnp.einsum('whqk,wkhe->wqhe', score_grad, key_heads).astype(jnp.bfloat16)
    key_grad = jnp.einsum('whqk,wqhe->wkhe', score_grad, query_heads).astype(jnp.bfloat16)
    packed_grad = jnp.stack([query_grad, key_grad, value_grad], axis=2).reshape(-1, 3 * INNER)
    shifted_grad = jnp.dot(packed_grad, qkv_weight.T, preferred_element_type=jnp.float32).astype(jnp.bfloat16)
    token_grad = (grads.reshape(-1, width).astype(jnp.float32) + shifted_grad.astype(jnp.float32)).astype(jnp.bfloat16)
    return (mixed.reshape(window_count, window_size, width), token_grad.reshape(window_count, window_size, width))

def reference(tokens, qkv_weight, out_weight, norm_gain, norm_bias, mixed_grad):
    shifted = jnp.roll(tokens, (-HALF, -HALF), axis=(1, 2))
    grad_shifted = jnp.roll(mixed_grad, (-HALF, -HALF), axis=(1, 2))
    windows = split_windows(shifted)
    grads = split_windows(grad_shifted)
    bands = jnp.arange(windows.shape[0], dtype=jnp.int32)
    worker = partial(band_pass, (qkv_weight, out_weight, norm_gain, norm_bias))
    mixed_w, grad_w = lax.map(worker, (windows, grads, bands))
    mixed = jnp.roll(join_windows(mixed_w), (HALF, HALF), axis=(1, 2))
    token_grad = jnp.roll(join_windows(grad_w), (HALF, HALF), axis=(1, 2))
    return (mixed, token_grad)
```

```python
import functools

import jax
import jax.numpy as jnp
from jax import lax
from jax.experimental import pallas as pl
from jax.experimental.pallas import tpu as pltpu
from jax.sharding import PartitionSpec as P

MESH = pl.DeviceIdType.MESH
BF = jnp.bfloat16
F32 = jnp.float32

D = 1024
HEADS = 8
HEAD_DIM = 64
LEV = 2
WIN = 12
INNER = 512
HALF = 6
TOK = LEV * WIN * WIN
QUARTER = TOK // 4
PIECE = 80
GROUP = 4
GW = GROUP * HEAD_DIM
CHUNK = 32
STEPS = TOK // CHUNK
LANES = GROUP * CHUNK
EPS = 1e-05

SENT = (64, 144, 208)


def nt(a, b):
    return lax.dot_general(a, b, (((1,), (1,)), ((), ())), preferred_element_type=F32)


def nn(a, b):
    return lax.dot_general(a, b, (((1,), (0,)), ((), ())), preferred_element_type=F32)


def tn(a, b):
    return lax.dot_general(a, b, (((0,), (0,)), ((), ())), preferred_element_type=F32)


def ds(start, size):
    return pl.ds(pl.multiple_of(start, size), size)


def kernel(
    n_lat, n_lon,
    t_ref, g_ref, wq_ref, wo_ref, gain_ref, bias_ref,
    m_out, d_out,
    wqf, wof, land_t, land_g, xw, gw, packed, heads, attn, agrad, hgrad, pgrad,
    pt, dst, qblk, doblk, mixed, tgrad,
    own_sem, zs, zr, xs, xr, ss, sr, hs, hr,
):
    lat, lon = lax.axis_index("lat"), lax.axis_index("lon")
    nz = n_lon // 2
    ns = nz // 2
    rq, ro = D // n_lon, INNER // n_lon
    core, par, z = lax.rem(lat, 2), lax.rem(lon, 2), lon // 2
    lat_lo, lat_hi = lax.rem(lat + n_lat - 1, n_lat), lax.rem(lat + 1, n_lat)
    lon_lo, lon_hi = lax.rem(lon + n_lon - 1, n_lon), lax.rem(lon + 1, n_lon)
    sib = (lat + 1 - 2 * core, lon)
    up = (lat, lax.rem(lon + 2, n_lon))
    down = (lat, lax.rem(lon + n_lon - 2, n_lon))
    differ = lax.rem(par + core, 2)
    across = lon + 1 - 2 * par
    x_to = (lax.rem(lat + differ * (n_lat // 2), n_lat), across)
    x_from = (lax.rem(lat + (1 - differ) * (n_lat // 2), n_lat), across)
    west, north, diag = (lat, lon_lo), (lat_lo, lon), (lat_lo, lon_lo)
    east, south, far = (lat, lon_hi), (lat_hi, lon), (lat_hi, lon_hi)

    barrier = pltpu.get_barrier_semaphore()
    met = (sib, up, down, x_to, x_from, west, north, diag, east, south, far)
    for who in met:
        pl.semaphore_signal(barrier, inc=1, device_id=who, device_id_type=MESH)
    pl.semaphore_wait(barrier, len(met))

    def remote(src, dst, send, recv, who):
        return pltpu.make_async_remote_copy(
            src_ref=src, dst_ref=dst, send_sem=send, recv_sem=recv, device_id=who, device_id_type=MESH
        )

    def halo_in(field, src, land):
        return [
            remote(src.at[pl.ds(SENT[k], PIECE), :], land.at[k], hs.at[field * 3 + k], hr.at[field * 3 + k], who)
            for k, who in enumerate((west, north, diag))
        ]

    in_t = halo_in(0, t_ref, land_t)
    in_g = halo_in(1, g_ref, land_g)
    for copy in in_t:
        copy.start()

    def piece(kind, zq, p, c):
        if kind == 0:
            return wqf.at[ds((zq * 2 + p) * rq + c * (rq // 2), rq // 2), :]
        return wof.at[ds((zq * 2 + p) * ro, ro), ds(c * (D // 2), D // 2)]

    def own_piece(kind):
        if kind == 0:
            return wq_ref.at[ds(core * (rq // 2), rq // 2), :]
        return wo_ref.at[:, ds(core * (D // 2), D // 2)]

    def z_copy(kind, way, s, zq, src=None):
        dst = piece(kind, zq, par, core)
        i = (way * (ns + 1) + s) * 2 + kind
        return remote(dst if src is None else src, dst, zs.at[i], zr.at[i], (up, down)[way])

    def x_copy(kind, d, zq, p, src=None):
        dst = piece(kind, zq, p, core)
        i = d * 2 + kind
        return remote(dst if src is None else src, dst, xs.at[i], xr.at[i], x_to)

    def s_copy(kind, other, d, zq, c):
        ref = piece(kind, zq, lax.rem(par + other, 2), c)
        i = (other * nz + d) * 2 + kind
        return remote(ref, ref, ss.at[i], sr.at[i], sib)

    def ahead(zq, s):
        return lax.rem(zq + s, nz)

    def behind(zq, s):
        return lax.rem(zq - s + nz, nz)

    local = [
        pltpu.make_async_copy(wq_ref, wqf.at[ds(lon * rq, rq), :], own_sem.at[0]),
        pltpu.make_async_copy(wo_ref, wof.at[ds(lon * ro, ro), :], own_sem.at[1]),
    ]
    for kind in (0, 1):
        src = own_piece(kind)
        z_copy(kind, 0, 1, z, src).start()
        if ns > 1:
            z_copy(kind, 1, 1, z, src).start()
        x_copy(kind, 0, z, par, src).start()
    for copy in local:
        copy.start()
    for copy in in_g:
        copy.start()

    def z_arrive(kind, way, s, last):
        zq, d = (behind(z, s), s) if way == 0 else (ahead(z, s), nz - s)
        z_copy(kind, way, s, zq).wait_recv()
        if not last:
            z_copy(kind, way, s + 1, zq).start()
        x_copy(kind, d, zq, par).start()
        s_copy(kind, 0, d, zq, core).start()

    def x_arrive(kind, d):
        zq = behind(z, d)
        x_copy(kind, d, zq, 1 - par).wait_recv()
        s_copy(kind, 1, d, zq, core).start()

    def z_step(s, up_last, down_in, down_last):
        for kind in (0, 1):
            z_arrive(kind, 0, s, up_last)
            if down_in:
                z_arrive(kind, 1, s, down_last)

    def x_step(s, both):
        for kind in (0, 1):
            x_arrive(kind, s)
            if both:
                x_arrive(kind, nz - s)

    def fixed_step(s):
        z_step(s, s == ns, s < ns, s == ns - 1)
        x_step(s - 1, s > 1)

    fixed_step(1)
    if ns > 3:
        def middle(s, carry):
            z_step(s, False, True, False)
            x_step(s - 1, True)
            return carry

        lax.fori_loop(2, ns - 1, middle, 0)
    for s in range(max(2, ns - 1), ns + 1):
        fixed_step(s)
    x_step(ns, False)

    def assemble(own, land, dst):
        row = lax.broadcasted_iota(jnp.int32, (16, D), 0)
        dst[0:64, :] = own[0:64, :]
        dst[64:80, :] = jnp.where(row < 8, own[64:80, :].astype(F32), land[0, 0:16, :].astype(F32)).astype(BF)
        dst[80:144, :] = land[0, 16:80, :]
        dst[144:208, :] = land[1, 0:64, :]
        dst[208:224, :] = jnp.where(row < 8, land[1, 64:80, :].astype(F32), land[2, 0:16, :].astype(F32)).astype(BF)
        dst[224:288, :] = land[2, 16:80, :]

    for copy in in_t:
        copy.wait_recv()
    assemble(t_ref, land_t, xw)

    def s_wait(d, carry):
        for kind in (0, 1):
            s_copy(kind, 0, d, behind(z, d), 1 - core).wait_recv()
            s_copy(kind, 1, d, behind(z, d), 1 - core).wait_recv()
        return carry

    for kind in (0, 1):
        s_copy(kind, 1, 0, z, 1 - core).wait_recv()
    lax.fori_loop(1, nz, s_wait, 0)
    for copy in local:
        copy.wait()

    def project(n, carry):
        cols = ds(n * 256, 256)
        packed[:, cols] = nn(xw[...], wqf[:, cols]).astype(BF)
        return carry

    lax.fori_loop(0, 3 * INNER // 256, project, 0)

    lane_head = lax.broadcasted_iota(jnp.int32, (CHUNK, GW), 1) // HEAD_DIM
    head_mask = [(lane_head == h).astype(F32).astype(BF) for h in range(GROUP)]
    banned = jnp.where(lat == n_lat - 1, -1e30, 0.0).astype(F32)
    lane_query = lax.rem(lax.broadcasted_iota(jnp.int32, (1, LANES), 1), CHUNK)

    def spread(rows):
        return jnp.concatenate([rows * m for m in head_mask], axis=0)

    def gather_heads(wide):
        out = wide[0:CHUNK, :]
        for h in range(1, GROUP):
            out = jnp.where(lane_head == h, wide[h * CHUNK : (h + 1) * CHUNK, :], out)
        return out

    for g in range(HEADS // GROUP):
        q_at, k_at, v_at = g * GW, INNER + g * GW, 2 * INNER + g * GW

        def forward(c, carry, g=g, q_at=q_at, k_at=k_at, v_at=v_at):
            rows, cols = ds(c * CHUNK, CHUNK), ds(c * LANES, LANES)
            q = spread(packed[rows, q_at : q_at + GW])
            qblk[g, cols, :] = q
            s = nt(packed[:, k_at : k_at + GW], q)
            side = ((c * CHUNK + lane_query) >= TOK // 2).astype(F32)
            s = jnp.concatenate([s[: TOK // 2] + side * banned, s[TOK // 2 :] + (1.0 - side) * banned], axis=0)
            top = jnp.max(s, axis=0, keepdims=True)
            e = jnp.exp((s - top) * (HEAD_DIM ** -0.5))
            p = (e * (1.0 / jnp.sum(e, axis=0, keepdims=True))).astype(BF)
            pt[g, :, cols] = p
            o = tn(p, packed[:, v_at : v_at + GW])
            heads[rows, q_at : q_at + GW] = gather_heads(o).astype(BF)
            return carry

        lax.fori_loop(0, STEPS, forward, 0)

    def out_project(n, carry):
        cols = ds(n * 256, 256)
        attn[:, cols] = nn(heads[...], wof[:, cols]).astype(BF)
        return carry

    lax.fori_loop(0, D // 256, out_project, 0)

    for copy in in_g:
        copy.wait_recv()
    assemble(g_ref, land_g, gw)

    def norm(c, carry):
        rows = ds(c * CHUNK, CHUNK)
        a = attn[rows, :].astype(F32)
        centered = a - jnp.mean(a, axis=-1, keepdims=True)
        inverse = lax.rsqrt(jnp.mean(centered * centered, axis=-1, keepdims=True) + EPS)
        normed = centered * inverse
        gain = gain_ref[...]
        mixed[rows, :] = (xw[rows, :].astype(F32) + normed * gain + bias_ref[...]).astype(BF)
        scaled = gw[rows, :].astype(F32) * gain
        back = scaled - jnp.mean(scaled, axis=-1, keepdims=True)
        back = back - normed * jnp.mean(scaled * normed, axis=-1, keepdims=True)
        agrad[rows, :] = (back * inverse).astype(BF)
        return carry

    lax.fori_loop(0, TOK // CHUNK, norm, 0)

    def halo_out(field, src, out):
        copies = [
            remote(
                src.at[pl.ds(SENT[k], PIECE), :], out.at[k + 1],
                hs.at[(field + 2) * 3 + k], hr.at[(field + 2) * 3 + k], who,
            )
            for k, who in enumerate((east, south, far))
        ]
        keep = pltpu.make_async_copy(src.at[pl.ds(0, PIECE), :], out.at[0], own_sem.at[2 + field])
        for copy in copies:
            copy.start()
        keep.start()
        return copies, keep

    out_m = halo_out(0, mixed, m_out)

    def back_project(n, carry):
        cols = ds(n * 256, 256)
        hgrad[:, cols] = nt(agrad[...], wof[cols, :]).astype(BF)
        return carry

    lax.fori_loop(0, INNER // 256, back_project, 0)

    for g in range(HEADS // GROUP):
        q_at, k_at, v_at = g * GW, INNER + g * GW, 2 * INNER + g * GW

        def backward(c, carry, g=g, q_at=q_at, k_at=k_at, v_at=v_at):
            rows, cols = ds(c * CHUNK, CHUNK), ds(c * LANES, LANES)
            do = spread(hgrad[rows, q_at : q_at + GW])
            doblk[cols, :] = do
            dp = nt(packed[:, v_at : v_at + GW], do)
            p = pt[g, :, cols].astype(F32)
            total = jnp.sum(p * dp, axis=0, keepdims=True)
            dscore = (p * (dp - total) * (HEAD_DIM ** -0.5)).astype(BF)
            dst[:, cols] = dscore
            dq = tn(dscore, packed[:, k_at : k_at + GW])
            pgrad[rows, q_at : q_at + GW] = gather_heads(dq).astype(BF)
            return carry

        lax.fori_loop(0, STEPS, backward, 0)
        pgrad[:, v_at : v_at + GW] = nn(pt[g], doblk[...]).astype(BF)
        pgrad[:, k_at : k_at + GW] = nn(dst[...], qblk[g]).astype(BF)

    def unproject(n, carry):
        cols = ds(n * 256, 256)
        sg = nt(pgrad[...], wqf[cols, :]).astype(BF).astype(F32)
        tgrad[:, cols] = (gw[:, cols].astype(F32) + sg).astype(BF)
        return carry

    lax.fori_loop(0, D // 256, unproject, 0)
    out_d = halo_out(1, tgrad, d_out)

    for kind in (0, 1):
        z_copy(kind, 0, 1, z).wait_send()
        x_copy(kind, 0, z, par).wait_send()
        s_copy(kind, 1, 0, z, core).wait_send()

    def sent(d, carry):
        for kind in (0, 1):
            x_copy(kind, d, behind(z, d), par).wait_send()
            s_copy(kind, 0, d, behind(z, d), core).wait_send()
            s_copy(kind, 1, d, behind(z, d), core).wait_send()
        return carry

    lax.fori_loop(1, nz, sent, 0)

    def sent_z(s, carry):
        for kind in (0, 1):
            z_copy(kind, 0, s, behind(z, s - 1)).wait_send()
            z_copy(kind, 1, s - 1, ahead(z, s - 2)).wait_send()
        return carry

    lax.fori_loop(2, ns + 1, sent_z, 0)
    for copy in in_t + in_g:
        copy.wait_send()
    for copies, keep in (out_m, out_d):
        keep.wait()
        for copy in copies:
            copy.wait()


def per_device(n_lat, n_lon, tokens, qkv_weight, out_weight, norm_gain, norm_bias, mixed_grad):
    def quarters(field):
        cut = field.reshape(LEV, 2, HALF, 2, HALF, D)
        return jnp.concatenate(
            [cut[:, i, :, j].reshape(QUARTER, D) for i, j in ((1, 1), (1, 0), (0, 1), (0, 0))], axis=0
        )

    def join(pieces):
        own, left, above, corner = (
            pieces[k, 8 * (k % 2) : 8 * (k % 2) + QUARTER].reshape(LEV, HALF, HALF, D) for k in range(4)
        )
        return jnp.concatenate(
            [jnp.concatenate([corner, above], axis=2), jnp.concatenate([left, own], axis=2)], axis=1
        )

    nz = n_lon // 2
    ns = nz // 2
    vmem = pl.BlockSpec(memory_space=pltpu.VMEM)
    m_out, d_out = pl.pallas_call(
        functools.partial(kernel, n_lat, n_lon),
        out_shape=[jax.ShapeDtypeStruct((4, PIECE, D), BF)] * 2,
        in_specs=[vmem] * 6,
        out_specs=[pl.BlockSpec(memory_space=pl.ANY)] * 2,
        scratch_shapes=[
            pltpu.VMEM((D, 3 * INNER), BF),
            pltpu.VMEM((INNER, D), BF),
            pltpu.VMEM((3, PIECE, D), BF),
            pltpu.VMEM((3, PIECE, D), BF),
            pltpu.VMEM((TOK, D), BF),
            pltpu.VMEM((TOK, D), BF),
            pltpu.VMEM((TOK, 3 * INNER), BF),
            pltpu.VMEM((TOK, INNER), BF),
            pltpu.VMEM((TOK, D), BF),
            pltpu.VMEM((TOK, D), BF),
            pltpu.VMEM((TOK, INNER), BF),
            pltpu.VMEM((TOK, 3 * INNER), BF),
            pltpu.VMEM((2, TOK, GROUP * TOK), BF),
            pltpu.VMEM((TOK, GROUP * TOK), BF),
            pltpu.VMEM((2, GROUP * TOK, GW), BF),
            pltpu.VMEM((GROUP * TOK, GW), BF),
            pltpu.VMEM((TOK, D), BF),
            pltpu.VMEM((TOK, D), BF),
            pltpu.SemaphoreType.DMA((4,)),
            pltpu.SemaphoreType.DMA((4 * (ns + 1),)),
            pltpu.SemaphoreType.DMA((4 * (ns + 1),)),
            pltpu.SemaphoreType.DMA((2 * nz,)),
            pltpu.SemaphoreType.DMA((2 * nz,)),
            pltpu.SemaphoreType.DMA((4 * nz,)),
            pltpu.SemaphoreType.DMA((4 * nz,)),
            pltpu.SemaphoreType.DMA((12,)),
            pltpu.SemaphoreType.DMA((12,)),
        ],
        compiler_params=pltpu.CompilerParams(
            collective_id=0, has_side_effects=True, vmem_limit_bytes=40 * 1024 * 1024
        ),
    )(
        quarters(tokens), quarters(mixed_grad), qkv_weight, out_weight,
        norm_gain.reshape(1, D), norm_bias.reshape(1, D),
    )
    return join(m_out), join(d_out)


def solution(mesh):
    placed = (
        P(None, "lat", "lon", None),
        P("lon", None),
        P("lon", None),
        P(),
        P(),
        P(None, "lat", "lon", None),
    )
    return jax.shard_map(
        functools.partial(per_device, mesh.shape["lat"], mesh.shape["lon"]),
        mesh=mesh,
        in_specs=placed,
        out_specs=(P(None, "lat", "lon", None), P(None, "lat", "lon", None)),
        check_vma=False,
    )
```

```python
import functools

import jax
import jax.numpy as jnp
from jax import lax
from jax.experimental import pallas as pl
from jax.experimental.pallas import tpu as pltpu
from jax.sharding import PartitionSpec as P

MESH = pl.DeviceIdType.MESH
BF = jnp.bfloat16
F32 = jnp.float32

D = 1024
HEADS = 8
HEAD_DIM = 64
LEV = 2
WIN = 12
INNER = 512
HALF = 6
TOK = LEV * WIN * WIN
QUARTER = TOK // 4
GROUP = 4
GW = GROUP * HEAD_DIM
WIDE = GROUP * TOK
ROWS = 32
EPS = 1e-05

HALVES = ((1, 1), (1, 0), (0, 1), (0, 0))


def nt(a, b):
    return lax.dot_general(a, b, (((1,), (1,)), ((), ())), preferred_element_type=F32)


def nn(a, b):
    return lax.dot_general(a, b, (((1,), (0,)), ((), ())), preferred_element_type=F32)


def tn(a, b):
    return lax.dot_general(a, b, (((0,), (0,)), ((), ())), preferred_element_type=F32)


def ds(start, size):
    return pl.ds(pl.multiple_of(start, size), size)


def kernel(
    n_lat, n_lon,
    t_ref, g_ref, wq_ref, wo_ref, gain_hbm, bias_hbm,
    m_out, d_out,
    wqf, wof, gain_ref, bias_ref, land_t, land_g, xw, gw, packed, heads, attn, agrad, hgrad, pgrad,
    scores, pt, dst, qblk, doblk, mixed, tgrad,
    own_sem, zs, zr, xs, xr, ss, sr, hs, hr,
):
    lat, lon = lax.axis_index("lat"), lax.axis_index("lon")
    nz = n_lon // 2
    ns = nz // 2
    rq, ro = D // n_lon, INNER // n_lon
    core, par, z = lax.rem(lat, 2), lax.rem(lon, 2), lon // 2
    lat_lo, lat_hi = lax.rem(lat + n_lat - 1, n_lat), lax.rem(lat + 1, n_lat)
    lon_lo, lon_hi = lax.rem(lon + n_lon - 1, n_lon), lax.rem(lon + 1, n_lon)
    sib = (lat + 1 - 2 * core, lon)
    up = (lat, lax.rem(lon + 2, n_lon))
    down = (lat, lax.rem(lon + n_lon - 2, n_lon))
    differ = lax.rem(par + core, 2)
    across = lon + 1 - 2 * par
    x_to = (lax.rem(lat + differ * (n_lat // 2), n_lat), across)
    x_from = (lax.rem(lat + (1 - differ) * (n_lat // 2), n_lat), across)
    west, north, diag = (lat, lon_lo), (lat_lo, lon), (lat_lo, lon_lo)
    east, south, far = (lat, lon_hi), (lat_hi, lon), (lat_hi, lon_hi)

    barrier = pltpu.get_barrier_semaphore()
    met = (sib, up, down, x_to, x_from, west, north, diag, east, south, far)
    for who in met:
        pl.semaphore_signal(barrier, inc=1, device_id=who, device_id_type=MESH)
    pl.semaphore_wait(barrier, len(met))

    def remote(src, dst, send, recv, who):
        return pltpu.make_async_remote_copy(
            src_ref=src, dst_ref=dst, send_sem=send, recv_sem=recv, device_id=who, device_id_type=MESH
        )

    def quarter(ref, k):
        i, j = HALVES[k]
        return ref.at[pl.ds(i * HALF, HALF), pl.ds(j * HALF, HALF)]

    def halo_in(field, src, land):
        copies = [
            remote(quarter(src, k), land.at[k], hs.at[field * 4 + k], hr.at[field * 4 + k], who)
            for k, who in ((1, west), (2, north), (3, diag))
        ]
        return copies, pltpu.make_async_copy(quarter(src, 0), land.at[0], own_sem.at[4 + field])

    in_t = halo_in(0, t_ref, land_t)
    in_g = halo_in(1, g_ref, land_g)
    for copy in in_t[0]:
        copy.start()

    def piece(kind, zq, p, c):
        if kind == 0:
            return wqf.at[ds((zq * 2 + p) * rq + c * (rq // 2), rq // 2), :]
        return wof.at[ds((zq * 2 + p) * ro, ro), ds(c * (D // 2), D // 2)]

    def own_piece(kind):
        if kind == 0:
            return wq_ref.at[ds(core * (rq // 2), rq // 2), :]
        return wo_ref.at[:, ds(core * (D // 2), D // 2)]

    def z_copy(kind, way, s, zq, src=None):
        dst = piece(kind, zq, par, core)
        i = (way * (ns + 1) + s) * 2 + kind
        return remote(dst if src is None else src, dst, zs.at[i], zr.at[i], (up, down)[way])

    def x_copy(kind, d, zq, p, src=None):
        dst = piece(kind, zq, p, core)
        i = d * 2 + kind
        return remote(dst if src is None else src, dst, xs.at[i], xr.at[i], x_to)

    def s_copy(kind, other, d, zq, c):
        ref = piece(kind, zq, lax.rem(par + other, 2), c)
        i = (other * nz + d) * 2 + kind
        return remote(ref, ref, ss.at[i], sr.at[i], sib)

    def ahead(zq, s):
        return lax.rem(zq + s, nz)

    def behind(zq, s):
        return lax.rem(zq - s + nz, nz)

    local = [
        pltpu.make_async_copy(wq_ref, wqf.at[ds(lon * rq, rq), :], own_sem.at[0]),
        pltpu.make_async_copy(wo_ref, wof.at[ds(lon * ro, ro), :], own_sem.at[1]),
        pltpu.make_async_copy(gain_hbm, gain_ref, own_sem.at[2]),
        pltpu.make_async_copy(bias_hbm, bias_ref, own_sem.at[3]),
        in_t[1],
    ]
    for kind in (0, 1):
        src = own_piece(kind)
        z_copy(kind, 0, 1, z, src).start()
        if ns > 1:
            z_copy(kind, 1, 1, z, src).start()
        x_copy(kind, 0, z, par, src).start()
    for copy in local:
        copy.start()
    for copy in in_g[0]:
        copy.start()
    in_g[1].start()

    def z_arrive(kind, way, s, last):
        zq, d = (behind(z, s), s) if way == 0 else (ahead(z, s), nz - s)
        z_copy(kind, way, s, zq).wait_recv()
        if not last:
            z_copy(kind, way, s + 1, zq).start()
        x_copy(kind, d, zq, par).start()
        s_copy(kind, 0, d, zq, core).start()

    def x_arrive(kind, d):
        zq = behind(z, d)
        x_copy(kind, d, zq, 1 - par).wait_recv()
        s_copy(kind, 1, d, zq, core).start()

    def z_step(s, up_last, down_in, down_last):
        for kind in (0, 1):
            z_arrive(kind, 0, s, up_last)
            if down_in:
                z_arrive(kind, 1, s, down_last)

    def x_step(s, both):
        for kind in (0, 1):
            x_arrive(kind, s)
            if both:
                x_arrive(kind, nz - s)

    def fixed_step(s):
        z_step(s, s == ns, s < ns, s == ns - 1)
        x_step(s - 1, s > 1)

    fixed_step(1)
    if ns > 3:
        def middle(s, carry):
            z_step(s, False, True, False)
            x_step(s - 1, True)
            return carry

        lax.fori_loop(2, ns - 1, middle, 0)
    for s in range(max(2, ns - 1), ns + 1):
        fixed_step(s)

    def rows_of(land, field):
        for k in range(4):
            field[k * QUARTER : (k + 1) * QUARTER, :] = land[k].reshape(QUARTER, D)

    for copy in in_t[0]:
        copy.wait_recv()
    for copy in local:
        copy.wait()
    rows_of(land_t, xw)
    x_step(ns, False)

    def s_wait(d, carry):
        for kind in (0, 1):
            s_copy(kind, 0, d, behind(z, d), 1 - core).wait_recv()
            s_copy(kind, 1, d, behind(z, d), 1 - core).wait_recv()
        return carry

    for kind in (0, 1):
        s_copy(kind, 1, 0, z, 1 - core).wait_recv()
    lax.fori_loop(1, nz, s_wait, 0)

    def project(n, carry):
        cols = ds(n * 256, 256)
        packed[:, cols] = nn(xw[...], wqf[:, cols]).astype(BF)
        return carry

    lax.fori_loop(0, 3 * INNER // 256, project, 0)

    lane_head = lax.broadcasted_iota(jnp.int32, (TOK, GW), 1) // HEAD_DIM
    banned = jnp.where(lat == n_lat - 1, -1e30, 0.0).astype(F32)

    def spread(rows):
        return [rows * (lane_head[0:1] == h).astype(F32).astype(BF) for h in range(GROUP)]

    def gather_heads(wide):
        out = wide[0:TOK, :]
        for h in range(1, GROUP):
            out = jnp.where(lane_head == h, wide[h * TOK : (h + 1) * TOK, :], out)
        return out

    for g in range(HEADS // GROUP):
        q_at, k_at, v_at = g * GW, INNER + g * GW, 2 * INNER + g * GW
        for h, rows in enumerate(spread(packed[:, q_at : q_at + GW])):
            qblk[g, h * TOK : (h + 1) * TOK, :] = rows

        def score(c, carry, g=g, k_at=k_at):
            cols = ds(c * 384, 384)
            scores[:, cols] = nt(packed[:, k_at : k_at + GW], qblk[g, cols, :])
            return carry

        lax.fori_loop(0, WIDE // 384, score, 0)

        def soften(c, carry, g=g):
            cols = ds(c * 128, 128)
            query = lax.rem(c * 128 + lax.broadcasted_iota(jnp.int32, (1, 128), 1), TOK)
            side = (query >= TOK // 2).astype(F32)
            s = jnp.concatenate(
                [scores[: TOK // 2, cols] + side * banned, scores[TOK // 2 :, cols] + (1.0 - side) * banned], axis=0
            )
            top = jnp.max(s, axis=0, keepdims=True)
            e = jnp.exp((s - top) * (HEAD_DIM ** -0.5))
            pt[g, :, cols] = (e * (1.0 / jnp.sum(e, axis=0, keepdims=True))).astype(BF)
            return carry

        lax.fori_loop(0, WIDE // 128, soften, 0, unroll=3)
        heads[:, q_at : q_at + GW] = gather_heads(tn(pt[g], packed[:, v_at : v_at + GW])).astype(BF)

    def out_project(n, carry):
        cols = ds(n * 256, 256)
        attn[:, cols] = nn(heads[...], wof[:, cols]).astype(BF)
        return carry

    lax.fori_loop(0, D // 256, out_project, 0)

    for copy in in_g[0]:
        copy.wait_recv()
    in_g[1].wait()
    rows_of(land_g, gw)

    def norm(c, carry):
        rows = ds(c * ROWS, ROWS)
        a = attn[rows, :].astype(F32)
        gain = gain_ref[...]
        scaled = gw[rows, :].astype(F32) * gain
        centered = a - jnp.mean(a, axis=-1, keepdims=True)
        level = scaled - jnp.mean(scaled, axis=-1, keepdims=True)
        inverse = lax.rsqrt(jnp.mean(centered * centered, axis=-1, keepdims=True) + EPS)
        along = jnp.mean(scaled * centered, axis=-1, keepdims=True) * inverse
        normed = centered * inverse
        mixed[rows, :] = (xw[rows, :].astype(F32) + normed * gain + bias_ref[...]).astype(BF)
        agrad[rows, :] = ((level - normed * along) * inverse).astype(BF)
        return carry

    lax.fori_loop(0, TOK // ROWS, norm, 0, unroll=3)

    def halo_out(field, rows, land, out):
        for k in range(4):
            land[k] = rows[k * QUARTER : (k + 1) * QUARTER, :].reshape(HALF, HALF, LEV, D)
        copies = [
            remote(land.at[k], quarter(out, k), hs.at[(field + 2) * 4 + k], hr.at[(field + 2) * 4 + k], who)
            for k, who in ((1, east), (2, south), (3, far))
        ]
        keep = pltpu.make_async_copy(land.at[0], quarter(out, 0), own_sem.at[6 + field])
        for copy in copies:
            copy.start()
        keep.start()
        return copies, keep

    out_m = halo_out(0, mixed, land_t, m_out)

    def back_project(n, carry):
        cols = ds(n * 256, 256)
        hgrad[:, cols] = nt(agrad[...], wof[cols, :]).astype(BF)
        return carry

    lax.fori_loop(0, INNER // 256, back_project, 0)

    for g in range(HEADS // GROUP):
        q_at, k_at, v_at = g * GW, INNER + g * GW, 2 * INNER + g * GW
        for h, rows in enumerate(spread(hgrad[:, q_at : q_at + GW])):
            doblk[h * TOK : (h + 1) * TOK, :] = rows

        def prob_grad(c, carry, v_at=v_at):
            cols = ds(c * 384, 384)
            scores[:, cols] = nt(packed[:, v_at : v_at + GW], doblk[cols, :])
            return carry

        lax.fori_loop(0, WIDE // 384, prob_grad, 0)

        def score_grad(c, carry, g=g):
            cols = ds(c * 128, 128)
            p, dp = pt[g, :, cols].astype(F32), scores[:, cols]
            total = jnp.sum(p * dp, axis=0, keepdims=True)
            dst[:, cols] = (p * (dp - total) * (HEAD_DIM ** -0.5)).astype(BF)
            return carry

        lax.fori_loop(0, WIDE // 128, score_grad, 0, unroll=3)
        pgrad[:, q_at : q_at + GW] = gather_heads(tn(dst[...], packed[:, k_at : k_at + GW])).astype(BF)
        pgrad[:, v_at : v_at + GW] = nn(pt[g], doblk[...]).astype(BF)
        pgrad[:, k_at : k_at + GW] = nn(dst[...], qblk[g]).astype(BF)

    def unproject(n, carry):
        cols = ds(n * 256, 256)
        sg = nt(pgrad[...], wqf[cols, :]).astype(BF).astype(F32)
        tgrad[:, cols] = (gw[:, cols].astype(F32) + sg).astype(BF)
        return carry

    lax.fori_loop(0, D // 256, unproject, 0)
    out_d = halo_out(1, tgrad, land_g, d_out)

    for kind in (0, 1):
        z_copy(kind, 0, 1, z).wait_send()
        x_copy(kind, 0, z, par).wait_send()
        s_copy(kind, 1, 0, z, core).wait_send()

    def sent(d, carry):
        for kind in (0, 1):
            x_copy(kind, d, behind(z, d), par).wait_send()
            s_copy(kind, 0, d, behind(z, d), core).wait_send()
            s_copy(kind, 1, d, behind(z, d), core).wait_send()
        return carry

    lax.fori_loop(1, nz, sent, 0)

    def sent_z(s, carry):
        for kind in (0, 1):
            z_copy(kind, 0, s, behind(z, s - 1)).wait_send()
            z_copy(kind, 1, s - 1, ahead(z, s - 2)).wait_send()
        return carry

    lax.fori_loop(2, ns + 1, sent_z, 0)
    for copy in in_t[0] + in_g[0]:
        copy.wait_send()
    for copies, keep in (out_m, out_d):
        keep.wait()
        for copy in copies:
            copy.wait()


def per_device(n_lat, n_lon, tokens, qkv_weight, out_weight, norm_gain, norm_bias, mixed_grad):
    nz = n_lon // 2
    ns = nz // 2
    hbm = pl.BlockSpec(memory_space=pltpu.HBM)
    cells = (WIN, WIN, LEV, D)
    m_out, d_out = pl.pallas_call(
        functools.partial(kernel, n_lat, n_lon),
        out_shape=[jax.ShapeDtypeStruct(cells, BF)] * 2,
        in_specs=[hbm] * 6,
        out_specs=[pl.BlockSpec(memory_space=pl.ANY)] * 2,
        scratch_shapes=[
            pltpu.VMEM((D, 3 * INNER), BF),
            pltpu.VMEM((INNER, D), BF),
            pltpu.VMEM((1, D), F32),
            pltpu.VMEM((1, D), F32),
            pltpu.VMEM((4, HALF, HALF, LEV, D), BF),
            pltpu.VMEM((4, HALF, HALF, LEV, D), BF),
            pltpu.VMEM((TOK, D), BF),
            pltpu.VMEM((TOK, D), BF),
            pltpu.VMEM((TOK, 3 * INNER), BF),
            pltpu.VMEM((TOK, INNER), BF),
            pltpu.VMEM((TOK, D), BF),
            pltpu.VMEM((TOK, D), BF),
            pltpu.VMEM((TOK, INNER), BF),
            pltpu.VMEM((TOK, 3 * INNER), BF),
            pltpu.VMEM((TOK, WIDE), F32),
            pltpu.VMEM((2, TOK, WIDE), BF),
            pltpu.VMEM((TOK, WIDE), BF),
            pltpu.VMEM((2, WIDE, GW), BF),
            pltpu.VMEM((WIDE, GW), BF),
            pltpu.VMEM((TOK, D), BF),
            pltpu.VMEM((TOK, D), BF),
            pltpu.SemaphoreType.DMA((8,)),
            pltpu.SemaphoreType.DMA((4 * (ns + 1),)),
            pltpu.SemaphoreType.DMA((4 * (ns + 1),)),
            pltpu.SemaphoreType.DMA((2 * nz,)),
            pltpu.SemaphoreType.DMA((2 * nz,)),
            pltpu.SemaphoreType.DMA((4 * nz,)),
            pltpu.SemaphoreType.DMA((4 * nz,)),
            pltpu.SemaphoreType.DMA((16,)),
            pltpu.SemaphoreType.DMA((16,)),
        ],
        compiler_params=pltpu.CompilerParams(
            collective_id=0, has_side_effects=True, vmem_limit_bytes=63 * 1024 * 1024
        ),
    )(
        tokens.transpose(1, 2, 0, 3), mixed_grad.transpose(1, 2, 0, 3), qkv_weight, out_weight,
        norm_gain.reshape(1, D), norm_bias.reshape(1, D),
    )
    return m_out.transpose(2, 0, 1, 3), d_out.transpose(2, 0, 1, 3)


def solution(mesh):
    placed = (
        P(None, "lat", "lon", None),
        P("lon", None),
        P("lon", None),
        P(),
        P(),
        P(None, "lat", "lon", None),
    )
    return jax.shard_map(
        functools.partial(per_device, mesh.shape["lat"], mesh.shape["lon"]),
        mesh=mesh,
        in_specs=placed,
        out_specs=(P(None, "lat", "lon", None), P(None, "lat", "lon", None)),
        check_vma=False,
    )
```

```python
import functools

import jax
import jax.numpy as jnp
from jax import lax
from jax.experimental import pallas as pl
from jax.experimental.pallas import tpu as pltpu
from jax.sharding import PartitionSpec as P

MESH = pl.DeviceIdType.MESH
BF = jnp.bfloat16
F32 = jnp.float32

D = 1024
HEADS = 8
HEAD_DIM = 64
LEV = 2
WIN = 12
INNER = 512
HALF = 6
TOK = LEV * WIN * WIN
QUARTER = TOK // 4
GROUP = 4
GW = GROUP * HEAD_DIM
WIDE = GROUP * TOK
ROWS = 32
EPS = 1e-05

HALVES = ((1, 1), (1, 0), (0, 1), (0, 0))


def nt(a, b):
    return lax.dot_general(a, b, (((1,), (1,)), ((), ())), preferred_element_type=F32)


def nn(a, b):
    return lax.dot_general(a, b, (((1,), (0,)), ((), ())), preferred_element_type=F32)


def tn(a, b):
    return lax.dot_general(a, b, (((0,), (0,)), ((), ())), preferred_element_type=F32)


def ds(start, size):
    return pl.ds(pl.multiple_of(start, size), size)


def kernel(
    n_lat, n_lon,
    t_ref, g_ref, wq_ref, wo_ref, gain_hbm, bias_hbm,
    m_out, d_out,
    wqf, wof, gain_ref, bias_ref, land_t, land_g, xw, gw, packed, heads, attn, agrad, hgrad, pgrad,
    scores, pt, dst, qblk, doblk, wide, mixed, tgrad,
    own_sem, zs, zr, ys, yr, xs, xr, ss, sr, hs, hr,
):
    lat, lon = lax.axis_index("lat"), lax.axis_index("lon")
    nz, ny = n_lon // 2, n_lat // 4
    rq, ro = D // n_lon, INNER // n_lon
    core, par, z = lax.rem(lat, 2), lax.rem(lon, 2), lon // 2
    half, y = lat // (2 * ny), lax.rem(lat // 2, ny)
    lat_lo, lat_hi = lax.rem(lat + n_lat - 1, n_lat), lax.rem(lat + 1, n_lat)
    lon_lo, lon_hi = lax.rem(lon + n_lon - 1, n_lon), lax.rem(lon + 1, n_lon)
    sib = (lat + 1 - 2 * core, lon)
    differ = lax.rem(par + core, 2)
    across = lon + 1 - 2 * par
    x_to = (lax.rem(lat + differ * (n_lat // 2), n_lat), across)
    x_from = (lax.rem(lat + (1 - differ) * (n_lat // 2), n_lat), across)
    west, north, diag = (lat, lon_lo), (lat_lo, lon), (lat_lo, lon_lo)
    east, south, far = (lat, lon_hi), (lat_hi, lon), (lat_hi, lon_hi)

    def offset(yy, e):
        far_pair = e // 2
        size = (1 - far_pair) * (yy + 1) + far_pair * (2 * ny - yy)
        return (1 - 2 * lax.rem(e, 2)) * size

    def z_to(e):
        return (lat, 2 * lax.rem(z + offset(y, e) + nz, nz) + par)

    def source(yy, e):
        return lax.rem(z - offset(yy, e) + nz, nz)

    def exists(yy, e):
        return jnp.logical_or(yy > 0, e < 3)

    def y_to(way):
        return ((half * ny + lax.rem(y + 1 - 2 * way + ny, ny)) * 2 + core, lon)

    def line(group, c):
        return lax.rem(y + ny + (0, 2 * c - 1, 1 - 2 * c, 2)[group], ny)

    barrier = pltpu.get_barrier_semaphore()
    met = [z_to(e) for e in range(4)]
    met += [y_to(0), y_to(1), sib, x_to, x_from, west, north, diag, east, south, far]
    for who in met:
        pl.semaphore_signal(barrier, inc=1, device_id=who, device_id_type=MESH)
    pl.semaphore_wait(barrier, len(met))

    def remote(src, dst, send, recv, who):
        return pltpu.make_async_remote_copy(
            src_ref=src, dst_ref=dst, send_sem=send, recv_sem=recv, device_id=who, device_id_type=MESH
        )

    def quarter(ref, k):
        i, j = HALVES[k]
        return ref.at[pl.ds(i * HALF, HALF), pl.ds(j * HALF, HALF)]

    def halo_in(field, src, land):
        copies = [
            remote(quarter(src, k), land.at[k], hs.at[field * 4 + k], hr.at[field * 4 + k], who)
            for k, who in ((1, west), (2, north), (3, diag))
        ]
        return copies, pltpu.make_async_copy(quarter(src, 0), land.at[0], own_sem.at[4 + field])

    in_t = halo_in(0, t_ref, land_t)
    in_g = halo_in(1, g_ref, land_g)
    for copy in in_t[0]:
        copy.start()

    def piece(kind, zq, p, c, both=1):
        if kind == 0:
            return wqf.at[pl.ds(pl.multiple_of((zq * 2 + p) * rq, rq), both * rq), ds(c * 768, 768)]
        return wof.at[pl.ds(pl.multiple_of((zq * 2 + p) * ro, ro), both * ro), ds(c * 512, 512)]

    def own_piece(kind):
        return wq_ref.at[:, ds(core * 768, 768)] if kind == 0 else wo_ref.at[:, ds(core * 512, 512)]

    def z_copy(kind, e, zq):
        i = kind * 4 + e
        return remote(own_piece(kind), piece(kind, zq, par, core), zs.at[i], zr.at[i], z_to(e))

    def y_copy(kind, way, e, zq, to):
        ref, i = piece(kind, zq, par, core), (kind * 3 + way) * 4 + e
        return remote(ref, ref, ys.at[i], yr.at[i], y_to(to))

    def x_copy(kind, slot, zq, p):
        ref, i = piece(kind, zq, p, core), kind * 17 + slot
        return remote(ref, ref, xs.at[i], xr.at[i], x_to)

    def x_own(kind):
        i = kind * 17 + 16
        return remote(own_piece(kind), piece(kind, z, par, core), xs.at[i], xr.at[i], x_to)

    def s_copy(kind, slot, zq, c):
        ref, i = piece(kind, zq, 0, c, 2), kind * 17 + slot
        return remote(ref, ref, ss.at[i], sr.at[i], sib)

    def s_own(kind, c):
        ref, i = piece(kind, z, 1 - par, c), kind * 17 + 16
        return remote(ref, ref, ss.at[i], sr.at[i], sib)

    def each(yy, do):
        def step(e, carry):
            @pl.when(exists(yy, e))
            def _():
                do(e)

            return carry

        lax.fori_loop(0, 4, step, 0)

    def begin(kind):
        each(y, lambda e: z_copy(kind, e, z).start())
        x_own(kind).start()

    def hop_z(kind):
        def do(e):
            zq = source(y, e)
            z_copy(kind, e, zq).wait_recv()
            y_copy(kind, 0, e, zq, 0).start()
            y_copy(kind, 1, e, zq, 1).start()
            x_copy(kind, e, zq, par).start()

        each(y, do)

    def hop_y(kind):
        def near(e):
            zq = source(line(1, core), e)
            y_copy(kind, core, e, zq, core).wait_recv()
            y_copy(kind, 2, e, zq, core).start()
            x_copy(kind, 4 + e, zq, par).start()

        def other(e):
            zq = source(line(2, core), e)
            y_copy(kind, 1 - core, e, zq, core).wait_recv()
            x_copy(kind, 8 + e, zq, par).start()

        each(line(1, core), near)
        each(line(2, core), other)

    def hop_y2(kind):
        def do(e):
            zq = source(line(3, core), e)
            y_copy(kind, 2, e, zq, core).wait_recv()
            x_copy(kind, 12 + e, zq, par).start()

        each(line(3, core), do)

    def hop_x(kind):
        x_copy(kind, 16, z, 1 - par).wait_recv()
        s_own(kind, core).start()
        for group in range(4):
            def do(e, group=group):
                zq = source(line(group, core), e)
                x_copy(kind, group * 4 + e, zq, 1 - par).wait_recv()
                s_copy(kind, group * 4 + e, zq, core).start()

            each(line(group, core), do)

    def finish(kind):
        s_own(kind, 1 - core).wait_recv()
        for group in range(4):
            def do(e, group=group):
                s_copy(kind, group * 4 + e, source(line(group, 1 - core), e), 1 - core).wait_recv()

            each(line(group, 1 - core), do)

    def all_sent(kind):
        x_own(kind).wait_send()
        s_own(kind, core).wait_send()

        def first(e):
            z_copy(kind, e, z).wait_send()
            y_copy(kind, 0, e, source(y, e), 0).wait_send()
            y_copy(kind, 1, e, source(y, e), 1).wait_send()

        each(y, first)
        each(line(1, core), lambda e: y_copy(kind, 2, e, source(line(1, core), e), core).wait_send())
        for group in range(4):
            def do(e, group=group):
                zq = source(line(group, core), e)
                x_copy(kind, group * 4 + e, zq, par).wait_send()
                s_copy(kind, group * 4 + e, zq, core).wait_send()

            each(line(group, core), do)

    local = [
        pltpu.make_async_copy(wq_ref, wqf.at[ds(lon * rq, rq), :], own_sem.at[0]),
        pltpu.make_async_copy(wo_ref, wof.at[ds(lon * ro, ro), :], own_sem.at[1]),
        pltpu.make_async_copy(gain_hbm, gain_ref, own_sem.at[2]),
        pltpu.make_async_copy(bias_hbm, bias_ref, own_sem.at[3]),
        in_t[1],
        in_g[1],
    ]
    begin(0)
    for copy in local:
        copy.start()
    hop_z(0)
    begin(1)
    for copy in in_g[0]:
        copy.start()
    hop_y(0)
    hop_y2(0)

    def rows_of(land, field):
        def step(t, carry):
            k, i = 2 * (t // 3), 2 * lax.rem(t, 3)
            two = [land[k + n, pl.ds(i, 2)].reshape(24, D) for n in (0, 1)]
            field[ds(t * 48, 48), :] = jnp.concatenate(two, axis=0)
            return carry

        lax.fori_loop(0, 6, step, 0)

    for copy in in_t[0]:
        copy.wait_recv()
    for copy in local:
        copy.wait()
    rows_of(land_t, xw)
    hop_x(0)
    hop_z(1)
    finish(0)

    def project(n, carry):
        cols = ds(n * 256, 256)
        packed[:, cols] = nn(xw[...], wqf[:, cols]).astype(BF)
        return carry

    lax.fori_loop(0, 3 * INNER // 256, project, 0)
    hop_y(1)
    hop_y2(1)

    lane_head = lax.broadcasted_iota(jnp.int32, (TOK, GW), 1) // HEAD_DIM
    banned = jnp.where(lat == n_lat - 1, -1e30, 0.0).astype(F32)

    def spread(rows):
        return [rows * (lane_head[0:1] == h).astype(F32).astype(BF) for h in range(GROUP)]

    def gather_heads(wide):
        out = wide[0:TOK, :]
        for h in range(1, GROUP):
            out = jnp.where(lane_head == h, wide[h * TOK : (h + 1) * TOK, :], out)
        return out

    def columns(g):
        return [ds(n * INNER + g * GW, GW) for n in range(3)]

    def narrow(left, right):
        def step(c, carry):
            cols = ds(c * 384, 384)
            wide[cols, :] = tn(left(cols), right)
            return carry

        lax.fori_loop(0, WIDE // 384, step, 0)
        return gather_heads(wide).astype(BF)

    def forward(g, carry):
        q_at, k_at, v_at = columns(g)
        for h, rows in enumerate(spread(packed[:, q_at])):
            qblk[g, h * TOK : (h + 1) * TOK, :] = rows

        def score(c, carry):
            cols = ds(c * 384, 384)
            scores[:, cols] = nt(packed[:, k_at], qblk[g, cols, :])
            return carry

        lax.fori_loop(0, WIDE // 384, score, 0)

        def soften(c, carry):
            cols = ds(c * 128, 128)
            query = lax.rem(c * 128 + lax.broadcasted_iota(jnp.int32, (1, 128), 1), TOK)
            side = (query >= TOK // 2).astype(F32)
            s = jnp.concatenate(
                [scores[: TOK // 2, cols] + side * banned, scores[TOK // 2 :, cols] + (1.0 - side) * banned], axis=0
            )
            top = jnp.max(s, axis=0, keepdims=True)
            e = jnp.exp((s - top) * (HEAD_DIM ** -0.5))
            pt[g, :, cols] = (e * (1.0 / jnp.sum(e, axis=0, keepdims=True))).astype(BF)
            return carry

        lax.fori_loop(0, WIDE // 128, soften, 0, unroll=3)
        heads[:, q_at] = narrow(lambda cols: pt[g, :, cols], packed[:, v_at])

        @pl.when(g == 0)
        def _():
            hop_x(1)

        return carry

    lax.fori_loop(0, HEADS // GROUP, forward, 0)
    finish(1)

    def out_project(n, carry):
        cols = ds(n * 256, 256)
        attn[:, cols] = nn(heads[...], wof[:, cols]).astype(BF)
        return carry

    lax.fori_loop(0, D // 256, out_project, 0)

    for copy in in_g[0]:
        copy.wait_recv()
    rows_of(land_g, gw)

    def norm(c, carry):
        rows = ds(c * ROWS, ROWS)
        a = attn[rows, :].astype(F32)
        gain = gain_ref[...]
        scaled = gw[rows, :].astype(F32) * gain
        centered = a - jnp.mean(a, axis=-1, keepdims=True)
        level = scaled - jnp.mean(scaled, axis=-1, keepdims=True)
        inverse = lax.rsqrt(jnp.mean(centered * centered, axis=-1, keepdims=True) + EPS)
        along = jnp.mean(scaled * centered, axis=-1, keepdims=True) * inverse
        normed = centered * inverse
        mixed[rows, :] = (xw[rows, :].astype(F32) + normed * gain + bias_ref[...]).astype(BF)
        agrad[rows, :] = ((level - normed * along) * inverse).astype(BF)
        return carry

    lax.fori_loop(0, TOK // ROWS, norm, 0, unroll=3)

    def halo_out(field, rows, land, out):
        def step(t, carry):
            k, i = 2 * (t // 3), 2 * lax.rem(t, 3)
            block = rows[ds(t * 48, 48), :]
            for n in (0, 1):
                land[k + n, pl.ds(i, 2)] = block[n * 24 : (n + 1) * 24].reshape(2, HALF, LEV, D)
            return carry

        lax.fori_loop(0, 6, step, 0)
        copies = [
            remote(land.at[k], quarter(out, k), hs.at[(field + 2) * 4 + k], hr.at[(field + 2) * 4 + k], who)
            for k, who in ((1, east), (2, south), (3, far))
        ]
        keep = pltpu.make_async_copy(land.at[0], quarter(out, 0), own_sem.at[6 + field])
        for copy in copies:
            copy.start()
        keep.start()
        return copies, keep

    out_m = halo_out(0, mixed, land_t, m_out)

    def back_project(n, carry):
        cols = ds(n * 256, 256)
        hgrad[:, cols] = nt(agrad[...], wof[cols, :]).astype(BF)
        return carry

    lax.fori_loop(0, INNER // 256, back_project, 0)

    def backward(g, carry):
        q_at, k_at, v_at = columns(g)
        for h, rows in enumerate(spread(hgrad[:, q_at])):
            doblk[h * TOK : (h + 1) * TOK, :] = rows

        def prob_grad(c, carry):
            cols = ds(c * 384, 384)
            scores[:, cols] = nt(packed[:, v_at], doblk[cols, :])
            return carry

        lax.fori_loop(0, WIDE // 384, prob_grad, 0)

        def score_grad(c, carry):
            cols = ds(c * 128, 128)
            p, dp = pt[g, :, cols].astype(F32), scores[:, cols]
            total = jnp.sum(p * dp, axis=0, keepdims=True)
            dst[:, cols] = (p * (dp - total) * (HEAD_DIM ** -0.5)).astype(BF)
            return carry

        lax.fori_loop(0, WIDE // 128, score_grad, 0, unroll=3)
        pgrad[:, q_at] = narrow(lambda cols: dst[:, cols], packed[:, k_at])
        pgrad[:, v_at] = nn(pt[g], doblk[...]).astype(BF)
        pgrad[:, k_at] = nn(dst[...], qblk[g]).astype(BF)
        return carry

    lax.fori_loop(0, HEADS // GROUP, backward, 0)

    def unproject(n, carry):
        cols = ds(n * 256, 256)
        sg = nt(pgrad[...], wqf[cols, :]).astype(BF).astype(F32)
        tgrad[:, cols] = (gw[:, cols].astype(F32) + sg).astype(BF)
        return carry

    lax.fori_loop(0, D // 256, unproject, 0)
    out_d = halo_out(1, tgrad, land_g, d_out)

    for kind in (0, 1):
        all_sent(kind)
    for copy in in_t[0] + in_g[0]:
        copy.wait_send()
    for copies, keep in (out_m, out_d):
        keep.wait()
        for copy in copies:
            copy.wait()


def per_device(n_lat, n_lon, tokens, qkv_weight, out_weight, norm_gain, norm_bias, mixed_grad):
    hbm = pl.BlockSpec(memory_space=pltpu.HBM)
    cells = (WIN, WIN, LEV, D)
    m_out, d_out = pl.pallas_call(
        functools.partial(kernel, n_lat, n_lon),
        out_shape=[jax.ShapeDtypeStruct(cells, BF)] * 2,
        in_specs=[hbm] * 6,
        out_specs=[pl.BlockSpec(memory_space=pl.ANY)] * 2,
        scratch_shapes=[
            pltpu.VMEM((D, 3 * INNER), BF),
            pltpu.VMEM((INNER, D), BF),
            pltpu.VMEM((1, D), F32),
            pltpu.VMEM((1, D), F32),
            pltpu.VMEM((4, HALF, HALF, LEV, D), BF),
            pltpu.VMEM((4, HALF, HALF, LEV, D), BF),
            pltpu.VMEM((TOK, D), BF),
            pltpu.VMEM((TOK, D), BF),
            pltpu.VMEM((TOK, 3 * INNER), BF),
            pltpu.VMEM((TOK, INNER), BF),
            pltpu.VMEM((TOK, D), BF),
            pltpu.VMEM((TOK, D), BF),
            pltpu.VMEM((TOK, INNER), BF),
            pltpu.VMEM((TOK, 3 * INNER), BF),
            pltpu.VMEM((TOK, WIDE), F32),
            pltpu.VMEM((2, TOK, WIDE), BF),
            pltpu.VMEM((TOK, WIDE), BF),
            pltpu.VMEM((2, WIDE, GW), BF),
            pltpu.VMEM((WIDE, GW), BF),
            pltpu.VMEM((WIDE, GW), F32),
            pltpu.VMEM((TOK, D), BF),
            pltpu.VMEM((TOK, D), BF),
            pltpu.SemaphoreType.DMA((8,)),
            pltpu.SemaphoreType.DMA((8,)),
            pltpu.SemaphoreType.DMA((8,)),
            pltpu.SemaphoreType.DMA((24,)),
            pltpu.SemaphoreType.DMA((24,)),
            pltpu.SemaphoreType.DMA((34,)),
            pltpu.SemaphoreType.DMA((34,)),
            pltpu.SemaphoreType.DMA((34,)),
            pltpu.SemaphoreType.DMA((34,)),
            pltpu.SemaphoreType.DMA((16,)),
            pltpu.SemaphoreType.DMA((16,)),
        ],
        compiler_params=pltpu.CompilerParams(
            collective_id=0, has_side_effects=True, vmem_limit_bytes=63 * 1024 * 1024
        ),
    )(
        tokens.transpose(1, 2, 0, 3), mixed_grad.transpose(1, 2, 0, 3), qkv_weight, out_weight,
        norm_gain.reshape(1, D), norm_bias.reshape(1, D),
    )
    return m_out.transpose(2, 0, 1, 3), d_out.transpose(2, 0, 1, 3)


def solution(mesh):
    placed = (
        P(None, "lat", "lon", None),
        P("lon", None),
        P("lon", None),
        P(),
        P(),
        P(None, "lat", "lon", None),
    )
    return jax.shard_map(
        functools.partial(per_device, mesh.shape["lat"], mesh.shape["lon"]),
        mesh=mesh,
        in_specs=placed,
        out_specs=(P(None, "lat", "lon", None), P(None, "lat", "lon", None)),
        check_vma=False,
    )
```

```python
import functools

import jax
import jax.numpy as jnp
from jax import lax
from jax.experimental import pallas as pl
from jax.experimental.pallas import tpu as pltpu
from jax.sharding import PartitionSpec as P

MESH = pl.DeviceIdType.MESH
BF = jnp.bfloat16
F32 = jnp.float32

D = 1024
HEADS = 8
HEAD_DIM = 64
LEV = 2
WIN = 12
INNER = 512
HALF = 6
TOK = LEV * WIN * WIN
QUARTER = TOK // 4
GROUP = 4
GW = GROUP * HEAD_DIM
WIDE = GROUP * TOK
ROWS = 32
EPS = 1e-05

HALVES = ((1, 1), (1, 0), (0, 1), (0, 0))


def nt(a, b):
    return lax.dot_general(a, b, (((1,), (1,)), ((), ())), preferred_element_type=F32)


def nn(a, b):
    return lax.dot_general(a, b, (((1,), (0,)), ((), ())), preferred_element_type=F32)


def tn(a, b):
    return lax.dot_general(a, b, (((0,), (0,)), ((), ())), preferred_element_type=F32)


def ds(start, size):
    return pl.ds(pl.multiple_of(start, size), size)


def kernel(
    n_lat, n_lon,
    t_ref, g_ref, wq_ref, wo_ref, gain_hbm, bias_hbm,
    m_out, d_out,
    wqf, wof, gain_ref, bias_ref, land_t, land_g, xw, gw, packed, heads, attn, agrad, hgrad, pgrad,
    scores, pt, dst, qblk, doblk, wide, mixed, tgrad,
    own_sem, zs, zr, ys, yr, xs, xr, ss, sr, hs, hr,
):
    lat, lon = lax.axis_index("lat"), lax.axis_index("lon")
    nz, ny = n_lon // 2, n_lat // 4
    rq, ro = D // n_lon, INNER // n_lon
    core, par, z = lax.rem(lat, 2), lax.rem(lon, 2), lon // 2
    half, y = lat // (2 * ny), lax.rem(lat // 2, ny)
    lat_lo, lat_hi = lax.rem(lat + n_lat - 1, n_lat), lax.rem(lat + 1, n_lat)
    lon_lo, lon_hi = lax.rem(lon + n_lon - 1, n_lon), lax.rem(lon + 1, n_lon)
    sib = (lat + 1 - 2 * core, lon)
    differ = lax.rem(par + core, 2)
    across = lon + 1 - 2 * par
    x_to = (lax.rem(lat + differ * (n_lat // 2), n_lat), across)
    x_from = (lax.rem(lat + (1 - differ) * (n_lat // 2), n_lat), across)
    west, north, diag = (lat, lon_lo), (lat_lo, lon), (lat_lo, lon_lo)
    east, south, far = (lat, lon_hi), (lat_hi, lon), (lat_hi, lon_hi)

    def offset(yy, e):
        far_pair = e // 2
        size = (1 - far_pair) * (yy + 1) + far_pair * (2 * ny - yy)
        return (1 - 2 * lax.rem(e, 2)) * size

    def z_to(e):
        return (lat, 2 * lax.rem(z + offset(y, e) + nz, nz) + par)

    def source(yy, e):
        return lax.rem(z - offset(yy, e) + nz, nz)

    def exists(yy, e):
        return jnp.logical_or(yy > 0, e < 3)

    def y_to(way):
        return ((half * ny + lax.rem(y + 1 - 2 * way + ny, ny)) * 2 + core, lon)

    def line(group, c):
        return lax.rem(y + ny + (0, 2 * c - 1, 1 - 2 * c, 2)[group], ny)

    barrier = pltpu.get_barrier_semaphore()
    met = [z_to(e) for e in range(4)]
    met += [y_to(0), y_to(1), sib, x_to, x_from, west, north, diag, east, south, far]
    for who in met:
        pl.semaphore_signal(barrier, inc=1, device_id=who, device_id_type=MESH)
    pl.semaphore_wait(barrier, len(met))

    def remote(src, dst, send, recv, who):
        return pltpu.make_async_remote_copy(
            src_ref=src, dst_ref=dst, send_sem=send, recv_sem=recv, device_id=who, device_id_type=MESH
        )

    def quarter(ref, k):
        i, j = HALVES[k]
        return ref.at[pl.ds(i * HALF, HALF), pl.ds(j * HALF, HALF)]

    def halo_in(field, src, land):
        copies = [
            remote(quarter(src, k), land.at[k], hs.at[field * 4 + k], hr.at[field * 4 + k], who)
            for k, who in ((1, west), (2, north), (3, diag))
        ]
        return copies, pltpu.make_async_copy(quarter(src, 0), land.at[0], own_sem.at[4 + field])

    in_t = halo_in(0, t_ref, land_t)
    in_g = halo_in(1, g_ref, land_g)
    for copy in in_t[0]:
        copy.start()

    def piece(kind, zq, p, c, both=1):
        if kind == 0:
            return wqf.at[pl.ds(pl.multiple_of((zq * 2 + p) * rq, rq), both * rq), ds(c * 768, 768)]
        return wof.at[pl.ds(pl.multiple_of((zq * 2 + p) * ro, ro), both * ro), ds(c * 512, 512)]

    def own_piece(kind):
        return wq_ref.at[:, ds(core * 768, 768)] if kind == 0 else wo_ref.at[:, ds(core * 512, 512)]

    def z_copy(kind, e, zq):
        i = kind * 4 + e
        return remote(own_piece(kind), piece(kind, zq, par, core), zs.at[i], zr.at[i], z_to(e))

    def y_copy(kind, way, e, zq, to):
        ref, i = piece(kind, zq, par, core), (kind * 3 + way) * 4 + e
        return remote(ref, ref, ys.at[i], yr.at[i], y_to(to))

    def x_copy(kind, slot, zq, p):
        ref, i = piece(kind, zq, p, core), kind * 17 + slot
        return remote(ref, ref, xs.at[i], xr.at[i], x_to)

    def x_own(kind):
        i = kind * 17 + 16
        return remote(own_piece(kind), piece(kind, z, par, core), xs.at[i], xr.at[i], x_to)

    def s_copy(kind, slot, zq, c):
        ref, i = piece(kind, zq, 0, c, 2), kind * 17 + slot
        return remote(ref, ref, ss.at[i], sr.at[i], sib)

    def s_own(kind, c):
        ref, i = piece(kind, z, 1 - par, c), kind * 17 + 16
        return remote(ref, ref, ss.at[i], sr.at[i], sib)

    def each(yy, do):
        def step(e, carry):
            @pl.when(exists(yy, e))
            def _():
                do(e)

            return carry

        lax.fori_loop(0, 4, step, 0)

    def begin(kind):
        each(y, lambda e: z_copy(kind, e, z).start())
        x_own(kind).start()

    def hop_z(kind):
        def do(e):
            zq = source(y, e)
            z_copy(kind, e, zq).wait_recv()
            y_copy(kind, 0, e, zq, 0).start()
            y_copy(kind, 1, e, zq, 1).start()
            x_copy(kind, e, zq, par).start()

        each(y, do)

    def hop_y(kind):
        def near(e):
            zq = source(line(1, core), e)
            y_copy(kind, core, e, zq, core).wait_recv()
            y_copy(kind, 2, e, zq, core).start()
            x_copy(kind, 4 + e, zq, par).start()

        def other(e):
            zq = source(line(2, core), e)
            y_copy(kind, 1 - core, e, zq, core).wait_recv()
            x_copy(kind, 8 + e, zq, par).start()

        each(line(1, core), near)
        each(line(2, core), other)

    def hop_y2(kind):
        def do(e):
            zq = source(line(3, core), e)
            y_copy(kind, 2, e, zq, core).wait_recv()
            x_copy(kind, 12 + e, zq, par).start()

        each(line(3, core), do)

    def hop_x(kind):
        x_copy(kind, 16, z, 1 - par).wait_recv()
        s_own(kind, core).start()
        for group in range(4):
            def do(e, group=group):
                zq = source(line(group, core), e)
                x_copy(kind, group * 4 + e, zq, 1 - par).wait_recv()
                s_copy(kind, group * 4 + e, zq, core).start()

            each(line(group, core), do)

    def finish(kind):
        s_own(kind, 1 - core).wait_recv()
        for group in range(4):
            def do(e, group=group):
                s_copy(kind, group * 4 + e, source(line(group, 1 - core), e), 1 - core).wait_recv()

            each(line(group, 1 - core), do)

    def all_sent(kind):
        x_own(kind).wait_send()
        s_own(kind, core).wait_send()

        def first(e):
            z_copy(kind, e, z).wait_send()
            y_copy(kind, 0, e, source(y, e), 0).wait_send()
            y_copy(kind, 1, e, source(y, e), 1).wait_send()

        each(y, first)
        each(line(1, core), lambda e: y_copy(kind, 2, e, source(line(1, core), e), core).wait_send())
        for group in range(4):
            def do(e, group=group):
                zq = source(line(group, core), e)
                x_copy(kind, group * 4 + e, zq, par).wait_send()
                s_copy(kind, group * 4 + e, zq, core).wait_send()

            each(line(group, core), do)

    local = [
        pltpu.make_async_copy(wq_ref, wqf.at[ds(lon * rq, rq), :], own_sem.at[0]),
        pltpu.make_async_copy(wo_ref, wof.at[ds(lon * ro, ro), :], own_sem.at[1]),
        pltpu.make_async_copy(gain_hbm, gain_ref, own_sem.at[2]),
        pltpu.make_async_copy(bias_hbm, bias_ref, own_sem.at[3]),
        in_t[1],
        in_g[1],
    ]
    begin(0)
    for copy in local:
        copy.start()
    hop_z(0)
    hop_y(0)
    hop_y2(0)

    def rows_of(land, field):
        def step(t, carry):
            k, i = 2 * (t // 3), 2 * lax.rem(t, 3)
            two = [land[k + n, pl.ds(i, 2)].reshape(24, D) for n in (0, 1)]
            field[ds(t * 48, 48), :] = jnp.concatenate(two, axis=0)
            return carry

        lax.fori_loop(0, 6, step, 0)

    for copy in in_t[0]:
        copy.wait_recv()
    for copy in local:
        copy.wait()
    rows_of(land_t, xw)
    hop_x(0)
    begin(1)
    for copy in in_g[0]:
        copy.start()
    finish(0)

    def project(n, carry):
        cols = ds(n * 256, 256)
        packed[:, cols] = nn(xw[...], wqf[:, cols]).astype(BF)
        return carry

    lax.fori_loop(0, 3 * INNER // 256, project, 0)
    hop_z(1)

    lane_head = lax.broadcasted_iota(jnp.int32, (TOK, GW), 1) // HEAD_DIM
    banned = jnp.where(lat == n_lat - 1, -1e30, 0.0).astype(F32)

    def spread(rows):
        return [rows * (lane_head[0:1] == h).astype(F32).astype(BF) for h in range(GROUP)]

    def gather_heads(wide):
        out = wide[0:TOK, :]
        for h in range(1, GROUP):
            out = jnp.where(lane_head == h, wide[h * TOK : (h + 1) * TOK, :], out)
        return out

    def columns(g):
        return [ds(n * INNER + g * GW, GW) for n in range(3)]

    def narrow(left, right):
        def step(c, carry):
            cols = ds(c * 384, 384)
            wide[cols, :] = tn(left(cols), right)
            return carry

        lax.fori_loop(0, WIDE // 384, step, 0)
        return gather_heads(wide).astype(BF)

    def forward(g, carry):
        q_at, k_at, v_at = columns(g)
        for h, rows in enumerate(spread(packed[:, q_at])):
            qblk[g, h * TOK : (h + 1) * TOK, :] = rows

        def score(c, carry):
            cols = ds(c * 384, 384)
            scores[:, cols] = nt(packed[:, k_at], qblk[g, cols, :])
            return carry

        lax.fori_loop(0, WIDE // 384, score, 0)

        @pl.when(g == 0)
        def _():
            hop_y(1)

        def soften(c, carry):
            cols = ds(c * 128, 128)
            query = lax.rem(c * 128 + lax.broadcasted_iota(jnp.int32, (1, 128), 1), TOK)
            side = (query >= TOK // 2).astype(F32)
            s = jnp.concatenate(
                [scores[: TOK // 2, cols] + side * banned, scores[TOK // 2 :, cols] + (1.0 - side) * banned], axis=0
            )
            top = jnp.max(s, axis=0, keepdims=True)
            e = jnp.exp((s - top) * (HEAD_DIM ** -0.5))
            pt[g, :, cols] = (e * (1.0 / jnp.sum(e, axis=0, keepdims=True))).astype(BF)
            return carry

        lax.fori_loop(0, WIDE // 128, soften, 0, unroll=3)
        heads[:, q_at] = narrow(lambda cols: pt[g, :, cols], packed[:, v_at])

        @pl.when(g == 0)
        def _():
            hop_y2(1)

        return carry

    lax.fori_loop(0, HEADS // GROUP, forward, 0)
    hop_x(1)
    for copy in in_g[0]:
        copy.wait_recv()
    rows_of(land_g, gw)
    finish(1)

    def out_project(n, carry):
        cols = ds(n * 256, 256)
        attn[:, cols] = nn(heads[...], wof[:, cols]).astype(BF)
        return carry

    lax.fori_loop(0, D // 256, out_project, 0)

    def norm(c, carry):
        rows = ds(c * ROWS, ROWS)
        a = attn[rows, :].astype(F32)
        gain = gain_ref[...]
        scaled = gw[rows, :].astype(F32) * gain
        centered = a - jnp.mean(a, axis=-1, keepdims=True)
        level = scaled - jnp.mean(scaled, axis=-1, keepdims=True)
        inverse = lax.rsqrt(jnp.mean(centered * centered, axis=-1, keepdims=True) + EPS)
        along = jnp.mean(scaled * centered, axis=-1, keepdims=True) * inverse
        normed = centered * inverse
        mixed[rows, :] = (xw[rows, :].astype(F32) + normed * gain + bias_ref[...]).astype(BF)
        agrad[rows, :] = ((level - normed * along) * inverse).astype(BF)
        return carry

    lax.fori_loop(0, TOK // ROWS, norm, 0, unroll=3)

    def halo_out(field, rows, land, out):
        def step(t, carry):
            k, i = 2 * (t // 3), 2 * lax.rem(t, 3)
            block = rows[ds(t * 48, 48), :]
            for n in (0, 1):
                land[k + n, pl.ds(i, 2)] = block[n * 24 : (n + 1) * 24].reshape(2, HALF, LEV, D)
            return carry

        lax.fori_loop(0, 6, step, 0)
        copies = [
            remote(land.at[k], quarter(out, k), hs.at[(field + 2) * 4 + k], hr.at[(field + 2) * 4 + k], who)
            for k, who in ((1, east), (2, south), (3, far))
        ]
        keep = pltpu.make_async_copy(land.at[0], quarter(out, 0), own_sem.at[6 + field])
        for copy in copies:
            copy.start()
        keep.start()
        return copies, keep

    out_m = halo_out(0, mixed, land_t, m_out)

    def back_project(n, carry):
        cols = ds(n * 256, 256)
        hgrad[:, cols] = nt(agrad[...], wof[cols, :]).astype(BF)
        return carry

    lax.fori_loop(0, INNER // 256, back_project, 0)

    def backward(g, carry):
        q_at, k_at, v_at = columns(g)
        for h, rows in enumerate(spread(hgrad[:, q_at])):
            doblk[h * TOK : (h + 1) * TOK, :] = rows

        def prob_grad(c, carry):
            cols = ds(c * 384, 384)
            scores[:, cols] = nt(packed[:, v_at], doblk[cols, :])
            return carry

        lax.fori_loop(0, WIDE // 384, prob_grad, 0)

        def score_grad(c, carry):
            cols = ds(c * 128, 128)
            p, dp = pt[g, :, cols].astype(F32), scores[:, cols]
            total = jnp.sum(p * dp, axis=0, keepdims=True)
            dst[:, cols] = (p * (dp - total) * (HEAD_DIM ** -0.5)).astype(BF)
            return carry

        lax.fori_loop(0, WIDE // 128, score_grad, 0, unroll=3)
        pgrad[:, q_at] = narrow(lambda cols: dst[:, cols], packed[:, k_at])
        pgrad[:, v_at] = nn(pt[g], doblk[...]).astype(BF)
        pgrad[:, k_at] = nn(dst[...], qblk[g]).astype(BF)
        return carry

    lax.fori_loop(0, HEADS // GROUP, backward, 0)

    def unproject(n, carry):
        cols = ds(n * 256, 256)
        sg = nt(pgrad[...], wqf[cols, :]).astype(BF).astype(F32)
        tgrad[:, cols] = (gw[:, cols].astype(F32) + sg).astype(BF)
        return carry

    lax.fori_loop(0, D // 256, unproject, 0)
    out_d = halo_out(1, tgrad, land_g, d_out)

    for kind in (0, 1):
        all_sent(kind)
    for copy in in_t[0] + in_g[0]:
        copy.wait_send()
    for copies, keep in (out_m, out_d):
        keep.wait()
        for copy in copies:
            copy.wait()


def per_device(n_lat, n_lon, tokens, qkv_weight, out_weight, norm_gain, norm_bias, mixed_grad):
    hbm = pl.BlockSpec(memory_space=pltpu.HBM)
    cells = (WIN, WIN, LEV, D)
    m_out, d_out = pl.pallas_call(
        functools.partial(kernel, n_lat, n_lon),
        out_shape=[jax.ShapeDtypeStruct(cells, BF)] * 2,
        in_specs=[hbm] * 6,
        out_specs=[pl.BlockSpec(memory_space=pl.ANY)] * 2,
        scratch_shapes=[
            pltpu.VMEM((D, 3 * INNER), BF),
            pltpu.VMEM((INNER, D), BF),
            pltpu.VMEM((1, D), F32),
            pltpu.VMEM((1, D), F32),
            pltpu.VMEM((4, HALF, HALF, LEV, D), BF),
            pltpu.VMEM((4, HALF, HALF, LEV, D), BF),
            pltpu.VMEM((TOK, D), BF),
            pltpu.VMEM((TOK, D), BF),
            pltpu.VMEM((TOK, 3 * INNER), BF),
            pltpu.VMEM((TOK, INNER), BF),
            pltpu.VMEM((TOK, D), BF),
            pltpu.VMEM((TOK, D), BF),
            pltpu.VMEM((TOK, INNER), BF),
            pltpu.VMEM((TOK, 3 * INNER), BF),
            pltpu.VMEM((TOK, WIDE), F32),
            pltpu.VMEM((2, TOK, WIDE), BF),
            pltpu.VMEM((TOK, WIDE), BF),
            pltpu.VMEM((2, WIDE, GW), BF),
            pltpu.VMEM((WIDE, GW), BF),
            pltpu.VMEM((WIDE, GW), F32),
            pltpu.VMEM((TOK, D), BF),
            pltpu.VMEM((TOK, D), BF),
            pltpu.SemaphoreType.DMA((8,)),
            pltpu.SemaphoreType.DMA((8,)),
            pltpu.SemaphoreType.DMA((8,)),
            pltpu.SemaphoreType.DMA((24,)),
            pltpu.SemaphoreType.DMA((24,)),
            pltpu.SemaphoreType.DMA((34,)),
            pltpu.SemaphoreType.DMA((34,)),
            pltpu.SemaphoreType.DMA((34,)),
            pltpu.SemaphoreType.DMA((34,)),
            pltpu.SemaphoreType.DMA((16,)),
            pltpu.SemaphoreType.DMA((16,)),
        ],
        compiler_params=pltpu.CompilerParams(
            collective_id=0, has_side_effects=True, vmem_limit_bytes=63 * 1024 * 1024
        ),
    )(
        tokens.transpose(1, 2, 0, 3), mixed_grad.transpose(1, 2, 0, 3), qkv_weight, out_weight,
        norm_gain.reshape(1, D), norm_bias.reshape(1, D),
    )
    return m_out.transpose(2, 0, 1, 3), d_out.transpose(2, 0, 1, 3)


def solution(mesh):
    placed = (
        P(None, "lat", "lon", None),
        P("lon", None),
        P("lon", None),
        P(),
        P(),
        P(None, "lat", "lon", None),
    )
    return jax.shard_map(
        functools.partial(per_device, mesh.shape["lat"], mesh.shape["lon"]),
        mesh=mesh,
        in_specs=placed,
        out_specs=(P(None, "lat", "lon", None), P(None, "lat", "lon", None)),
        check_vma=False,
    )
```

```python
import functools

import jax
import jax.numpy as jnp
from jax import lax
from jax.experimental import pallas as pl
from jax.experimental.pallas import tpu as pltpu
from jax.sharding import PartitionSpec as P

MESH = pl.DeviceIdType.MESH
BF = jnp.bfloat16
F32 = jnp.float32

D = 1024
HEADS = 8
HEAD_DIM = 64
LEV = 2
WIN = 12
INNER = 512
HALF = 6
TOK = LEV * WIN * WIN
QUARTER = TOK // 4
GROUP = 4
GW = GROUP * HEAD_DIM
WIDE = GROUP * TOK
ROWS = 32
EPS = 1e-05

HALVES = ((1, 1), (1, 0), (0, 1), (0, 0))


def nt(a, b):
    return lax.dot_general(a, b, (((1,), (1,)), ((), ())), preferred_element_type=F32)


def nn(a, b):
    return lax.dot_general(a, b, (((1,), (0,)), ((), ())), preferred_element_type=F32)


def tn(a, b):
    return lax.dot_general(a, b, (((0,), (0,)), ((), ())), preferred_element_type=F32)


def ds(start, size):
    return pl.ds(pl.multiple_of(start, size), size)


def kernel(
    n_lat, n_lon,
    t_ref, g_ref, wq_ref, wo_ref, gain_hbm, bias_hbm,
    m_out, d_out,
    wqf, wof, gain_ref, bias_ref, land_t, land_g, xw, gw, packed, heads, attn, agrad, hgrad, pgrad,
    scores, pt, dst, qblk, doblk, wide, mixed, tgrad,
    own_sem, zs, zr, ys, yr, xs, xr, ss, sr, hs, hr,
):
    lat, lon = lax.axis_index("lat"), lax.axis_index("lon")
    nz, ny = n_lon // 2, n_lat // 4
    rq, ro = D // n_lon, INNER // n_lon
    core, par, z = lax.rem(lat, 2), lax.rem(lon, 2), lon // 2
    half, y = lat // (2 * ny), lax.rem(lat // 2, ny)
    lat_lo, lat_hi = lax.rem(lat + n_lat - 1, n_lat), lax.rem(lat + 1, n_lat)
    lon_lo, lon_hi = lax.rem(lon + n_lon - 1, n_lon), lax.rem(lon + 1, n_lon)
    sib = (lat + 1 - 2 * core, lon)
    differ = lax.rem(par + core, 2)
    across = lon + 1 - 2 * par
    x_to = (lax.rem(lat + differ * (n_lat // 2), n_lat), across)
    x_from = (lax.rem(lat + (1 - differ) * (n_lat // 2), n_lat), across)
    west, north, diag = (lat, lon_lo), (lat_lo, lon), (lat_lo, lon_lo)
    east, south, far = (lat, lon_hi), (lat_hi, lon), (lat_hi, lon_hi)

    def offset(yy, e):
        far_pair = e // 2
        size = (1 - far_pair) * (yy + 1) + far_pair * (2 * ny - yy)
        return (1 - 2 * lax.rem(e, 2)) * size

    def z_to(e):
        return (lat, 2 * lax.rem(z + offset(y, e) + nz, nz) + par)

    def source(yy, e):
        return lax.rem(z - offset(yy, e) + nz, nz)

    def exists(yy, e):
        return jnp.logical_or(yy > 0, e < 3)

    def y_to(way):
        return ((half * ny + lax.rem(y + 1 - 2 * way + ny, ny)) * 2 + core, lon)

    def line(group, c):
        return lax.rem(y + ny + (0, 2 * c - 1, 1 - 2 * c, 2)[group], ny)

    barrier = pltpu.get_barrier_semaphore()
    met = [z_to(e) for e in range(4)]
    met += [y_to(0), y_to(1), sib, x_to, x_from, west, north, diag, east, south, far]
    for who in met:
        pl.semaphore_signal(barrier, inc=1, device_id=who, device_id_type=MESH)
    pl.semaphore_wait(barrier, len(met))

    def remote(src, dst, send, recv, who):
        return pltpu.make_async_remote_copy(
            src_ref=src, dst_ref=dst, send_sem=send, recv_sem=recv, device_id=who, device_id_type=MESH
        )

    def quarter(ref, k):
        i, j = HALVES[k]
        return ref.at[pl.ds(i * HALF, HALF), pl.ds(j * HALF, HALF)]

    def halo_in(field, src, land):
        copies = [
            remote(quarter(src, k), land.at[k], hs.at[field * 4 + k], hr.at[field * 4 + k], who)
            for k, who in ((1, west), (2, north), (3, diag))
        ]
        return copies, pltpu.make_async_copy(quarter(src, 0), land.at[0], own_sem.at[4 + field])

    in_t = halo_in(0, t_ref, land_t)
    in_g = halo_in(1, g_ref, land_g)
    def piece(kind, zq, p, c, both=1):
        if kind == 0:
            return wqf.at[pl.ds(pl.multiple_of((zq * 2 + p) * rq, rq), both * rq), ds(c * 768, 768)]
        return wof.at[pl.ds(pl.multiple_of((zq * 2 + p) * ro, ro), both * ro), ds(c * 512, 512)]

    def own_piece(kind):
        return wq_ref.at[:, ds(core * 768, 768)] if kind == 0 else wo_ref.at[:, ds(core * 512, 512)]

    def z_copy(kind, e, zq):
        i = kind * 4 + e
        return remote(own_piece(kind), piece(kind, zq, par, core), zs.at[i], zr.at[i], z_to(e))

    def y_copy(kind, way, e, zq, to):
        ref, i = piece(kind, zq, par, core), (kind * 3 + way) * 4 + e
        return remote(ref, ref, ys.at[i], yr.at[i], y_to(to))

    def x_copy(kind, slot, zq, p):
        ref, i = piece(kind, zq, p, core), kind * 17 + slot
        return remote(ref, ref, xs.at[i], xr.at[i], x_to)

    def x_own(kind):
        i = kind * 17 + 16
        return remote(own_piece(kind), piece(kind, z, par, core), xs.at[i], xr.at[i], x_to)

    def s_copy(kind, slot, zq, c):
        ref, i = piece(kind, zq, 0, c, 2), kind * 17 + slot
        return remote(ref, ref, ss.at[i], sr.at[i], sib)

    def s_own(kind, c):
        ref, i = piece(kind, z, 1 - par, c), kind * 17 + 16
        return remote(ref, ref, ss.at[i], sr.at[i], sib)

    def each(yy, do, waves=(0, 1)):
        def step(e, carry):
            @pl.when(exists(yy, e))
            def _():
                do(e)

            return carry

        lax.fori_loop(2 * waves[0], 2 * waves[-1] + 2, step, 0)

    def begin(kind, waves):
        each(y, lambda e: z_copy(kind, e, z).start(), waves)

    def hop_z(kind, waves, then=None):
        each(y, lambda e: z_copy(kind, e, source(y, e)).wait_recv(), waves)
        if then is not None:
            then()

        def do(e):
            zq = source(y, e)
            y_copy(kind, 0, e, zq, 0).start()
            y_copy(kind, 1, e, zq, 1).start()
            x_copy(kind, e, zq, par).start()

        each(y, do, waves)

    def hop_y(kind, waves):
        def near(e):
            zq = source(line(1, core), e)
            y_copy(kind, core, e, zq, core).wait_recv()
            y_copy(kind, 2, e, zq, core).start()
            x_copy(kind, 4 + e, zq, par).start()

        def other(e):
            zq = source(line(2, core), e)
            y_copy(kind, 1 - core, e, zq, core).wait_recv()
            x_copy(kind, 8 + e, zq, par).start()

        each(line(1, core), near, waves)
        each(line(2, core), other, waves)

    def hop_y2(kind, waves):
        def do(e):
            zq = source(line(3, core), e)
            y_copy(kind, 2, e, zq, core).wait_recv()
            x_copy(kind, 12 + e, zq, par).start()

        each(line(3, core), do, waves)

    def hop_x(kind, waves):
        if waves[0] == 0:
            x_copy(kind, 16, z, 1 - par).wait_recv()
            s_own(kind, core).start()
        for group in range(4):
            def do(e, group=group):
                zq = source(line(group, core), e)
                x_copy(kind, group * 4 + e, zq, 1 - par).wait_recv()
                s_copy(kind, group * 4 + e, zq, core).start()

            each(line(group, core), do, waves)

    def finish(kind):
        s_own(kind, 1 - core).wait_recv()
        for group in range(4):
            def do(e, group=group):
                s_copy(kind, group * 4 + e, source(line(group, 1 - core), e), 1 - core).wait_recv()

            each(line(group, 1 - core), do)

    def all_sent(kind):
        x_own(kind).wait_send()
        s_own(kind, core).wait_send()

        def first(e):
            z_copy(kind, e, z).wait_send()
            y_copy(kind, 0, e, source(y, e), 0).wait_send()
            y_copy(kind, 1, e, source(y, e), 1).wait_send()

        each(y, first)
        each(line(1, core), lambda e: y_copy(kind, 2, e, source(line(1, core), e), core).wait_send())
        for group in range(4):
            def do(e, group=group):
                zq = source(line(group, core), e)
                x_copy(kind, group * 4 + e, zq, par).wait_send()
                s_copy(kind, group * 4 + e, zq, core).wait_send()

            each(line(group, core), do)

    local = [
        pltpu.make_async_copy(wq_ref, wqf.at[ds(lon * rq, rq), :], own_sem.at[0]),
        pltpu.make_async_copy(wo_ref, wof.at[ds(lon * ro, ro), :], own_sem.at[1]),
        pltpu.make_async_copy(gain_hbm, gain_ref, own_sem.at[2]),
        pltpu.make_async_copy(bias_hbm, bias_ref, own_sem.at[3]),
        in_t[1],
        in_g[1],
    ]
    def rows_of(land, field):
        def step(t, carry):
            k, i = 2 * (t // 3), 2 * lax.rem(t, 3)
            two = [land[k + n, pl.ds(i, 2)].reshape(24, D) for n in (0, 1)]
            field[ds(t * 48, 48), :] = jnp.concatenate(two, axis=0)
            return carry

        lax.fori_loop(0, 6, step, 0)

    both = (0, 1)
    begin(0, (0,))
    x_own(0).start()
    for copy in local:
        copy.start()

    def second():
        begin(0, (1,))
        for copy in in_t[0]:
            copy.start()

    hop_z(0, (0,), second)
    hop_y(0, (0,))
    hop_y2(0, (0,))

    def third():
        begin(1, both)
        x_own(1).start()
        for copy in in_g[0]:
            copy.start()

    hop_z(0, (1,), third)
    hop_x(0, (0,))
    hop_y(0, (1,))
    hop_y2(0, (1,))
    for copy in in_t[0]:
        copy.wait_recv()
    for copy in local:
        copy.wait()
    rows_of(land_t, xw)
    hop_x(0, (1,))
    hop_z(1, both)
    for copy in in_g[0]:
        copy.wait_recv()
    rows_of(land_g, gw)
    hop_y(1, both)
    finish(0)

    for n in range(3 * INNER // 256):
        cols = slice(n * 256, n * 256 + 256)
        packed[:, cols] = nn(xw[...], wqf[:, cols]).astype(BF)
    hop_y2(1, both)

    lane_head = lax.broadcasted_iota(jnp.int32, (TOK, GW), 1) // HEAD_DIM
    banned = jnp.where(lat == n_lat - 1, -1e30, 0.0).astype(F32)

    def spread(rows):
        return [rows * (lane_head[0:1] == h).astype(F32).astype(BF) for h in range(GROUP)]

    def columns(g):
        return [ds(n * INNER + g * GW, GW) for n in range(3)]

    def turned(block):
        return block.astype(F32).T.astype(BF)

    def narrow(right, left):
        for c in range(0, WIDE, 384):
            wide[:, c : c + 384] = nn(right, left(slice(c, c + 384)))
        blocks = [wide[h * HEAD_DIM : (h + 1) * HEAD_DIM, h * TOK : (h + 1) * TOK] for h in range(GROUP)]
        return jnp.concatenate(blocks, axis=0).T.astype(BF)

    def forward(g, carry):
        q_at, k_at, v_at = columns(g)
        for h, rows in enumerate(spread(packed[:, q_at])):
            qblk[g, h * TOK : (h + 1) * TOK, :] = rows

        for c in range(0, WIDE, 384):
            scores[:, c : c + 384] = nt(packed[:, k_at], qblk[g, c : c + 384, :])
        for c in range(0, WIDE, 128):
            cols = slice(c, c + 128)
            query = lax.rem(c + lax.broadcasted_iota(jnp.int32, (1, 128), 1), TOK)
            side = (query >= TOK // 2).astype(F32)
            s = jnp.concatenate(
                [scores[: TOK // 2, cols] + side * banned, scores[TOK // 2 :, cols] + (1.0 - side) * banned], axis=0
            )
            top = jnp.max(s, axis=0, keepdims=True)
            e = jnp.exp((s - top) * (HEAD_DIM ** -0.5))
            pt[g, :, cols] = (e * (1.0 / jnp.sum(e, axis=0, keepdims=True))).astype(BF)
        heads[:, q_at] = narrow(turned(packed[:, v_at]), lambda cols: pt[g, :, cols])

        @pl.when(g == 0)
        def _():
            hop_x(1, both)

        return carry

    lax.fori_loop(0, HEADS // GROUP, forward, 0)
    finish(1)

    for n in range(0, D, 256):
        attn[:, n : n + 256] = nn(heads[...], wof[:, n : n + 256]).astype(BF)

    def norm(c, carry):
        rows = ds(c * ROWS, ROWS)
        a = attn[rows, :].astype(F32)
        gain = gain_ref[...]
        scaled = gw[rows, :].astype(F32) * gain
        centered = a - jnp.mean(a, axis=-1, keepdims=True)
        level = scaled - jnp.mean(scaled, axis=-1, keepdims=True)
        inverse = lax.rsqrt(jnp.mean(centered * centered, axis=-1, keepdims=True) + EPS)
        along = jnp.mean(scaled * centered, axis=-1, keepdims=True) * inverse
        normed = centered * inverse
        mixed[rows, :] = (xw[rows, :].astype(F32) + normed * gain + bias_ref[...]).astype(BF)
        agrad[rows, :] = ((level - normed * along) * inverse).astype(BF)
        return carry

    lax.fori_loop(0, TOK // ROWS, norm, 0, unroll=3)

    def halo_out(field, rows, land, out):
        def step(t, carry):
            k, i = 2 * (t // 3), 2 * lax.rem(t, 3)
            block = rows[ds(t * 48, 48), :]
            for n in (0, 1):
                land[k + n, pl.ds(i, 2)] = block[n * 24 : (n + 1) * 24].reshape(2, HALF, LEV, D)
            return carry

        lax.fori_loop(0, 6, step, 0)
        copies = [
            remote(land.at[k], quarter(out, k), hs.at[(field + 2) * 4 + k], hr.at[(field + 2) * 4 + k], who)
            for k, who in ((1, east), (2, south), (3, far))
        ]
        keep = pltpu.make_async_copy(land.at[0], quarter(out, 0), own_sem.at[6 + field])
        for copy in copies:
            copy.start()
        keep.start()
        return copies, keep

    out_m = halo_out(0, mixed, land_t, m_out)

    for n in range(0, INNER, 256):
        hgrad[:, n : n + 256] = nt(agrad[...], wof[n : n + 256, :]).astype(BF)

    def backward(g, carry):
        q_at, k_at, v_at = columns(g)
        for h, rows in enumerate(spread(hgrad[:, q_at])):
            doblk[h * TOK : (h + 1) * TOK, :] = rows

        for c in range(0, WIDE, 384):
            scores[:, c : c + 384] = nt(packed[:, v_at], doblk[c : c + 384, :])
        for c in range(0, WIDE, 128):
            cols = slice(c, c + 128)
            p, dp = pt[g, :, cols].astype(F32), scores[:, cols]
            total = jnp.sum(p * dp, axis=0, keepdims=True)
            dst[:, cols] = (p * (dp - total) * (HEAD_DIM ** -0.5)).astype(BF)
        pgrad[:, q_at] = narrow(turned(packed[:, k_at]), lambda cols: dst[:, cols])
        pgrad[:, v_at] = nn(pt[g], doblk[...]).astype(BF)
        pgrad[:, k_at] = nn(dst[...], qblk[g]).astype(BF)
        return carry

    lax.fori_loop(0, HEADS // GROUP, backward, 0)

    for n in range(0, D, 256):
        cols = slice(n, n + 256)
        sg = nt(pgrad[...], wqf[cols, :]).astype(BF).astype(F32)
        tgrad[:, cols] = (gw[:, cols].astype(F32) + sg).astype(BF)
    out_d = halo_out(1, tgrad, land_g, d_out)

    for kind in (0, 1):
        all_sent(kind)
    for copy in in_t[0] + in_g[0]:
        copy.wait_send()
    for copies, keep in (out_m, out_d):
        keep.wait()
        for copy in copies:
            copy.wait()


def per_device(n_lat, n_lon, tokens, qkv_weight, out_weight, norm_gain, norm_bias, mixed_grad):
    hbm = pl.BlockSpec(memory_space=pltpu.HBM)
    cells = (WIN, WIN, LEV, D)
    m_out, d_out = pl.pallas_call(
        functools.partial(kernel, n_lat, n_lon),
        out_shape=[jax.ShapeDtypeStruct(cells, BF)] * 2,
        in_specs=[hbm] * 6,
        out_specs=[pl.BlockSpec(memory_space=pl.ANY)] * 2,
        scratch_shapes=[
            pltpu.VMEM((D, 3 * INNER), BF),
            pltpu.VMEM((INNER, D), BF),
            pltpu.VMEM((1, D), F32),
            pltpu.VMEM((1, D), F32),
            pltpu.VMEM((4, HALF, HALF, LEV, D), BF),
            pltpu.VMEM((4, HALF, HALF, LEV, D), BF),
            pltpu.VMEM((TOK, D), BF),
            pltpu.VMEM((TOK, D), BF),
            pltpu.VMEM((TOK, 3 * INNER), BF),
            pltpu.VMEM((TOK, INNER), BF),
            pltpu.VMEM((TOK, D), BF),
            pltpu.VMEM((TOK, D), BF),
            pltpu.VMEM((TOK, INNER), BF),
            pltpu.VMEM((TOK, 3 * INNER), BF),
            pltpu.VMEM((TOK, WIDE), F32),
            pltpu.VMEM((2, TOK, WIDE), BF),
            pltpu.VMEM((TOK, WIDE), BF),
            pltpu.VMEM((2, WIDE, GW), BF),
            pltpu.VMEM((WIDE, GW), BF),
            pltpu.VMEM((GW, WIDE), F32),
            pltpu.VMEM((TOK, D), BF),
            pltpu.VMEM((TOK, D), BF),
            pltpu.SemaphoreType.DMA((8,)),
            pltpu.SemaphoreType.DMA((8,)),
            pltpu.SemaphoreType.DMA((8,)),
            pltpu.SemaphoreType.DMA((24,)),
            pltpu.SemaphoreType.DMA((24,)),
            pltpu.SemaphoreType.DMA((34,)),
            pltpu.SemaphoreType.DMA((34,)),
            pltpu.SemaphoreType.DMA((34,)),
            pltpu.SemaphoreType.DMA((34,)),
            pltpu.SemaphoreType.DMA((16,)),
            pltpu.SemaphoreType.DMA((16,)),
        ],
        compiler_params=pltpu.CompilerParams(
            collective_id=0, has_side_effects=True, vmem_limit_bytes=63 * 1024 * 1024
        ),
    )(
        tokens.transpose(1, 2, 0, 3), mixed_grad.transpose(1, 2, 0, 3), qkv_weight, out_weight,
        norm_gain.reshape(1, D), norm_bias.reshape(1, D),
    )
    return m_out.transpose(2, 0, 1, 3), d_out.transpose(2, 0, 1, 3)


def solution(mesh):
    placed = (
        P(None, "lat", "lon", None),
        P("lon", None),
        P("lon", None),
        P(),
        P(),
        P(None, "lat", "lon", None),
    )
    return jax.shard_map(
        functools.partial(per_device, mesh.shape["lat"], mesh.shape["lon"]),
        mesh=mesh,
        in_specs=placed,
        out_specs=(P(None, "lat", "lon", None), P(None, "lat", "lon", None)),
        check_vma=False,
    )
```

```python
import functools

import jax
import jax.numpy as jnp
from jax import lax
from jax.experimental import pallas as pl
from jax.experimental.pallas import tpu as pltpu
from jax.sharding import PartitionSpec as P

MESH = pl.DeviceIdType.MESH
BF = jnp.bfloat16
F32 = jnp.float32

D = 1024
HEADS = 8
HEAD_DIM = 64
LEV = 2
WIN = 12
INNER = 512
HALF = 6
TOK = LEV * WIN * WIN
QUARTER = TOK // 4
GROUP = 4
GW = GROUP * HEAD_DIM
WIDE = GROUP * TOK
ROWS = 32
EPS = 1e-05

HALVES = ((1, 1), (1, 0), (0, 1), (0, 0))


def nt(a, b):
    return lax.dot_general(a, b, (((1,), (1,)), ((), ())), preferred_element_type=F32)


def nn(a, b):
    return lax.dot_general(a, b, (((1,), (0,)), ((), ())), preferred_element_type=F32)


def tn(a, b):
    return lax.dot_general(a, b, (((0,), (0,)), ((), ())), preferred_element_type=F32)


def ds(start, size):
    return pl.ds(pl.multiple_of(start, size), size)


def kernel(
    n_lat, n_lon,
    t_ref, g_ref, wq_ref, wo_ref, gain_hbm, bias_hbm,
    m_out, d_out,
    comb, wqf, wof, gain_ref, bias_ref, land_t, land_g, xw, gw, packed, heads, attn, agrad, hgrad, pgrad,
    scores, pt, dst, qblk, doblk, wide, mixed, tgrad,
    own_sem, zs, zr, ys, yr, xs, xr, ss, sr, hs, hr,
):
    lat, lon = lax.axis_index("lat"), lax.axis_index("lon")
    nz, ny = n_lon // 2, n_lat // 4
    rq, ro = D // n_lon, INNER // n_lon
    core, par, z = lax.rem(lat, 2), lax.rem(lon, 2), lon // 2
    half, y = lat // (2 * ny), lax.rem(lat // 2, ny)
    lat_lo, lat_hi = lax.rem(lat + n_lat - 1, n_lat), lax.rem(lat + 1, n_lat)
    lon_lo, lon_hi = lax.rem(lon + n_lon - 1, n_lon), lax.rem(lon + 1, n_lon)
    sib = (lat + 1 - 2 * core, lon)
    differ = lax.rem(par + core, 2)
    across = lon + 1 - 2 * par
    x_to = (lax.rem(lat + differ * (n_lat // 2), n_lat), across)
    x_from = (lax.rem(lat + (1 - differ) * (n_lat // 2), n_lat), across)
    west, north, diag = (lat, lon_lo), (lat_lo, lon), (lat_lo, lon_lo)
    east, south, far = (lat, lon_hi), (lat_hi, lon), (lat_hi, lon_hi)

    def offset(yy, e):
        far_pair = e // 2
        size = (1 - far_pair) * (yy + 1) + far_pair * (2 * ny - yy)
        return (1 - 2 * lax.rem(e, 2)) * size

    def z_to(e):
        return (lat, 2 * lax.rem(z + offset(y, e) + nz, nz) + par)

    def source(yy, e):
        return lax.rem(z - offset(yy, e) + nz, nz)

    def y_to(way):
        return ((half * ny + lax.rem(y + 1 - 2 * way + ny, ny)) * 2 + core, lon)

    def line(group, c):
        return lax.rem(y + ny + (0, 2 * c - 1, 1 - 2 * c, 2)[group], ny)

    own = [
        (wq_ref.at[:, 0:D], comb.at[0, par, 0]),
        (wq_ref.at[:, D:], comb.at[1, par, 0, :, 0:INNER]),
        (wo_ref.at[:, 0:INNER], comb.at[1, par, 0, 0:ro, INNER:]),
        (wo_ref.at[:, INNER:], comb.at[1, par, 0, ro:, INNER:]),
    ]
    own = [pltpu.make_async_copy(src, to, own_sem.at[8 + k]) for k, (src, to) in enumerate(own)]
    for copy in own:
        copy.start()

    barrier = pltpu.get_barrier_semaphore()
    met = [z_to(e) for e in range(4)]
    met += [y_to(0), y_to(1), sib, x_to, x_from, west, north, diag, east, south, far]
    for who in met:
        pl.semaphore_signal(barrier, inc=1, device_id=who, device_id_type=MESH)
    for copy in own:
        copy.wait()
    pl.semaphore_wait(barrier, len(met))

    def remote(src, dst, send, recv, who):
        return pltpu.make_async_remote_copy(
            src_ref=src, dst_ref=dst, send_sem=send, recv_sem=recv, device_id=who, device_id_type=MESH
        )

    def quarter(ref, k):
        i, j = HALVES[k]
        return ref.at[pl.ds(i * HALF, HALF), pl.ds(j * HALF, HALF)]

    def halo_in(field, src, land):
        copies = [
            remote(quarter(src, k), land.at[k], hs.at[field * 4 + k], hr.at[field * 4 + k], who)
            for k, who in ((1, west), (2, north), (3, diag))
        ]
        return copies, pltpu.make_async_copy(quarter(src, 0), land.at[0], own_sem.at[4 + field])

    in_t = halo_in(0, t_ref, land_t)
    in_g = halo_in(1, g_ref, land_g)
    def slots(wave, group, count=1):
        return pl.ds(1 + wave * 8 + group * 2, count * 2)

    def z_copy(e):
        return remote(
            comb.at[core, par, 0], comb.at[core, par, 1 + e // 2 * 8 + e % 2], zs.at[e], zr.at[e], z_to(e)
        )

    def y_copy(wave, k):
        src, dst = ((0, 1), (0, 2), (1, 3))[k]
        i = wave * 3 + k
        return remote(
            comb.at[core, par, slots(wave, src)], comb.at[core, par, slots(wave, dst)], ys.at[i], yr.at[i],
            y_to(1 - core if k == 1 else core),
        )

    def x_copy(wave, k, p):
        ref = comb.at[core, p, slots(wave, (0, 1, 3)[k], (1, 2, 1)[k])] if wave < 2 else comb.at[core, p, 0]
        i = wave * 3 + k
        return remote(ref, ref, xs.at[i], xr.at[i], x_to)

    def s_copy(wave, c):
        ref = comb.at[c, :, slots(wave, 0, 4)] if wave < 2 else comb.at[c, 1 - par, 0]
        return remote(ref, ref, ss.at[wave], sr.at[wave], sib)

    def place(wave):
        found = [(c, slots(wave, j).start + i, source(line(j, c), 2 * wave + i))
                 for c in range(2) for j in range(4) for i in range(2)]
        if wave == 0:
            found += [(0, 0, z), (1, 0, z)]
        for c, slot, zq in found:
            for p in range(2):
                rows = ds((zq * 2 + p) * rq, rq)
                if c == 0:
                    wqf[rows, 0:D] = comb[0, p, slot]
                else:
                    out_rows = ds((zq * 2 + p) * ro, ro)
                    wqf[rows, D:] = comb[1, p, slot, :, 0:INNER]
                    wof[out_rows, 0:INNER] = comb[1, p, slot, 0:ro, INNER:]
                    wof[out_rows, INNER:] = comb[1, p, slot, ro:, INNER:]

    local = [
        pltpu.make_async_copy(gain_hbm, gain_ref, own_sem.at[2]),
        pltpu.make_async_copy(bias_hbm, bias_ref, own_sem.at[3]),
        in_t[1],
        in_g[1],
    ]

    def rows_of(land, field):
        def step(t, carry):
            k, i = 2 * (t // 3), 2 * lax.rem(t, 3)
            two = [land[k + n, pl.ds(i, 2)].reshape(24, D) for n in (0, 1)]
            field[ds(t * 48, 48), :] = jnp.concatenate(two, axis=0)
            return carry

        lax.fori_loop(0, 6, step, 0)

    z_copies = [z_copy(e) for e in range(4)]
    for copy in z_copies[:2]:
        copy.start()
    x_copy(2, 0, par).start()
    for copy in local:
        copy.start()

    def from_z(wave):
        for copy in z_copies[2 * wave : 2 * wave + 2]:
            copy.wait_recv()
        if wave == 0:
            for copy in z_copies[2:]:
                copy.start()
        y_copy(wave, 0).start()
        y_copy(wave, 1).start()
        x_copy(wave, 0, par).start()
        for copy in (in_t, in_g)[wave][0]:
            copy.start()

    def from_y(wave):
        y_copy(wave, 0).wait_recv()
        y_copy(wave, 2).start()
        y_copy(wave, 1).wait_recv()
        x_copy(wave, 1, par).start()

    def from_y2(wave):
        y_copy(wave, 2).wait_recv()
        x_copy(wave, 2, par).start()

    def from_x(wave):
        for k in range(3):
            x_copy(wave, k, 1 - par).wait_recv()
        s_copy(wave, core).start()

    from_z(0)
    from_y(0)
    from_y2(0)
    from_z(1)
    x_copy(2, 0, 1 - par).wait_recv()
    s_copy(2, core).start()
    from_x(0)
    from_y(1)
    from_y2(1)
    for copy in in_t[0]:
        copy.wait_recv()
    for copy in local:
        copy.wait()
    rows_of(land_t, xw)
    s_copy(2, 1 - core).wait_recv()
    s_copy(0, 1 - core).wait_recv()
    place(0)
    from_x(1)
    for copy in in_g[0]:
        copy.wait_recv()
    rows_of(land_g, gw)
    s_copy(1, 1 - core).wait_recv()
    place(1)

    for n in range(3 * INNER // 256):
        cols = slice(n * 256, n * 256 + 256)
        packed[:, cols] = nn(xw[...], wqf[:, cols]).astype(BF)

    lane_head = lax.broadcasted_iota(jnp.int32, (TOK, GW), 1) // HEAD_DIM
    banned = jnp.where(lat == n_lat - 1, -1e30, 0.0).astype(F32)

    def spread(rows):
        return [rows * (lane_head[0:1] == h).astype(F32).astype(BF) for h in range(GROUP)]

    def columns(g):
        return [ds(n * INNER + g * GW, GW) for n in range(3)]

    def turned(block):
        return block.astype(F32).T.astype(BF)

    def narrow(right, left):
        for c in range(0, WIDE, 384):
            wide[:, c : c + 384] = nn(right, left(slice(c, c + 384)))
        blocks = [wide[h * HEAD_DIM : (h + 1) * HEAD_DIM, h * TOK : (h + 1) * TOK] for h in range(GROUP)]
        return jnp.concatenate(blocks, axis=0).T.astype(BF)

    def forward(g, carry):
        q_at, k_at, v_at = columns(g)
        for h, rows in enumerate(spread(packed[:, q_at])):
            qblk[g, h * TOK : (h + 1) * TOK, :] = rows

        for c in range(0, WIDE, 384):
            scores[:, c : c + 384] = nt(packed[:, k_at], qblk[g, c : c + 384, :])
        for c in range(0, WIDE, 128):
            cols = slice(c, c + 128)
            query = lax.rem(c + lax.broadcasted_iota(jnp.int32, (1, 128), 1), TOK)
            side = (query >= TOK // 2).astype(F32)
            s = jnp.concatenate(
                [scores[: TOK // 2, cols] + side * banned, scores[TOK // 2 :, cols] + (1.0 - side) * banned], axis=0
            )
            top = jnp.max(s, axis=0, keepdims=True)
            e = jnp.exp((s - top) * (HEAD_DIM ** -0.5))
            pt[g, :, cols] = (e * (1.0 / jnp.sum(e, axis=0, keepdims=True))).astype(BF)
        heads[:, q_at] = narrow(turned(packed[:, v_at]), lambda cols: pt[g, :, cols])

        return carry

    lax.fori_loop(0, HEADS // GROUP, forward, 0)

    for n in range(0, D, 256):
        attn[:, n : n + 256] = nn(heads[...], wof[:, n : n + 256]).astype(BF)

    def norm(c, carry):
        rows = ds(c * ROWS, ROWS)
        a = attn[rows, :].astype(F32)
        gain = gain_ref[...]
        scaled = gw[rows, :].astype(F32) * gain
        centered = a - jnp.mean(a, axis=-1, keepdims=True)
        level = scaled - jnp.mean(scaled, axis=-1, keepdims=True)
        inverse = lax.rsqrt(jnp.mean(centered * centered, axis=-1, keepdims=True) + EPS)
        along = jnp.mean(scaled * centered, axis=-1, keepdims=True) * inverse
        normed = centered * inverse
        mixed[rows, :] = (xw[rows, :].astype(F32) + normed * gain + bias_ref[...]).astype(BF)
        agrad[rows, :] = ((level - normed * along) * inverse).astype(BF)
        return carry

    lax.fori_loop(0, TOK // ROWS, norm, 0, unroll=3)

    def halo_out(field, rows, land, out):
        def step(t, carry):
            k, i = 2 * (t // 3), 2 * lax.rem(t, 3)
            block = rows[ds(t * 48, 48), :]
            for n in (0, 1):
                land[k + n, pl.ds(i, 2)] = block[n * 24 : (n + 1) * 24].reshape(2, HALF, LEV, D)
            return carry

        lax.fori_loop(0, 6, step, 0)
        copies = [
            remote(land.at[k], quarter(out, k), hs.at[(field + 2) * 4 + k], hr.at[(field + 2) * 4 + k], who)
            for k, who in ((1, east), (2, south), (3, far))
        ]
        keep = pltpu.make_async_copy(land.at[0], quarter(out, 0), own_sem.at[6 + field])
        for copy in copies:
            copy.start()
        keep.start()
        return copies, keep

    out_m = halo_out(0, mixed, land_t, m_out)

    for n in range(0, INNER, 256):
        hgrad[:, n : n + 256] = nt(agrad[...], wof[n : n + 256, :]).astype(BF)

    def backward(g, carry):
        q_at, k_at, v_at = columns(g)
        for h, rows in enumerate(spread(hgrad[:, q_at])):
            doblk[h * TOK : (h + 1) * TOK, :] = rows

        for c in range(0, WIDE, 384):
            scores[:, c : c + 384] = nt(packed[:, v_at], doblk[c : c + 384, :])
        for c in range(0, WIDE, 128):
            cols = slice(c, c + 128)
            p, dp = pt[g, :, cols].astype(F32), scores[:, cols]
            total = jnp.sum(p * dp, axis=0, keepdims=True)
            dst[:, cols] = (p * (dp - total) * (HEAD_DIM ** -0.5)).astype(BF)
        pgrad[:, q_at] = narrow(turned(packed[:, k_at]), lambda cols: dst[:, cols])
        pgrad[:, v_at] = nn(pt[g], doblk[...]).astype(BF)
        pgrad[:, k_at] = nn(dst[...], qblk[g]).astype(BF)
        return carry

    lax.fori_loop(0, HEADS // GROUP, backward, 0)

    for n in range(0, D, 256):
        cols = slice(n, n + 256)
        sg = nt(pgrad[...], wqf[cols, :]).astype(BF).astype(F32)
        tgrad[:, cols] = (gw[:, cols].astype(F32) + sg).astype(BF)
    out_d = halo_out(1, tgrad, land_g, d_out)

    for copy in z_copies:
        copy.wait_send()
    for wave in range(2):
        for k in range(3):
            y_copy(wave, k).wait_send()
            x_copy(wave, k, par).wait_send()
        s_copy(wave, core).wait_send()
    x_copy(2, 0, par).wait_send()
    s_copy(2, core).wait_send()
    for copy in in_t[0] + in_g[0]:
        copy.wait_send()
    for copies, keep in (out_m, out_d):
        keep.wait()
        for copy in copies:
            copy.wait()


def per_device(n_lat, n_lon, tokens, qkv_weight, out_weight, norm_gain, norm_bias, mixed_grad):
    hbm = pl.BlockSpec(memory_space=pltpu.HBM)
    cells = (WIN, WIN, LEV, D)
    m_out, d_out = pl.pallas_call(
        functools.partial(kernel, n_lat, n_lon),
        out_shape=[jax.ShapeDtypeStruct(cells, BF)] * 2,
        in_specs=[hbm] * 6,
        out_specs=[pl.BlockSpec(memory_space=pl.ANY)] * 2,
        scratch_shapes=[
            pltpu.VMEM((2, 2, 17, D // n_lon, D), BF),
            pltpu.VMEM((D, 3 * INNER), BF),
            pltpu.VMEM((INNER, D), BF),
            pltpu.VMEM((1, D), F32),
            pltpu.VMEM((1, D), F32),
            pltpu.VMEM((4, HALF, HALF, LEV, D), BF),
            pltpu.VMEM((4, HALF, HALF, LEV, D), BF),
            pltpu.VMEM((TOK, D), BF),
            pltpu.VMEM((TOK, D), BF),
            pltpu.VMEM((TOK, 3 * INNER), BF),
            pltpu.VMEM((TOK, INNER), BF),
            pltpu.VMEM((TOK, D), BF),
            pltpu.VMEM((TOK, D), BF),
            pltpu.VMEM((TOK, INNER), BF),
            pltpu.VMEM((TOK, 3 * INNER), BF),
            pltpu.VMEM((TOK, WIDE), F32),
            pltpu.VMEM((2, TOK, WIDE), BF),
            pltpu.VMEM((TOK, WIDE), BF),
            pltpu.VMEM((2, WIDE, GW), BF),
            pltpu.VMEM((WIDE, GW), BF),
            pltpu.VMEM((GW, WIDE), F32),
            pltpu.VMEM((TOK, D), BF),
            pltpu.VMEM((TOK, D), BF),
            pltpu.SemaphoreType.DMA((12,)),
            pltpu.SemaphoreType.DMA((4,)),
            pltpu.SemaphoreType.DMA((4,)),
            pltpu.SemaphoreType.DMA((6,)),
            pltpu.SemaphoreType.DMA((6,)),
            pltpu.SemaphoreType.DMA((7,)),
            pltpu.SemaphoreType.DMA((7,)),
            pltpu.SemaphoreType.DMA((3,)),
            pltpu.SemaphoreType.DMA((3,)),
            pltpu.SemaphoreType.DMA((16,)),
            pltpu.SemaphoreType.DMA((16,)),
        ],
        compiler_params=pltpu.CompilerParams(
            collective_id=0, has_side_effects=True, vmem_limit_bytes=63 * 1024 * 1024
        ),
    )(
        tokens.transpose(1, 2, 0, 3), mixed_grad.transpose(1, 2, 0, 3), qkv_weight, out_weight,
        norm_gain.reshape(1, D), norm_bias.reshape(1, D),
    )
    return m_out.transpose(2, 0, 1, 3), d_out.transpose(2, 0, 1, 3)


def solution(mesh):
    placed = (
        P(None, "lat", "lon", None),
        P("lon", None),
        P("lon", None),
        P(),
        P(),
        P(None, "lat", "lon", None),
    )
    return jax.shard_map(
        functools.partial(per_device, mesh.shape["lat"], mesh.shape["lon"]),
        mesh=mesh,
        in_specs=placed,
        out_specs=(P(None, "lat", "lon", None), P(None, "lat", "lon", None)),
        check_vma=False,
    )
```

```python
import functools

import jax
import jax.numpy as jnp
from jax import lax
from jax.experimental import pallas as pl
from jax.experimental.pallas import tpu as pltpu
from jax.sharding import PartitionSpec as P

MESH = pl.DeviceIdType.MESH
BF = jnp.bfloat16
F32 = jnp.float32

D = 1024
HEADS = 8
HEAD_DIM = 64
LEV = 2
WIN = 12
INNER = 512
HALF = 6
TOK = LEV * WIN * WIN
QUARTER = TOK // 4
GROUP = 4
GW = GROUP * HEAD_DIM
WIDE = GROUP * TOK
ROWS = 32
EPS = 1e-05

HALVES = ((1, 1), (1, 0), (0, 1), (0, 0))


def nt(a, b):
    return lax.dot_general(a, b, (((1,), (1,)), ((), ())), preferred_element_type=F32)


def nn(a, b):
    return lax.dot_general(a, b, (((1,), (0,)), ((), ())), preferred_element_type=F32)


def tn(a, b):
    return lax.dot_general(a, b, (((0,), (0,)), ((), ())), preferred_element_type=F32)


def ds(start, size):
    return pl.ds(pl.multiple_of(start, size), size)


def kernel(
    n_lat, n_lon,
    t_ref, g_ref, wq_ref, wo_ref, gain_hbm, bias_hbm,
    m_out, d_out,
    comb_q, comb_o, wqf, wof, gain_ref, bias_ref, land_t, land_g, xw, gw, packed, heads, attn, agrad, hgrad, pgrad,
    scores, pt, dst, qblk, doblk, wide, mixed, tgrad,
    own_sem, zs, zr, ys, yr, xs, xr, ss, sr, hs, hr,
):
    lat, lon = lax.axis_index("lat"), lax.axis_index("lon")
    nz, ny = n_lon // 2, n_lat // 4
    rq, ro = D // n_lon, INNER // n_lon
    core, par, z = lax.rem(lat, 2), lax.rem(lon, 2), lon // 2
    half, y = lat // (2 * ny), lax.rem(lat // 2, ny)
    lat_lo, lat_hi = lax.rem(lat + n_lat - 1, n_lat), lax.rem(lat + 1, n_lat)
    lon_lo, lon_hi = lax.rem(lon + n_lon - 1, n_lon), lax.rem(lon + 1, n_lon)
    sib = (lat + 1 - 2 * core, lon)
    differ = lax.rem(par + core, 2)
    across = lon + 1 - 2 * par
    x_to = (lax.rem(lat + differ * (n_lat // 2), n_lat), across)
    x_from = (lax.rem(lat + (1 - differ) * (n_lat // 2), n_lat), across)
    west, north, diag = (lat, lon_lo), (lat_lo, lon), (lat_lo, lon_lo)
    east, south, far = (lat, lon_hi), (lat_hi, lon), (lat_hi, lon_hi)

    def offset(yy, e):
        far_pair = e // 2
        size = (1 - far_pair) * (yy + 1) + far_pair * (2 * ny - yy)
        return (1 - 2 * lax.rem(e, 2)) * size

    def z_to(e):
        return (lat, 2 * lax.rem(z + offset(y, e) + nz, nz) + par)

    def source(yy, e):
        return lax.rem(z - offset(yy, e) + nz, nz)

    def y_to(way):
        return ((half * ny + lax.rem(y + 1 - 2 * way + ny, ny)) * 2 + core, lon)

    def line(group, c):
        return lax.rem(y + ny + (0, 2 * c - 1, 1 - 2 * c, 2)[group], ny)

    comb, cut = (comb_q, comb_o), (3 * INNER // 2, D // 2)
    own = [
        ((wq_ref, wo_ref)[b].at[:, c * cut[b] : (c + 1) * cut[b]], comb[b].at[c, par, 0])
        for b in range(2) for c in range(2)
    ]
    own = [pltpu.make_async_copy(src, to, own_sem.at[8 + k]) for k, (src, to) in enumerate(own)]
    for copy in own:
        copy.start()

    barrier = pltpu.get_barrier_semaphore()
    met = [z_to(e) for e in range(4)]
    met += [y_to(0), y_to(1), sib, x_to, x_from, west, north, diag, east, south, far]
    for who in met:
        pl.semaphore_signal(barrier, inc=1, device_id=who, device_id_type=MESH)
    for copy in own:
        copy.wait()
    pl.semaphore_wait(barrier, len(met))

    def remote(src, dst, send, recv, who):
        return pltpu.make_async_remote_copy(
            src_ref=src, dst_ref=dst, send_sem=send, recv_sem=recv, device_id=who, device_id_type=MESH
        )

    def quarter(ref, k):
        i, j = HALVES[k]
        return ref.at[pl.ds(i * HALF, HALF), pl.ds(j * HALF, HALF)]

    def halo_in(field, src, land):
        copies = [
            remote(quarter(src, k), land.at[k], hs.at[field * 4 + k], hr.at[field * 4 + k], who)
            for k, who in ((1, west), (2, north), (3, diag))
        ]
        return copies, pltpu.make_async_copy(quarter(src, 0), land.at[0], own_sem.at[4 + field])

    in_t = halo_in(0, t_ref, land_t)
    in_g = halo_in(1, g_ref, land_g)
    def slots(wave, group, count=1):
        if wave < 2:
            return pl.ds(1 + wave * 8 + group * 2, count * 2)
        return pl.ds(1 + group * 4, count * 4)

    def z_copy(b, e):
        slot = 1 + e if b else 1 + e // 2 * 8 + e % 2
        i = b * 4 + e
        return remote(comb[b].at[core, par, 0], comb[b].at[core, par, slot], zs.at[i], zr.at[i], z_to(e))

    def y_copy(wave, k):
        src, dst = ((0, 1), (0, 2), (1, 3))[k]
        i, buf = wave * 3 + k, comb[wave // 2]
        return remote(
            buf.at[core, par, slots(wave, src)], buf.at[core, par, slots(wave, dst)], ys.at[i], yr.at[i],
            y_to(1 - core if k == 1 else core),
        )

    def x_copy(wave, k, p):
        ref = comb[wave // 2].at[core, p, slots(wave, (0, 1, 3)[k], (1, 2, 1)[k])]
        i = wave * 3 + k
        return remote(ref, ref, xs.at[i], xr.at[i], x_to)

    def x_own(b, p):
        ref = comb[b].at[core, p, 0]
        return remote(ref, ref, xs.at[9 + b], xr.at[9 + b], x_to)

    def s_copy(wave, c):
        ref = comb[wave // 2].at[c, :, slots(wave, 0, 4)]
        return remote(ref, ref, ss.at[wave], sr.at[wave], sib)

    def s_own(b, c):
        ref = comb[b].at[c, 1 - par, 0]
        return remote(ref, ref, ss.at[3 + b], sr.at[3 + b], sib)

    def place(wave):
        b = wave // 2
        full, size = ((wqf, rq), (wof, ro))[b]
        for c in range(2):
            found = [] if wave == 1 else [(0, z)]
            for j in range(4):
                for i in range(4 if b else 2):
                    e = i if b else 2 * wave + i
                    found.append((slots(wave, j).start + i, source(line(j, c), e)))
            for slot, zq in found:
                for p in range(2):
                    full[ds((zq * 2 + p) * size, size), c * cut[b] : (c + 1) * cut[b]] = comb[b][c, p, slot]

    local = [
        pltpu.make_async_copy(gain_hbm, gain_ref, own_sem.at[2]),
        pltpu.make_async_copy(bias_hbm, bias_ref, own_sem.at[3]),
        in_t[1],
        in_g[1],
    ]

    def rows_of(land, field):
        def step(t, carry):
            k, i = 2 * (t // 3), 2 * lax.rem(t, 3)
            two = [land[k + n, pl.ds(i, 2)].reshape(24, D) for n in (0, 1)]
            field[ds(t * 48, 48), :] = jnp.concatenate(two, axis=0)
            return carry

        lax.fori_loop(0, 6, step, 0)

    z_copies = [[z_copy(b, e) for e in range(4)] for b in range(2)]
    for copy in z_copies[0][:2]:
        copy.start()
    x_own(0, par).start()
    for copy in local:
        copy.start()

    def from_z(wave):
        b = wave // 2
        for copy in z_copies[1] if b else z_copies[0][2 * wave : 2 * wave + 2]:
            copy.wait_recv()
        if wave == 0:
            for copy in z_copies[0][2:]:
                copy.start()
        y_copy(wave, 0).start()
        y_copy(wave, 1).start()
        x_copy(wave, 0, par).start()
        if wave == 0:
            for copy in in_t[0]:
                copy.start()
        if wave == 1:
            for copy in z_copies[1]:
                copy.start()
            x_own(1, par).start()

    def from_y(wave):
        y_copy(wave, 0).wait_recv()
        y_copy(wave, 2).start()
        y_copy(wave, 1).wait_recv()
        x_copy(wave, 1, par).start()

    def from_y2(wave):
        y_copy(wave, 2).wait_recv()
        x_copy(wave, 2, par).start()

    def from_x(wave):
        if wave != 1:
            x_own(wave // 2, 1 - par).wait_recv()
            s_own(wave // 2, core).start()
        for k in range(3):
            x_copy(wave, k, 1 - par).wait_recv()
        s_copy(wave, core).start()

    def from_s(wave):
        if wave != 1:
            s_own(wave // 2, 1 - core).wait_recv()
        s_copy(wave, 1 - core).wait_recv()
        place(wave)

    from_z(0)
    from_y(0)
    from_y2(0)
    from_z(1)
    from_x(0)
    from_y(1)
    from_y2(1)
    for copy in in_t[0]:
        copy.wait_recv()
    for copy in local:
        copy.wait()
    rows_of(land_t, xw)
    from_s(0)
    from_x(1)
    from_z(2)
    for copy in in_g[0]:
        copy.start()
    from_s(1)
    from_y(2)

    for n in range(3 * INNER // 256):
        cols = slice(n * 256, n * 256 + 256)
        packed[:, cols] = nn(xw[...], wqf[:, cols]).astype(BF)
    from_y2(2)

    lane_head = lax.broadcasted_iota(jnp.int32, (TOK, GW), 1) // HEAD_DIM
    banned = jnp.where(lat == n_lat - 1, -1e30, 0.0).astype(F32)

    def spread(rows):
        return [rows * (lane_head[0:1] == h).astype(F32).astype(BF) for h in range(GROUP)]

    def columns(g):
        return [ds(n * INNER + g * GW, GW) for n in range(3)]

    def turned(block):
        return block.astype(F32).T.astype(BF)

    def narrow(right, left):
        for c in range(0, WIDE, 384):
            wide[:, c : c + 384] = nn(right, left(slice(c, c + 384)))
        blocks = [wide[h * HEAD_DIM : (h + 1) * HEAD_DIM, h * TOK : (h + 1) * TOK] for h in range(GROUP)]
        return jnp.concatenate(blocks, axis=0).T.astype(BF)

    def forward(g, carry):
        q_at, k_at, v_at = columns(g)
        for h, rows in enumerate(spread(packed[:, q_at])):
            qblk[g, h * TOK : (h + 1) * TOK, :] = rows

        for c in range(0, WIDE, 384):
            scores[:, c : c + 384] = nt(packed[:, k_at], qblk[g, c : c + 384, :])
        for c in range(0, WIDE, 128):
            cols = slice(c, c + 128)
            query = lax.rem(c + lax.broadcasted_iota(jnp.int32, (1, 128), 1), TOK)
            side = (query >= TOK // 2).astype(F32)
            s = jnp.concatenate(
                [scores[: TOK // 2, cols] + side * banned, scores[TOK // 2 :, cols] + (1.0 - side) * banned], axis=0
            )
            top = jnp.max(s, axis=0, keepdims=True)
            e = jnp.exp((s - top) * (HEAD_DIM ** -0.5))
            pt[g, :, cols] = (e * (1.0 / jnp.sum(e, axis=0, keepdims=True))).astype(BF)
        heads[:, q_at] = narrow(turned(packed[:, v_at]), lambda cols: pt[g, :, cols])

        @pl.when(g == 0)
        def _():
            from_x(2)

        return carry

    lax.fori_loop(0, HEADS // GROUP, forward, 0)
    from_s(2)

    for n in range(0, D, 256):
        attn[:, n : n + 256] = nn(heads[...], wof[:, n : n + 256]).astype(BF)

    for copy in in_g[0]:
        copy.wait_recv()
    rows_of(land_g, gw)

    def norm(c, carry):
        rows = ds(c * ROWS, ROWS)
        a = attn[rows, :].astype(F32)
        gain = gain_ref[...]
        scaled = gw[rows, :].astype(F32) * gain
        centered = a - jnp.mean(a, axis=-1, keepdims=True)
        level = scaled - jnp.mean(scaled, axis=-1, keepdims=True)
        inverse = lax.rsqrt(jnp.mean(centered * centered, axis=-1, keepdims=True) + EPS)
        along = jnp.mean(scaled * centered, axis=-1, keepdims=True) * inverse
        normed = centered * inverse
        mixed[rows, :] = (xw[rows, :].astype(F32) + normed * gain + bias_ref[...]).astype(BF)
        agrad[rows, :] = ((level - normed * along) * inverse).astype(BF)
        return carry

    lax.fori_loop(0, TOK // ROWS, norm, 0, unroll=3)

    def halo_out(field, rows, land, out):
        def step(t, carry):
            k, i = 2 * (t // 3), 2 * lax.rem(t, 3)
            block = rows[ds(t * 48, 48), :]
            for n in (0, 1):
                land[k + n, pl.ds(i, 2)] = block[n * 24 : (n + 1) * 24].reshape(2, HALF, LEV, D)
            return carry

        lax.fori_loop(0, 6, step, 0)
        copies = [
            remote(land.at[k], quarter(out, k), hs.at[(field + 2) * 4 + k], hr.at[(field + 2) * 4 + k], who)
            for k, who in ((1, east), (2, south), (3, far))
        ]
        keep = pltpu.make_async_copy(land.at[0], quarter(out, 0), own_sem.at[6 + field])
        for copy in copies:
            copy.start()
        keep.start()
        return copies, keep

    out_m = halo_out(0, mixed, land_t, m_out)

    for n in range(0, INNER, 256):
        hgrad[:, n : n + 256] = nt(agrad[...], wof[n : n + 256, :]).astype(BF)

    def backward(g, carry):
        q_at, k_at, v_at = columns(g)
        for h, rows in enumerate(spread(hgrad[:, q_at])):
            doblk[h * TOK : (h + 1) * TOK, :] = rows

        for c in range(0, WIDE, 384):
            scores[:, c : c + 384] = nt(packed[:, v_at], doblk[c : c + 384, :])
        for c in range(0, WIDE, 128):
            cols = slice(c, c + 128)
            p, dp = pt[g, :, cols].astype(F32), scores[:, cols]
            total = jnp.sum(p * dp, axis=0, keepdims=True)
            dst[:, cols] = (p * (dp - total) * (HEAD_DIM ** -0.5)).astype(BF)
        pgrad[:, q_at] = narrow(turned(packed[:, k_at]), lambda cols: dst[:, cols])
        pgrad[:, v_at] = nn(pt[g], doblk[...]).astype(BF)
        pgrad[:, k_at] = nn(dst[...], qblk[g]).astype(BF)
        return carry

    lax.fori_loop(0, HEADS // GROUP, backward, 0)

    for n in range(0, D, 256):
        cols = slice(n, n + 256)
        sg = nt(pgrad[...], wqf[cols, :]).astype(BF).astype(F32)
        tgrad[:, cols] = (gw[:, cols].astype(F32) + sg).astype(BF)
    out_d = halo_out(1, tgrad, land_g, d_out)

    for copy in z_copies[0] + z_copies[1]:
        copy.wait_send()
    for wave in range(3):
        for k in range(3):
            y_copy(wave, k).wait_send()
            x_copy(wave, k, par).wait_send()
        s_copy(wave, core).wait_send()
    for b in range(2):
        x_own(b, par).wait_send()
        s_own(b, core).wait_send()
    for copy in in_t[0] + in_g[0]:
        copy.wait_send()
    for copies, keep in (out_m, out_d):
        keep.wait()
        for copy in copies:
            copy.wait()


def write_out(m_ref, d_ref, m_out, d_out, sem):
    copies = [pltpu.make_async_copy(m_ref, m_out, sem.at[0]), pltpu.make_async_copy(d_ref, d_out, sem.at[1])]
    for copy in copies:
        copy.start()
    for copy in copies:
        copy.wait()


def per_device(n_lat, n_lon, tokens, qkv_weight, out_weight, norm_gain, norm_bias, mixed_grad):
    hbm = pl.BlockSpec(memory_space=pltpu.HBM)
    cells = (WIN, WIN, LEV, D)
    m_out, d_out = pl.pallas_call(
        functools.partial(kernel, n_lat, n_lon),
        out_shape=[jax.ShapeDtypeStruct(cells, BF)] * 2,
        in_specs=[hbm] * 6,
        out_specs=[pl.BlockSpec(memory_space=pl.ANY)] * 2,
        scratch_shapes=[
            pltpu.VMEM((2, 2, 17, D // n_lon, 3 * INNER // 2), BF),
            pltpu.VMEM((2, 2, 17, INNER // n_lon, D // 2), BF),
            pltpu.VMEM((D, 3 * INNER), BF),
            pltpu.VMEM((INNER, D), BF),
            pltpu.VMEM((1, D), F32),
            pltpu.VMEM((1, D), F32),
            pltpu.VMEM((4, HALF, HALF, LEV, D), BF),
            pltpu.VMEM((4, HALF, HALF, LEV, D), BF),
            pltpu.VMEM((TOK, D), BF),
            pltpu.VMEM((TOK, D), BF),
            pltpu.VMEM((TOK, 3 * INNER), BF),
            pltpu.VMEM((TOK, INNER), BF),
            pltpu.VMEM((TOK, D), BF),
            pltpu.VMEM((TOK, D), BF),
            pltpu.VMEM((TOK, INNER), BF),
            pltpu.VMEM((TOK, 3 * INNER), BF),
            pltpu.VMEM((TOK, WIDE), F32),
            pltpu.VMEM((2, TOK, WIDE), BF),
            pltpu.VMEM((TOK, WIDE), BF),
            pltpu.VMEM((2, WIDE, GW), BF),
            pltpu.VMEM((WIDE, GW), BF),
            pltpu.VMEM((GW, WIDE), F32),
            pltpu.VMEM((TOK, D), BF),
            pltpu.VMEM((TOK, D), BF),
            pltpu.SemaphoreType.DMA((12,)),
            pltpu.SemaphoreType.DMA((8,)),
            pltpu.SemaphoreType.DMA((8,)),
            pltpu.SemaphoreType.DMA((9,)),
            pltpu.SemaphoreType.DMA((9,)),
            pltpu.SemaphoreType.DMA((11,)),
            pltpu.SemaphoreType.DMA((11,)),
            pltpu.SemaphoreType.DMA((5,)),
            pltpu.SemaphoreType.DMA((5,)),
            pltpu.SemaphoreType.DMA((16,)),
            pltpu.SemaphoreType.DMA((16,)),
        ],
        compiler_params=pltpu.CompilerParams(
            collective_id=0, has_side_effects=True, vmem_limit_bytes=63 * 1024 * 1024
        ),
    )(
        tokens.transpose(1, 2, 0, 3), mixed_grad.transpose(1, 2, 0, 3), qkv_weight, out_weight,
        norm_gain.reshape(1, D), norm_bias.reshape(1, D),
    )
    m_out, d_out = pl.pallas_call(
        write_out,
        out_shape=[jax.ShapeDtypeStruct(cells, BF)] * 2,
        in_specs=[pl.BlockSpec(memory_space=pl.ANY)] * 2,
        out_specs=[pl.BlockSpec(memory_space=pl.ANY)] * 2,
        scratch_shapes=[pltpu.SemaphoreType.DMA((2,))],
        compiler_params=pltpu.CompilerParams(vmem_limit_bytes=63 * 1024 * 1024),
    )(m_out, d_out)
    return m_out.transpose(2, 0, 1, 3), d_out.transpose(2, 0, 1, 3)


def solution(mesh):
    placed = (
        P(None, "lat", "lon", None),
        P("lon", None),
        P("lon", None),
        P(),
        P(),
        P(None, "lat", "lon", None),
    )
    return jax.shard_map(
        functools.partial(per_device, mesh.shape["lat"], mesh.shape["lon"]),
        mesh=mesh,
        in_specs=placed,
        out_specs=(P(None, "lat", "lon", None), P(None, "lat", "lon", None)),
        check_vma=False,
    )
```

```python
import functools

import jax
import jax.numpy as jnp
from jax import lax
from jax.experimental import pallas as pl
from jax.experimental.pallas import tpu as pltpu
from jax.sharding import PartitionSpec as P

MESH = pl.DeviceIdType.MESH
BF = jnp.bfloat16
F32 = jnp.float32

D = 1024
HEADS = 8
HEAD_DIM = 64
LEV = 2
WIN = 12
INNER = 512
HALF = 6
TOK = LEV * WIN * WIN
QUARTER = TOK // 4
GROUP = 4
GW = GROUP * HEAD_DIM
WIDE = GROUP * TOK
ROWS = 32
EPS = 1e-05

PIECE = 80
HALVES = ((1, 1), (1, 0), (0, 1), (0, 0))
SENT, INSIDE = (64, 144, 208), (0, 8, 0, 8)


def nt(a, b):
    return lax.dot_general(a, b, (((1,), (1,)), ((), ())), preferred_element_type=F32)


def nn(a, b):
    return lax.dot_general(a, b, (((1,), (0,)), ((), ())), preferred_element_type=F32)


def tn(a, b):
    return lax.dot_general(a, b, (((0,), (0,)), ((), ())), preferred_element_type=F32)


def ds(start, size):
    return pl.ds(pl.multiple_of(start, size), size)


def kernel(
    n_lat, n_lon,
    t_ref, g_ref, wq_ref, wo_ref, gain_hbm, bias_hbm,
    m_out, d_out,
    comb_q, comb_o, wqf, wof, gain_ref, bias_ref, land_t, land_g, own_t, own_g, xw, gw, packed, heads, attn, agrad, hgrad, pgrad,
    scores, pt, dst, qblk, doblk, wide, mixed, tgrad,
    own_sem, zs, zr, ys, yr, xs, xr, ss, sr, hs, hr,
):
    lat, lon = lax.axis_index("lat"), lax.axis_index("lon")
    nz, ny = n_lon // 2, n_lat // 4
    rq, ro = D // n_lon, INNER // n_lon
    core, par, z = lax.rem(lat, 2), lax.rem(lon, 2), lon // 2
    half, y = lat // (2 * ny), lax.rem(lat // 2, ny)
    lat_lo, lat_hi = lax.rem(lat + n_lat - 1, n_lat), lax.rem(lat + 1, n_lat)
    lon_lo, lon_hi = lax.rem(lon + n_lon - 1, n_lon), lax.rem(lon + 1, n_lon)
    sib = (lat + 1 - 2 * core, lon)
    differ = lax.rem(par + core, 2)
    across = lon + 1 - 2 * par
    x_to = (lax.rem(lat + differ * (n_lat // 2), n_lat), across)
    x_from = (lax.rem(lat + (1 - differ) * (n_lat // 2), n_lat), across)
    west, north, diag = (lat, lon_lo), (lat_lo, lon), (lat_lo, lon_lo)
    east, south, far = (lat, lon_hi), (lat_hi, lon), (lat_hi, lon_hi)

    def offset(yy, e):
        far_pair = e // 2
        size = (1 - far_pair) * (yy + 1) + far_pair * (2 * ny - yy)
        return (1 - 2 * lax.rem(e, 2)) * size

    def z_to(e):
        return (lat, 2 * lax.rem(z + offset(y, e) + nz, nz) + par)

    def source(yy, e):
        return lax.rem(z - offset(yy, e) + nz, nz)

    def y_to(way):
        return ((half * ny + lax.rem(y + 1 - 2 * way + ny, ny)) * 2 + core, lon)

    def line(group, c):
        return lax.rem(y + ny + (0, 2 * c - 1, 1 - 2 * c, 2)[group], ny)

    comb, cut = (comb_q, comb_o), (3 * INNER // 2, D // 2)
    own = [
        ((wq_ref, wo_ref)[b].at[:, c * cut[b] : (c + 1) * cut[b]], comb[b].at[c, par, 0])
        for b in range(2) for c in range(2)
    ]
    own = [pltpu.make_async_copy(src, to, own_sem.at[8 + k]) for k, (src, to) in enumerate(own)]
    for copy in own:
        copy.start()

    barrier = pltpu.get_barrier_semaphore()
    met = [z_to(e) for e in range(4)]
    met += [y_to(0), y_to(1), sib, x_to, x_from, west, north, diag, east, south, far]
    for who in met:
        pl.semaphore_signal(barrier, inc=1, device_id=who, device_id_type=MESH)
    for copy in own:
        copy.wait()
    pl.semaphore_wait(barrier, len(met))

    def remote(src, dst, send, recv, who):
        return pltpu.make_async_remote_copy(
            src_ref=src, dst_ref=dst, send_sem=send, recv_sem=recv, device_id=who, device_id_type=MESH
        )

    def rows_of(cells, rows):
        for k, (i, j) in enumerate(HALVES):
            block = cells[i * HALF : (i + 1) * HALF, j * HALF : (j + 1) * HALF]
            rows[k * QUARTER : (k + 1) * QUARTER, :] = block.reshape(QUARTER, D)

    def halo_in(field, rows, land):
        return [
            remote(rows.at[pl.ds(SENT[k], PIECE)], land.at[k], hs.at[field * 3 + k], hr.at[field * 3 + k], who)
            for k, who in enumerate((west, north, diag))
        ]

    def assemble(rows, land, field):
        row = lax.broadcasted_iota(jnp.int32, (16, D), 0)

        def seam(above, below):
            return jnp.where(row < 8, above.astype(F32), below.astype(F32)).astype(BF)

        field[0:64, :] = rows[0:64, :]
        field[64:80, :] = seam(rows[64:80, :], land[0, 0:16, :])
        field[80:144, :] = land[0, 16:80, :]
        field[144:208, :] = land[1, 0:64, :]
        field[208:224, :] = seam(land[1, 64:80, :], land[2, 0:16, :])
        field[224:288, :] = land[2, 16:80, :]

    in_t = halo_in(0, own_t, land_t)
    in_g = halo_in(1, own_g, land_g)
    def slots(wave, group, count=1):
        if wave < 2:
            return pl.ds(1 + wave * 8 + group * 2, count * 2)
        return pl.ds(1 + group * 4, count * 4)

    def z_copy(b, e):
        slot = 1 + e if b else 1 + e // 2 * 8 + e % 2
        i = b * 4 + e
        return remote(comb[b].at[core, par, 0], comb[b].at[core, par, slot], zs.at[i], zr.at[i], z_to(e))

    def y_copy(wave, k):
        src, dst = ((0, 1), (0, 2), (1, 3))[k]
        i, buf = wave * 3 + k, comb[wave // 2]
        return remote(
            buf.at[core, par, slots(wave, src)], buf.at[core, par, slots(wave, dst)], ys.at[i], yr.at[i],
            y_to(1 - core if k == 1 else core),
        )

    def x_copy(wave, k, p):
        ref = comb[wave // 2].at[core, p, slots(wave, (0, 1, 3)[k], (1, 2, 1)[k])]
        i = wave * 3 + k
        return remote(ref, ref, xs.at[i], xr.at[i], x_to)

    def x_own(b, p):
        ref = comb[b].at[core, p, 0]
        return remote(ref, ref, xs.at[9 + b], xr.at[9 + b], x_to)

    def s_copy(wave, c):
        ref = comb[wave // 2].at[c, :, slots(wave, 0, 4)]
        return remote(ref, ref, ss.at[wave], sr.at[wave], sib)

    def s_own(b, c):
        ref = comb[b].at[c, 1 - par, 0]
        return remote(ref, ref, ss.at[3 + b], sr.at[3 + b], sib)

    def place(wave):
        b = wave // 2
        full, size = ((wqf, rq), (wof, ro))[b]
        for c in range(2):
            found = [] if wave == 1 else [(0, z)]
            for j in range(4):
                for i in range(4 if b else 2):
                    e = i if b else 2 * wave + i
                    found.append((slots(wave, j).start + i, source(line(j, c), e)))
            for slot, zq in found:
                for p in range(2):
                    full[ds((zq * 2 + p) * size, size), c * cut[b] : (c + 1) * cut[b]] = comb[b][c, p, slot]

    local = [
        pltpu.make_async_copy(gain_hbm, gain_ref, own_sem.at[2]),
        pltpu.make_async_copy(bias_hbm, bias_ref, own_sem.at[3]),
    ]

    z_copies = [[z_copy(b, e) for e in range(4)] for b in range(2)]
    for copy in z_copies[0][:2]:
        copy.start()
    x_own(0, par).start()
    for copy in local:
        copy.start()
    rows_of(t_ref, own_t)

    def from_z(wave):
        b = wave // 2
        for copy in z_copies[1] if b else z_copies[0][2 * wave : 2 * wave + 2]:
            copy.wait_recv()
        if wave == 0:
            for copy in z_copies[0][2:]:
                copy.start()
        y_copy(wave, 0).start()
        y_copy(wave, 1).start()
        x_copy(wave, 0, par).start()
        if wave == 0:
            for copy in in_t:
                copy.start()
        if wave == 1:
            for copy in z_copies[1]:
                copy.start()
            x_own(1, par).start()

    def from_y(wave):
        y_copy(wave, 0).wait_recv()
        y_copy(wave, 2).start()
        y_copy(wave, 1).wait_recv()
        x_copy(wave, 1, par).start()

    def from_y2(wave):
        y_copy(wave, 2).wait_recv()
        x_copy(wave, 2, par).start()

    def from_x(wave):
        if wave != 1:
            x_own(wave // 2, 1 - par).wait_recv()
            s_own(wave // 2, core).start()
        for k in range(3):
            x_copy(wave, k, 1 - par).wait_recv()
        s_copy(wave, core).start()

    def from_s(wave):
        if wave != 1:
            s_own(wave // 2, 1 - core).wait_recv()
        s_copy(wave, 1 - core).wait_recv()
        place(wave)

    from_z(0)
    from_y(0)
    from_y2(0)
    rows_of(g_ref, own_g)
    from_z(1)
    from_x(0)
    from_y(1)
    from_y2(1)
    for copy in in_t:
        copy.wait_recv()
    for copy in local:
        copy.wait()
    assemble(own_t, land_t, xw)
    from_s(0)
    from_x(1)
    from_z(2)
    for copy in in_g:
        copy.start()
    from_s(1)
    from_y(2)

    for n in range(3 * INNER // 256):
        cols = slice(n * 256, n * 256 + 256)
        packed[:, cols] = nn(xw[...], wqf[:, cols]).astype(BF)
    from_y2(2)

    lane_head = lax.broadcasted_iota(jnp.int32, (TOK, GW), 1) // HEAD_DIM
    banned = jnp.where(lat == n_lat - 1, -1e30, 0.0).astype(F32)

    def spread(rows):
        return [rows * (lane_head[0:1] == h).astype(F32).astype(BF) for h in range(GROUP)]

    def columns(g):
        return [ds(n * INNER + g * GW, GW) for n in range(3)]

    def turned(block):
        return block.astype(F32).T.astype(BF)

    def narrow(right, left):
        for c in range(0, WIDE, 384):
            wide[:, c : c + 384] = nn(right, left(slice(c, c + 384)))
        blocks = [wide[h * HEAD_DIM : (h + 1) * HEAD_DIM, h * TOK : (h + 1) * TOK] for h in range(GROUP)]
        return jnp.concatenate(blocks, axis=0).T.astype(BF)

    def forward(g, carry):
        q_at, k_at, v_at = columns(g)
        for h, rows in enumerate(spread(packed[:, q_at])):
            qblk[g, h * TOK : (h + 1) * TOK, :] = rows

        for c in range(0, WIDE, 384):
            scores[:, c : c + 384] = nt(packed[:, k_at], qblk[g, c : c + 384, :])
        for c in range(0, WIDE, 128):
            cols = slice(c, c + 128)
            query = lax.rem(c + lax.broadcasted_iota(jnp.int32, (1, 128), 1), TOK)
            side = (query >= TOK // 2).astype(F32)
            s = jnp.concatenate(
                [scores[: TOK // 2, cols] + side * banned, scores[TOK // 2 :, cols] + (1.0 - side) * banned], axis=0
            )
            top = jnp.max(s, axis=0, keepdims=True)
            e = jnp.exp((s - top) * (HEAD_DIM ** -0.5))
            pt[g, :, cols] = (e * (1.0 / jnp.sum(e, axis=0, keepdims=True))).astype(BF)
        heads[:, q_at] = narrow(turned(packed[:, v_at]), lambda cols: pt[g, :, cols])

        @pl.when(g == 0)
        def _():
            from_x(2)

        return carry

    lax.fori_loop(0, HEADS // GROUP, forward, 0)
    from_s(2)

    for n in range(0, D, 256):
        attn[:, n : n + 256] = nn(heads[...], wof[:, n : n + 256]).astype(BF)

    for copy in in_g:
        copy.wait_recv()
    assemble(own_g, land_g, gw)

    def norm(c, carry):
        rows = ds(c * ROWS, ROWS)
        a = attn[rows, :].astype(F32)
        gain = gain_ref[...]
        scaled = gw[rows, :].astype(F32) * gain
        centered = a - jnp.mean(a, axis=-1, keepdims=True)
        level = scaled - jnp.mean(scaled, axis=-1, keepdims=True)
        inverse = lax.rsqrt(jnp.mean(centered * centered, axis=-1, keepdims=True) + EPS)
        along = jnp.mean(scaled * centered, axis=-1, keepdims=True) * inverse
        normed = centered * inverse
        mixed[rows, :] = (xw[rows, :].astype(F32) + normed * gain + bias_ref[...]).astype(BF)
        agrad[rows, :] = ((level - normed * along) * inverse).astype(BF)
        return carry

    lax.fori_loop(0, TOK // ROWS, norm, 0, unroll=3)

    def halo_out(field, rows, out):
        copies = [
            remote(
                rows.at[pl.ds(SENT[k], PIECE)], out.at[k + 1],
                hs.at[(field + 2) * 3 + k], hr.at[(field + 2) * 3 + k], who,
            )
            for k, who in enumerate((east, south, far))
        ]
        keep = pltpu.make_async_copy(rows.at[pl.ds(0, PIECE)], out.at[0], own_sem.at[6 + field])
        for copy in copies:
            copy.start()
        keep.start()
        return copies, keep

    out_m = halo_out(0, mixed, m_out)

    for n in range(0, INNER, 256):
        hgrad[:, n : n + 256] = nt(agrad[...], wof[n : n + 256, :]).astype(BF)

    def backward(g, carry):
        q_at, k_at, v_at = columns(g)
        for h, rows in enumerate(spread(hgrad[:, q_at])):
            doblk[h * TOK : (h + 1) * TOK, :] = rows

        for c in range(0, WIDE, 384):
            scores[:, c : c + 384] = nt(packed[:, v_at], doblk[c : c + 384, :])
        for c in range(0, WIDE, 128):
            cols = slice(c, c + 128)
            p, dp = pt[g, :, cols].astype(F32), scores[:, cols]
            total = jnp.sum(p * dp, axis=0, keepdims=True)
            dst[:, cols] = (p * (dp - total) * (HEAD_DIM ** -0.5)).astype(BF)
        pgrad[:, q_at] = narrow(turned(packed[:, k_at]), lambda cols: dst[:, cols])
        pgrad[:, v_at] = nn(pt[g], doblk[...]).astype(BF)
        pgrad[:, k_at] = nn(dst[...], qblk[g]).astype(BF)
        return carry

    lax.fori_loop(0, HEADS // GROUP, backward, 0)

    for n in range(0, D, 256):
        cols = slice(n, n + 256)
        sg = nt(pgrad[...], wqf[cols, :]).astype(BF).astype(F32)
        tgrad[:, cols] = (gw[:, cols].astype(F32) + sg).astype(BF)
    out_d = halo_out(1, tgrad, d_out)

    for copy in z_copies[0] + z_copies[1]:
        copy.wait_send()
    for wave in range(3):
        for k in range(3):
            y_copy(wave, k).wait_send()
            x_copy(wave, k, par).wait_send()
        s_copy(wave, core).wait_send()
    for b in range(2):
        x_own(b, par).wait_send()
        s_own(b, core).wait_send()
    for copy in in_t + in_g:
        copy.wait_send()
    for copies, keep in (out_m, out_d):
        keep.wait()
        for copy in copies:
            copy.wait()


def per_device(n_lat, n_lon, tokens, qkv_weight, out_weight, norm_gain, norm_bias, mixed_grad):
    hbm = pl.BlockSpec(memory_space=pltpu.HBM)
    vmem = pl.BlockSpec(memory_space=pltpu.VMEM)

    def join(pieces):
        own, left, above, corner = (
            pieces[k, INSIDE[k] : INSIDE[k] + QUARTER].reshape(HALF, HALF, LEV, D) for k in range(4)
        )
        cells = jnp.concatenate(
            [jnp.concatenate([corner, above], axis=1), jnp.concatenate([left, own], axis=1)], axis=0
        )
        return cells.transpose(2, 0, 1, 3)

    m_out, d_out = pl.pallas_call(
        functools.partial(kernel, n_lat, n_lon),
        out_shape=[jax.ShapeDtypeStruct((4, PIECE, D), BF)] * 2,
        in_specs=[vmem, vmem, hbm, hbm, hbm, hbm],
        out_specs=[pl.BlockSpec(memory_space=pl.ANY)] * 2,
        scratch_shapes=[
            pltpu.VMEM((2, 2, 17, D // n_lon, 3 * INNER // 2), BF),
            pltpu.VMEM((2, 2, 17, INNER // n_lon, D // 2), BF),
            pltpu.VMEM((D, 3 * INNER), BF),
            pltpu.VMEM((INNER, D), BF),
            pltpu.VMEM((1, D), F32),
            pltpu.VMEM((1, D), F32),
            pltpu.VMEM((3, PIECE, D), BF),
            pltpu.VMEM((3, PIECE, D), BF),
            pltpu.VMEM((TOK, D), BF),
            pltpu.VMEM((TOK, D), BF),
            pltpu.VMEM((TOK, D), BF),
            pltpu.VMEM((TOK, D), BF),
            pltpu.VMEM((TOK, 3 * INNER), BF),
            pltpu.VMEM((TOK, INNER), BF),
            pltpu.VMEM((TOK, D), BF),
            pltpu.VMEM((TOK, D), BF),
            pltpu.VMEM((TOK, INNER), BF),
            pltpu.VMEM((TOK, 3 * INNER), BF),
            pltpu.VMEM((TOK, WIDE), F32),
            pltpu.VMEM((2, TOK, WIDE), BF),
            pltpu.VMEM((TOK, WIDE), BF),
            pltpu.VMEM((2, WIDE, GW), BF),
            pltpu.VMEM((WIDE, GW), BF),
            pltpu.VMEM((GW, WIDE), F32),
            pltpu.VMEM((TOK, D), BF),
            pltpu.VMEM((TOK, D), BF),
            pltpu.SemaphoreType.DMA((12,)),
            pltpu.SemaphoreType.DMA((8,)),
            pltpu.SemaphoreType.DMA((8,)),
            pltpu.SemaphoreType.DMA((9,)),
            pltpu.SemaphoreType.DMA((9,)),
            pltpu.SemaphoreType.DMA((11,)),
            pltpu.SemaphoreType.DMA((11,)),
            pltpu.SemaphoreType.DMA((5,)),
            pltpu.SemaphoreType.DMA((5,)),
            pltpu.SemaphoreType.DMA((16,)),
            pltpu.SemaphoreType.DMA((16,)),
        ],
        compiler_params=pltpu.CompilerParams(
            collective_id=0, has_side_effects=True, vmem_limit_bytes=40 * 1024 * 1024
        ),
    )(
        tokens.transpose(1, 2, 0, 3), mixed_grad.transpose(1, 2, 0, 3), qkv_weight, out_weight,
        norm_gain.reshape(1, D), norm_bias.reshape(1, D),
    )
    return join(m_out), join(d_out)


def solution(mesh):
    placed = (
        P(None, "lat", "lon", None),
        P("lon", None),
        P("lon", None),
        P(),
        P(),
        P(None, "lat", "lon", None),
    )
    return jax.shard_map(
        functools.partial(per_device, mesh.shape["lat"], mesh.shape["lon"]),
        mesh=mesh,
        in_specs=placed,
        out_specs=(P(None, "lat", "lon", None), P(None, "lat", "lon", None)),
        check_vma=False,
    )
```

```python
import functools

import jax
import jax.numpy as jnp
from jax import lax
from jax.experimental import pallas as pl
from jax.experimental.pallas import tpu as pltpu
from jax.sharding import PartitionSpec as P

MESH = pl.DeviceIdType.MESH
BF = jnp.bfloat16
F32 = jnp.float32

D = 1024
HEADS = 8
HEAD_DIM = 64
LEV = 2
WIN = 12
INNER = 512
HALF = 6
TOK = LEV * WIN * WIN
QUARTER = TOK // 4
GROUP = 4
GW = GROUP * HEAD_DIM
WIDE = GROUP * TOK
PARTS = (slice(0, 512), slice(512, WIDE))
ROWS = 32
EPS = 1e-05

HALVES = ((1, 1), (1, 0), (0, 1), (0, 0))


def nt(a, b):
    return lax.dot_general(a, b, (((1,), (1,)), ((), ())), preferred_element_type=F32)


def nn(a, b):
    return lax.dot_general(a, b, (((1,), (0,)), ((), ())), preferred_element_type=F32)


def tn(a, b):
    return lax.dot_general(a, b, (((0,), (0,)), ((), ())), preferred_element_type=F32)


def ds(start, size):
    return pl.ds(pl.multiple_of(start, size), size)


def kernel(
    n_lat, n_lon,
    t_ref, g_ref, wq_ref, wo_ref, gain_hbm, bias_hbm,
    m_out, d_out,
    comb_q, comb_o, wqf, wof, gain_ref, bias_ref, land_t, land_g, xw, gw, packed, heads, attn, agrad, hgrad, pgrad,
    scores, pt, dst, qblk, doblk, wide, mixed, tgrad,
    own_sem, zs, zr, ys, yr, xs, xr, ss, sr, hs, hr,
):
    lat, lon = lax.axis_index("lat"), lax.axis_index("lon")
    nz, ny = n_lon // 2, n_lat // 4
    rq, ro = D // n_lon, INNER // n_lon
    core, par, z = lax.rem(lat, 2), lax.rem(lon, 2), lon // 2
    half, y = lat // (2 * ny), lax.rem(lat // 2, ny)
    lat_lo, lat_hi = lax.rem(lat + n_lat - 1, n_lat), lax.rem(lat + 1, n_lat)
    lon_lo, lon_hi = lax.rem(lon + n_lon - 1, n_lon), lax.rem(lon + 1, n_lon)
    sib = (lat + 1 - 2 * core, lon)
    differ = lax.rem(par + core, 2)
    across = lon + 1 - 2 * par
    x_to = (lax.rem(lat + differ * (n_lat // 2), n_lat), across)
    x_from = (lax.rem(lat + (1 - differ) * (n_lat // 2), n_lat), across)
    west, north, diag = (lat, lon_lo), (lat_lo, lon), (lat_lo, lon_lo)
    east, south, far = (lat, lon_hi), (lat_hi, lon), (lat_hi, lon_hi)

    def offset(yy, e):
        far_pair = e // 2
        size = (1 - far_pair) * (yy + 1) + far_pair * (2 * ny - yy)
        return (1 - 2 * lax.rem(e, 2)) * size

    def z_to(e):
        return (lat, 2 * lax.rem(z + offset(y, e) + nz, nz) + par)

    def source(yy, e):
        return lax.rem(z - offset(yy, e) + nz, nz)

    def y_to(way):
        return ((half * ny + lax.rem(y + 1 - 2 * way + ny, ny)) * 2 + core, lon)

    def line(group, c):
        return lax.rem(y + ny + (0, 2 * c - 1, 1 - 2 * c, 2)[group], ny)

    comb, cut = (comb_q, comb_o), (3 * INNER // 2, D // 2)
    own = [
        ((wq_ref, wo_ref)[b].at[:, c * cut[b] : (c + 1) * cut[b]], comb[b].at[c, par, 0])
        for b in range(2) for c in range(2)
    ]
    own = [pltpu.make_async_copy(src, to, own_sem.at[8 + k]) for k, (src, to) in enumerate(own)]
    for copy in own:
        copy.start()

    barrier = pltpu.get_barrier_semaphore()
    met = [z_to(e) for e in range(4)]
    met += [y_to(0), y_to(1), sib, x_to, x_from, west, north, diag, east, south, far]
    for who in met:
        pl.semaphore_signal(barrier, inc=1, device_id=who, device_id_type=MESH)
    for copy in own:
        copy.wait()
    pl.semaphore_wait(barrier, len(met))

    def remote(src, dst, send, recv, who):
        return pltpu.make_async_remote_copy(
            src_ref=src, dst_ref=dst, send_sem=send, recv_sem=recv, device_id=who, device_id_type=MESH
        )

    def quarter(ref, k):
        i, j = HALVES[k]
        return ref.at[pl.ds(i * HALF, HALF), pl.ds(j * HALF, HALF)]

    def halo_in(field, src, land):
        copies = [
            remote(quarter(src, k), land.at[k], hs.at[field * 4 + k], hr.at[field * 4 + k], who)
            for k, who in ((1, west), (2, north), (3, diag))
        ]
        return copies, pltpu.make_async_copy(quarter(src, 0), land.at[0], own_sem.at[4 + field])

    in_t = halo_in(0, t_ref, land_t)
    in_g = halo_in(1, g_ref, land_g)
    def slots(wave, group, count=1):
        if wave < 2:
            return pl.ds(1 + wave * 8 + group * 2, count * 2)
        return pl.ds(1 + group * 4, count * 4)

    def z_copy(b, e):
        slot = 1 + e if b else 1 + e // 2 * 8 + e % 2
        i = b * 4 + e
        return remote(comb[b].at[core, par, 0], comb[b].at[core, par, slot], zs.at[i], zr.at[i], z_to(e))

    def y_copy(wave, k):
        src, dst = ((0, 1), (0, 2), (1, 3))[k]
        i, buf = wave * 3 + k, comb[wave // 2]
        return remote(
            buf.at[core, par, slots(wave, src)], buf.at[core, par, slots(wave, dst)], ys.at[i], yr.at[i],
            y_to(1 - core if k == 1 else core),
        )

    def x_copy(wave, k, p):
        ref = comb[wave // 2].at[core, p, slots(wave, (0, 1, 3)[k], (1, 2, 1)[k])]
        i = wave * 3 + k
        return remote(ref, ref, xs.at[i], xr.at[i], x_to)

    def x_own(b, p):
        ref = comb[b].at[core, p, 0]
        return remote(ref, ref, xs.at[9 + b], xr.at[9 + b], x_to)

    def s_copy(wave, c):
        ref = comb[wave // 2].at[c, :, slots(wave, 0, 4)]
        return remote(ref, ref, ss.at[wave], sr.at[wave], sib)

    def s_own(b, c):
        ref = comb[b].at[c, 1 - par, 0]
        return remote(ref, ref, ss.at[3 + b], sr.at[3 + b], sib)

    def place(wave):
        b = wave // 2
        full, size = ((wqf, rq), (wof, ro))[b]
        each = 4 if b else 2

        def put(c, slot, zq):
            for p in range(2):
                full[ds((zq * 2 + p) * size, size), c * cut[b] : (c + 1) * cut[b]] = comb[b][c, p, slot]

        for c in range(2):
            def step(t, carry, c=c):
                j = t // each
                beside = (j == 1).astype(jnp.int32) - (j == 2).astype(jnp.int32)
                yy = lax.rem(y + ny + (2 * c - 1) * beside + 2 * (j // 3), ny)
                e = lax.rem(t, each) + (2 * wave if b == 0 else 0)
                put(c, slots(wave, 0).start + t, source(yy, e))
                return carry

            lax.fori_loop(0, 4 * each, step, 0)
            if wave != 1:
                put(c, 0, z)

    local = [
        pltpu.make_async_copy(gain_hbm, gain_ref, own_sem.at[2]),
        pltpu.make_async_copy(bias_hbm, bias_ref, own_sem.at[3]),
        in_t[1],
        in_g[1],
    ]

    def rows_of(land, field):
        def step(t, carry):
            k, i = 2 * (t // 3), 2 * lax.rem(t, 3)
            two = [land[k + n, pl.ds(i, 2)].reshape(24, D) for n in (0, 1)]
            field[ds(t * 48, 48), :] = jnp.concatenate(two, axis=0)
            return carry

        lax.fori_loop(0, 6, step, 0)

    z_copies = [[z_copy(b, e) for e in range(4)] for b in range(2)]
    for copy in z_copies[0][:2]:
        copy.start()
    x_own(0, par).start()
    for copy in local:
        copy.start()

    def from_z(wave):
        b = wave // 2
        for copy in z_copies[1] if b else z_copies[0][2 * wave : 2 * wave + 2]:
            copy.wait_recv()
        if wave == 0:
            for copy in z_copies[0][2:]:
                copy.start()
        y_copy(wave, 0).start()
        y_copy(wave, 1).start()
        x_copy(wave, 0, par).start()
        if wave == 0:
            for copy in in_t[0]:
                copy.start()
        if wave == 1:
            for copy in z_copies[1]:
                copy.start()
            x_own(1, par).start()

    def from_y(wave):
        y_copy(wave, 0).wait_recv()
        y_copy(wave, 2).start()
        y_copy(wave, 1).wait_recv()
        x_copy(wave, 1, par).start()

    def from_y2(wave):
        y_copy(wave, 2).wait_recv()
        x_copy(wave, 2, par).start()

    def from_x(wave):
        if wave != 1:
            x_own(wave // 2, 1 - par).wait_recv()
            s_own(wave // 2, core).start()
        for k in range(3):
            x_copy(wave, k, 1 - par).wait_recv()
        s_copy(wave, core).start()

    def from_s(wave):
        if wave != 1:
            s_own(wave // 2, 1 - core).wait_recv()
        s_copy(wave, 1 - core).wait_recv()
        place(wave)

    from_z(0)
    from_y(0)
    from_y2(0)
    from_z(1)
    from_x(0)
    from_y(1)
    from_y2(1)
    for copy in in_t[0]:
        copy.wait_recv()
    for copy in local:
        copy.wait()
    rows_of(land_t, xw)
    from_s(0)
    from_x(1)
    from_z(2)
    for copy in in_g[0]:
        copy.start()
    from_s(1)
    from_y(2)

    for n in range(0, 3 * INNER, 512):
        cols = slice(n, n + 512)
        packed[:, cols] = nn(xw[...], wqf[:, cols]).astype(BF)
    from_y2(2)

    lane_head = lax.broadcasted_iota(jnp.int32, (TOK, GW), 1) // HEAD_DIM
    banned = jnp.where(lat == n_lat - 1, -1e30, 0.0).astype(F32)

    def spread(rows):
        return [rows * (lane_head[0:1] == h).astype(F32).astype(BF) for h in range(GROUP)]

    def columns(g):
        return [ds(n * INNER + g * GW, GW) for n in range(3)]

    def turned(block):
        return block.astype(F32).T.astype(BF)

    def narrow(right, left):
        for cols in PARTS:
            wide[:, cols] = nn(right, left(cols))
        blocks = [wide[h * HEAD_DIM : (h + 1) * HEAD_DIM, h * TOK : (h + 1) * TOK] for h in range(GROUP)]
        return jnp.concatenate(blocks, axis=0).T.astype(BF)

    def forward(g, carry):
        q_at, k_at, v_at = columns(g)
        for h, rows in enumerate(spread(packed[:, q_at])):
            qblk[g, h * TOK : (h + 1) * TOK, :] = rows

        for cols in PARTS:
            scores[:, cols] = nt(packed[:, k_at], qblk[g, cols, :])

        def soften(c, carry):
            cols = ds(c * 128, 128)
            query = lax.rem(c * 128 + lax.broadcasted_iota(jnp.int32, (1, 128), 1), TOK)
            side = (query >= TOK // 2).astype(F32)
            s = jnp.concatenate(
                [scores[: TOK // 2, cols] + side * banned, scores[TOK // 2 :, cols] + (1.0 - side) * banned], axis=0
            )
            top = jnp.max(s, axis=0, keepdims=True)
            e = jnp.exp((s - top) * (HEAD_DIM ** -0.5))
            pt[g, :, cols] = (e * (1.0 / jnp.sum(e, axis=0, keepdims=True))).astype(BF)
            return carry

        lax.fori_loop(0, WIDE // 128, soften, 0, unroll=3)
        heads[:, q_at] = narrow(turned(packed[:, v_at]), lambda cols: pt[g, :, cols])

        @pl.when(g == 0)
        def _():
            from_x(2)

        return carry

    lax.fori_loop(0, HEADS // GROUP, forward, 0)
    from_s(2)

    for n in range(0, D, 512):
        attn[:, n : n + 512] = nn(heads[...], wof[:, n : n + 512]).astype(BF)

    for copy in in_g[0]:
        copy.wait_recv()
    rows_of(land_g, gw)

    def norm(c, carry):
        rows = ds(c * ROWS, ROWS)
        a = attn[rows, :].astype(F32)
        gain = gain_ref[...]
        scaled = gw[rows, :].astype(F32) * gain
        centered = a - jnp.mean(a, axis=-1, keepdims=True)
        level = scaled - jnp.mean(scaled, axis=-1, keepdims=True)
        inverse = lax.rsqrt(jnp.mean(centered * centered, axis=-1, keepdims=True) + EPS)
        along = jnp.mean(scaled * centered, axis=-1, keepdims=True) * inverse
        normed = centered * inverse
        mixed[rows, :] = (xw[rows, :].astype(F32) + normed * gain + bias_ref[...]).astype(BF)
        agrad[rows, :] = ((level - normed * along) * inverse).astype(BF)
        return carry

    lax.fori_loop(0, TOK // ROWS, norm, 0, unroll=3)

    def halo_out(part, rows, land, out, cols):
        def step(t, carry):
            k, i = 2 * (t // 3), 2 * lax.rem(t, 3)
            block = rows[ds(t * 48, 48), cols]
            for n in (0, 1):
                cells = block[n * 24 : (n + 1) * 24].reshape(2, HALF, LEV, block.shape[-1])
                land[k + n, pl.ds(i, 2), :, :, cols] = cells
            return carry

        lax.fori_loop(0, 6, step, 0)

        def view(ref, k):
            i, j = HALVES[k]
            return ref.at[pl.ds(i * HALF, HALF), pl.ds(j * HALF, HALF), :, cols]

        copies = [
            remote(land.at[k, :, :, :, cols], view(out, k), hs.at[part * 4 + k], hr.at[part * 4 + k], who)
            for k, who in ((1, east), (2, south), (3, far))
        ]
        keep = pltpu.make_async_copy(land.at[0, :, :, :, cols], view(out, 0), own_sem.at[10 + part])
        for copy in copies:
            copy.start()
        keep.start()
        return copies, keep

    going = [halo_out(2, mixed, land_t, m_out, pl.ds(0, D))]

    hgrad[...] = nt(agrad[...], wof[...]).astype(BF)

    def backward(g, carry):
        q_at, k_at, v_at = columns(g)
        for h, rows in enumerate(spread(hgrad[:, q_at])):
            doblk[h * TOK : (h + 1) * TOK, :] = rows

        for cols in PARTS:
            scores[:, cols] = nt(packed[:, v_at], doblk[cols, :])

        def score_grad(c, carry):
            cols = ds(c * 128, 128)
            p, dp = pt[g, :, cols].astype(F32), scores[:, cols]
            total = jnp.sum(p * dp, axis=0, keepdims=True)
            dst[:, cols] = (p * (dp - total) * (HEAD_DIM ** -0.5)).astype(BF)
            return carry

        lax.fori_loop(0, WIDE // 128, score_grad, 0, unroll=3)
        pgrad[:, q_at] = narrow(turned(packed[:, k_at]), lambda cols: dst[:, cols])
        pgrad[:, v_at] = nn(pt[g], doblk[...]).astype(BF)
        pgrad[:, k_at] = nn(dst[...], qblk[g]).astype(BF)
        return carry

    lax.fori_loop(0, HEADS // GROUP, backward, 0)

    for part in range(2):
        cols = pl.ds(part * 512, 512)
        sg = nt(pgrad[...], wqf[cols, :]).astype(BF).astype(F32)
        tgrad[:, cols] = (gw[:, cols].astype(F32) + sg).astype(BF)
        going.append(halo_out(3 + part, tgrad, land_g, d_out, cols))

    for copy in z_copies[0] + z_copies[1]:
        copy.wait_send()
    for wave in range(3):
        for k in range(3):
            y_copy(wave, k).wait_send()
            x_copy(wave, k, par).wait_send()
        s_copy(wave, core).wait_send()
    for b in range(2):
        x_own(b, par).wait_send()
        s_own(b, core).wait_send()
    for copy in in_t[0] + in_g[0]:
        copy.wait_send()
    for copies, keep in going:
        keep.wait()
        for copy in copies:
            copy.wait()


def per_device(n_lat, n_lon, tokens, qkv_weight, out_weight, norm_gain, norm_bias, mixed_grad):
    hbm = pl.BlockSpec(memory_space=pltpu.HBM)
    cells = (WIN, WIN, LEV, D)
    m_out, d_out = pl.pallas_call(
        functools.partial(kernel, n_lat, n_lon),
        out_shape=[jax.ShapeDtypeStruct(cells, BF)] * 2,
        in_specs=[hbm] * 6,
        out_specs=[pl.BlockSpec(memory_space=pl.ANY)] * 2,
        scratch_shapes=[
            pltpu.VMEM((2, 2, 17, D // n_lon, 3 * INNER // 2), BF),
            pltpu.VMEM((2, 2, 17, INNER // n_lon, D // 2), BF),
            pltpu.VMEM((D, 3 * INNER), BF),
            pltpu.VMEM((INNER, D), BF),
            pltpu.VMEM((1, D), F32),
            pltpu.VMEM((1, D), F32),
            pltpu.VMEM((4, HALF, HALF, LEV, D), BF),
            pltpu.VMEM((4, HALF, HALF, LEV, D), BF),
            pltpu.VMEM((TOK, D), BF),
            pltpu.VMEM((TOK, D), BF),
            pltpu.VMEM((TOK, 3 * INNER), BF),
            pltpu.VMEM((TOK, INNER), BF),
            pltpu.VMEM((TOK, D), BF),
            pltpu.VMEM((TOK, D), BF),
            pltpu.VMEM((TOK, INNER), BF),
            pltpu.VMEM((TOK, 3 * INNER), BF),
            pltpu.VMEM((TOK, WIDE), F32),
            pltpu.VMEM((2, TOK, WIDE), BF),
            pltpu.VMEM((TOK, WIDE), BF),
            pltpu.VMEM((2, WIDE, GW), BF),
            pltpu.VMEM((WIDE, GW), BF),
            pltpu.VMEM((GW, WIDE), F32),
            pltpu.VMEM((TOK, D), BF),
            pltpu.VMEM((TOK, D), BF),
            pltpu.SemaphoreType.DMA((15,)),
            pltpu.SemaphoreType.DMA((8,)),
            pltpu.SemaphoreType.DMA((8,)),
            pltpu.SemaphoreType.DMA((9,)),
            pltpu.SemaphoreType.DMA((9,)),
            pltpu.SemaphoreType.DMA((11,)),
            pltpu.SemaphoreType.DMA((11,)),
            pltpu.SemaphoreType.DMA((5,)),
            pltpu.SemaphoreType.DMA((5,)),
            pltpu.SemaphoreType.DMA((20,)),
            pltpu.SemaphoreType.DMA((20,)),
        ],
        compiler_params=pltpu.CompilerParams(
            collective_id=0, has_side_effects=True, vmem_limit_bytes=63 * 1024 * 1024
        ),
    )(
        tokens.transpose(1, 2, 0, 3), mixed_grad.transpose(1, 2, 0, 3), qkv_weight, out_weight,
        norm_gain.reshape(1, D), norm_bias.reshape(1, D),
    )
    return m_out.transpose(2, 0, 1, 3), d_out.transpose(2, 0, 1, 3)


def solution(mesh):
    placed = (
        P(None, "lat", "lon", None),
        P("lon", None),
        P("lon", None),
        P(),
        P(),
        P(None, "lat", "lon", None),
    )
    return jax.shard_map(
        functools.partial(per_device, mesh.shape["lat"], mesh.shape["lon"]),
        mesh=mesh,
        in_specs=placed,
        out_specs=(P(None, "lat", "lon", None), P(None, "lat", "lon", None)),
        check_vma=False,
    )
```

```python
import functools

import jax
import jax.numpy as jnp
from jax import lax
from jax.experimental import pallas as pl
from jax.experimental.pallas import tpu as pltpu
from jax.sharding import PartitionSpec as P

MESH = pl.DeviceIdType.MESH
BF = jnp.bfloat16
F32 = jnp.float32

D = 1024
HEADS = 8
HEAD_DIM = 64
LEV = 2
WIN = 12
INNER = 512
HALF = 6
TOK = LEV * WIN * WIN
QUARTER = TOK // 4
GROUP = 4
GW = GROUP * HEAD_DIM
WIDE = GROUP * TOK
ROWS = 32
EPS = 1e-05

HALVES = ((1, 1), (1, 0), (0, 1), (0, 0))


def nt(a, b):
    return lax.dot_general(a, b, (((1,), (1,)), ((), ())), preferred_element_type=F32)


def nn(a, b):
    return lax.dot_general(a, b, (((1,), (0,)), ((), ())), preferred_element_type=F32)


def tn(a, b):
    return lax.dot_general(a, b, (((0,), (0,)), ((), ())), preferred_element_type=F32)


def ds(start, size):
    return pl.ds(pl.multiple_of(start, size), size)


def kernel(
    n_lat, n_lon,
    t_ref, g_ref, wq_ref, wo_ref, gain_hbm, bias_hbm,
    m_out, d_out,
    comb_q, comb_o, wqf, wof, gain_ref, bias_ref, land_t, land_g, xw, gw, packed, heads, attn, agrad, hgrad, pgrad,
    scores, pt, dst, qblk, doblk, wide, mixed, tgrad,
    own_sem, zs, zr, ys, yr, xs, xr, ss, sr, hs, hr,
):
    lat, lon = lax.axis_index("lat"), lax.axis_index("lon")
    nz, ny = n_lon // 2, n_lat // 4
    rq, ro = D // n_lon, INNER // n_lon
    core, par, z = lax.rem(lat, 2), lax.rem(lon, 2), lon // 2
    half, y = lat // (2 * ny), lax.rem(lat // 2, ny)
    lat_lo, lat_hi = lax.rem(lat + n_lat - 1, n_lat), lax.rem(lat + 1, n_lat)
    lon_lo, lon_hi = lax.rem(lon + n_lon - 1, n_lon), lax.rem(lon + 1, n_lon)
    sib = (lat + 1 - 2 * core, lon)
    differ = lax.rem(par + core, 2)
    across = lon + 1 - 2 * par
    x_to = (lax.rem(lat + differ * (n_lat // 2), n_lat), across)
    x_from = (lax.rem(lat + (1 - differ) * (n_lat // 2), n_lat), across)
    west, north, diag = (lat, lon_lo), (lat_lo, lon), (lat_lo, lon_lo)
    east, south, far = (lat, lon_hi), (lat_hi, lon), (lat_hi, lon_hi)

    def offset(yy, e):
        far_pair = e // 2
        size = (1 - far_pair) * (yy + 1) + far_pair * (2 * ny - yy)
        return (1 - 2 * lax.rem(e, 2)) * size

    def z_to(e):
        return (lat, 2 * lax.rem(z + offset(y, e) + nz, nz) + par)

    def source(yy, e):
        return lax.rem(z - offset(yy, e) + nz, nz)

    def y_to(way):
        return ((half * ny + lax.rem(y + 1 - 2 * way + ny, ny)) * 2 + core, lon)

    opposite = ((half * ny + lax.rem(y + 2, ny)) * 2 + core, lon)

    def line(group, c):
        return lax.rem(y + ny + (0, 2 * c - 1, 1 - 2 * c, 2)[group], ny)

    comb, cut = (comb_q, comb_o), (3 * INNER // 2, D // 2)
    own = [
        ((wq_ref, wo_ref)[b].at[:, c * cut[b] : (c + 1) * cut[b]], comb[b].at[c, par, 0])
        for b in range(2) for c in range(2)
    ]
    own = [pltpu.make_async_copy(src, to, own_sem.at[8 + k]) for k, (src, to) in enumerate(own)]
    for copy in own:
        copy.start()

    barrier = pltpu.get_barrier_semaphore()
    met = [z_to(e) for e in range(4)]
    met += [y_to(0), y_to(1), opposite, sib, x_to, x_from, west, north, diag, east, south, far]
    for who in met:
        pl.semaphore_signal(barrier, inc=1, device_id=who, device_id_type=MESH)
    for copy in own:
        copy.wait()
    pl.semaphore_wait(barrier, len(met))

    def remote(src, dst, send, recv, who):
        return pltpu.make_async_remote_copy(
            src_ref=src, dst_ref=dst, send_sem=send, recv_sem=recv, device_id=who, device_id_type=MESH
        )

    def quarter(ref, k):
        i, j = HALVES[k]
        return ref.at[pl.ds(i * HALF, HALF), pl.ds(j * HALF, HALF)]

    def halo_in(field, src, land):
        copies = [
            remote(quarter(src, k), land.at[k], hs.at[field * 4 + k], hr.at[field * 4 + k], who)
            for k, who in ((1, west), (2, north), (3, diag))
        ]
        return copies, pltpu.make_async_copy(quarter(src, 0), land.at[0], own_sem.at[4 + field])

    in_t = halo_in(0, t_ref, land_t)
    in_g = halo_in(1, g_ref, land_g)
    def slots(wave, group, count=1):
        if wave < 2:
            return pl.ds(1 + wave * 8 + group * 2, count * 2)
        return pl.ds(1 + group * 4, count * 4)

    def z_copy(b, e):
        slot = 1 + e if b else 1 + e // 2 * 8 + e % 2
        i = b * 4 + e
        return remote(comb[b].at[core, par, 0], comb[b].at[core, par, slot], zs.at[i], zr.at[i], z_to(e))

    def y_copy(wave, k):
        i, buf = wave * 3 + k, comb[wave // 2]
        return remote(
            buf.at[core, par, slots(wave, 0)], buf.at[core, par, slots(wave, k + 1)], ys.at[i], yr.at[i],
            (y_to(core), y_to(1 - core), opposite)[k],
        )

    def x_copy(wave, k, p):
        ref = comb[wave // 2].at[core, p, slots(wave, k, 1 + 2 * k)]
        i = wave * 2 + k
        return remote(ref, ref, xs.at[i], xr.at[i], x_to)

    def x_own(b, p):
        ref = comb[b].at[core, p, 0]
        return remote(ref, ref, xs.at[6 + b], xr.at[6 + b], x_to)

    def s_copy(wave, other, c):
        ref = comb[wave // 2].at[c, lax.rem(par + other, 2), slots(wave, 0, 4)]
        i = wave * 2 + other
        return remote(ref, ref, ss.at[i], sr.at[i], sib)

    def s_own(b, c):
        ref = comb[b].at[c, 1 - par, 0]
        return remote(ref, ref, ss.at[6 + b], sr.at[6 + b], sib)

    def place(wave):
        b = wave // 2
        full, size = ((wqf, rq), (wof, ro))[b]
        for c in range(2):
            found = [] if wave == 1 else [(0, z)]
            for j in range(4):
                for i in range(4 if b else 2):
                    e = i if b else 2 * wave + i
                    found.append((slots(wave, j).start + i, source(line(j, c), e)))
            for slot, zq in found:
                for p in range(2):
                    full[ds((zq * 2 + p) * size, size), c * cut[b] : (c + 1) * cut[b]] = comb[b][c, p, slot]

    local = [
        pltpu.make_async_copy(gain_hbm, gain_ref, own_sem.at[2]),
        pltpu.make_async_copy(bias_hbm, bias_ref, own_sem.at[3]),
        in_t[1],
        in_g[1],
    ]

    def rows_of(land, field):
        def step(t, carry):
            k, i = 2 * (t // 3), 2 * lax.rem(t, 3)
            two = [land[k + n, pl.ds(i, 2)].reshape(24, D) for n in (0, 1)]
            field[ds(t * 48, 48), :] = jnp.concatenate(two, axis=0)
            return carry

        lax.fori_loop(0, 6, step, 0)

    z_copies = [[z_copy(b, e) for e in range(4)] for b in range(2)]
    for copy in z_copies[0]:
        copy.start()
    x_own(0, par).start()
    for copy in local:
        copy.start()

    def from_z(wave):
        b = wave // 2
        for copy in z_copies[1] if b else z_copies[0][2 * wave : 2 * wave + 2]:
            copy.wait_recv()
        for k in (2, 0, 1):
            y_copy(wave, k).start()
        x_copy(wave, 0, par).start()
        if wave == 0:
            for copy in in_t[0]:
                copy.start()
        if wave == 1:
            for copy in z_copies[1]:
                copy.start()
            x_own(1, par).start()

    def from_y(wave):
        for k in range(3):
            y_copy(wave, k).wait_recv()
        x_copy(wave, 1, par).start()
        s_copy(wave, 0, core).start()

    def from_x(wave):
        if wave != 1:
            x_own(wave // 2, 1 - par).wait_recv()
            s_own(wave // 2, core).start()
        for k in range(2):
            x_copy(wave, k, 1 - par).wait_recv()
        s_copy(wave, 1, core).start()

    def from_s(wave):
        if wave != 1:
            s_own(wave // 2, 1 - core).wait_recv()
        for other in range(2):
            s_copy(wave, other, 1 - core).wait_recv()
        place(wave)

    from_z(0)
    from_y(0)
    from_z(1)
    from_x(0)
    from_y(1)
    for copy in in_t[0]:
        copy.wait_recv()
    for copy in local:
        copy.wait()
    rows_of(land_t, xw)
    from_s(0)
    from_x(1)
    from_z(2)
    for copy in in_g[0]:
        copy.start()
    from_s(1)
    from_y(2)

    for n in range(3 * INNER // 256):
        cols = slice(n * 256, n * 256 + 256)
        packed[:, cols] = nn(xw[...], wqf[:, cols]).astype(BF)

    lane_head = lax.broadcasted_iota(jnp.int32, (TOK, GW), 1) // HEAD_DIM
    banned = jnp.where(lat == n_lat - 1, -1e30, 0.0).astype(F32)

    def spread(rows):
        return [rows * (lane_head[0:1] == h).astype(F32).astype(BF) for h in range(GROUP)]

    def columns(g):
        return [ds(n * INNER + g * GW, GW) for n in range(3)]

    def turned(block):
        return block.astype(F32).T.astype(BF)

    def narrow(right, left):
        for c in range(0, WIDE, 384):
            wide[:, c : c + 384] = nn(right, left(slice(c, c + 384)))
        blocks = [wide[h * HEAD_DIM : (h + 1) * HEAD_DIM, h * TOK : (h + 1) * TOK] for h in range(GROUP)]
        return jnp.concatenate(blocks, axis=0).T.astype(BF)

    def forward(g, carry):
        q_at, k_at, v_at = columns(g)
        for h, rows in enumerate(spread(packed[:, q_at])):
            qblk[g, h * TOK : (h + 1) * TOK, :] = rows

        for c in range(0, WIDE, 384):
            scores[:, c : c + 384] = nt(packed[:, k_at], qblk[g, c : c + 384, :])
        for c in range(0, WIDE, 128):
            cols = slice(c, c + 128)
            query = lax.rem(c + lax.broadcasted_iota(jnp.int32, (1, 128), 1), TOK)
            side = (query >= TOK // 2).astype(F32)
            s = jnp.concatenate(
                [scores[: TOK // 2, cols] + side * banned, scores[TOK // 2 :, cols] + (1.0 - side) * banned], axis=0
            )
            top = jnp.max(s, axis=0, keepdims=True)
            e = jnp.exp((s - top) * (HEAD_DIM ** -0.5))
            pt[g, :, cols] = (e * (1.0 / jnp.sum(e, axis=0, keepdims=True))).astype(BF)
        heads[:, q_at] = narrow(turned(packed[:, v_at]), lambda cols: pt[g, :, cols])

        @pl.when(g == 0)
        def _():
            from_x(2)

        return carry

    lax.fori_loop(0, HEADS // GROUP, forward, 0)
    from_s(2)

    for n in range(0, D, 256):
        attn[:, n : n + 256] = nn(heads[...], wof[:, n : n + 256]).astype(BF)

    for copy in in_g[0]:
        copy.wait_recv()
    rows_of(land_g, gw)

    def norm(c, carry):
        rows = ds(c * ROWS, ROWS)
        a = attn[rows, :].astype(F32)
        gain = gain_ref[...]
        scaled = gw[rows, :].astype(F32) * gain
        centered = a - jnp.mean(a, axis=-1, keepdims=True)
        level = scaled - jnp.mean(scaled, axis=-1, keepdims=True)
        inverse = lax.rsqrt(jnp.mean(centered * centered, axis=-1, keepdims=True) + EPS)
        along = jnp.mean(scaled * centered, axis=-1, keepdims=True) * inverse
        normed = centered * inverse
        mixed[rows, :] = (xw[rows, :].astype(F32) + normed * gain + bias_ref[...]).astype(BF)
        agrad[rows, :] = ((level - normed * along) * inverse).astype(BF)
        return carry

    lax.fori_loop(0, TOK // ROWS, norm, 0, unroll=3)

    def halo_out(field, rows, land, out):
        def step(t, carry):
            k, i = 2 * (t // 3), 2 * lax.rem(t, 3)
            block = rows[ds(t * 48, 48), :]
            for n in (0, 1):
                land[k + n, pl.ds(i, 2)] = block[n * 24 : (n + 1) * 24].reshape(2, HALF, LEV, D)
            return carry

        lax.fori_loop(0, 6, step, 0)
        copies = [
            remote(land.at[k], quarter(out, k), hs.at[(field + 2) * 4 + k], hr.at[(field + 2) * 4 + k], who)
            for k, who in ((1, east), (2, south), (3, far))
        ]
        keep = pltpu.make_async_copy(land.at[0], quarter(out, 0), own_sem.at[6 + field])
        for copy in copies:
            copy.start()
        keep.start()
        return copies, keep

    out_m = halo_out(0, mixed, land_t, m_out)

    for n in range(0, INNER, 256):
        hgrad[:, n : n + 256] = nt(agrad[...], wof[n : n + 256, :]).astype(BF)

    def backward(g, carry):
        q_at, k_at, v_at = columns(g)
        for h, rows in enumerate(spread(hgrad[:, q_at])):
            doblk[h * TOK : (h + 1) * TOK, :] = rows

        for c in range(0, WIDE, 384):
            scores[:, c : c + 384] = nt(packed[:, v_at], doblk[c : c + 384, :])
        for c in range(0, WIDE, 128):
            cols = slice(c, c + 128)
            p, dp = pt[g, :, cols].astype(F32), scores[:, cols]
            total = jnp.sum(p * dp, axis=0, keepdims=True)
            dst[:, cols] = (p * (dp - total) * (HEAD_DIM ** -0.5)).astype(BF)
        pgrad[:, q_at] = narrow(turned(packed[:, k_at]), lambda cols: dst[:, cols])
        pgrad[:, v_at] = nn(pt[g], doblk[...]).astype(BF)
        pgrad[:, k_at] = nn(dst[...], qblk[g]).astype(BF)
        return carry

    lax.fori_loop(0, HEADS // GROUP, backward, 0)

    for n in range(0, D, 256):
        cols = slice(n, n + 256)
        sg = nt(pgrad[...], wqf[cols, :]).astype(BF).astype(F32)
        tgrad[:, cols] = (gw[:, cols].astype(F32) + sg).astype(BF)
    out_d = halo_out(1, tgrad, land_g, d_out)

    for copy in z_copies[0] + z_copies[1]:
        copy.wait_send()
    for wave in range(3):
        for k in range(3):
            y_copy(wave, k).wait_send()
        for k in range(2):
            x_copy(wave, k, par).wait_send()
            s_copy(wave, k, core).wait_send()
    for b in range(2):
        x_own(b, par).wait_send()
        s_own(b, core).wait_send()
    for copy in in_t[0] + in_g[0]:
        copy.wait_send()
    for copies, keep in (out_m, out_d):
        keep.wait()
        for copy in copies:
            copy.wait()


def per_device(n_lat, n_lon, tokens, qkv_weight, out_weight, norm_gain, norm_bias, mixed_grad):
    hbm = pl.BlockSpec(memory_space=pltpu.HBM)
    cells = (WIN, WIN, LEV, D)
    m_out, d_out = pl.pallas_call(
        functools.partial(kernel, n_lat, n_lon),
        out_shape=[jax.ShapeDtypeStruct(cells, BF)] * 2,
        in_specs=[hbm] * 6,
        out_specs=[pl.BlockSpec(memory_space=pl.ANY)] * 2,
        scratch_shapes=[
            pltpu.VMEM((2, 2, 17, D // n_lon, 3 * INNER // 2), BF),
            pltpu.VMEM((2, 2, 17, INNER // n_lon, D // 2), BF),
            pltpu.VMEM((D, 3 * INNER), BF),
            pltpu.VMEM((INNER, D), BF),
            pltpu.VMEM((1, D), F32),
            pltpu.VMEM((1, D), F32),
            pltpu.VMEM((4, HALF, HALF, LEV, D), BF),
            pltpu.VMEM((4, HALF, HALF, LEV, D), BF),
            pltpu.VMEM((TOK, D), BF),
            pltpu.VMEM((TOK, D), BF),
            pltpu.VMEM((TOK, 3 * INNER), BF),
            pltpu.VMEM((TOK, INNER), BF),
            pltpu.VMEM((TOK, D), BF),
            pltpu.VMEM((TOK, D), BF),
            pltpu.VMEM((TOK, INNER), BF),
            pltpu.VMEM((TOK, 3 * INNER), BF),
            pltpu.VMEM((TOK, WIDE), F32),
            pltpu.VMEM((2, TOK, WIDE), BF),
            pltpu.VMEM((TOK, WIDE), BF),
            pltpu.VMEM((2, WIDE, GW), BF),
            pltpu.VMEM((WIDE, GW), BF),
            pltpu.VMEM((GW, WIDE), F32),
            pltpu.VMEM((TOK, D), BF),
            pltpu.VMEM((TOK, D), BF),
            pltpu.SemaphoreType.DMA((12,)),
            pltpu.SemaphoreType.DMA((8,)),
            pltpu.SemaphoreType.DMA((8,)),
            pltpu.SemaphoreType.DMA((9,)),
            pltpu.SemaphoreType.DMA((9,)),
            pltpu.SemaphoreType.DMA((11,)),
            pltpu.SemaphoreType.DMA((11,)),
            pltpu.SemaphoreType.DMA((8,)),
            pltpu.SemaphoreType.DMA((8,)),
            pltpu.SemaphoreType.DMA((16,)),
            pltpu.SemaphoreType.DMA((16,)),
        ],
        compiler_params=pltpu.CompilerParams(
            collective_id=0, has_side_effects=True, vmem_limit_bytes=63 * 1024 * 1024
        ),
    )(
        tokens.transpose(1, 2, 0, 3), mixed_grad.transpose(1, 2, 0, 3), qkv_weight, out_weight,
        norm_gain.reshape(1, D), norm_bias.reshape(1, D),
    )
    return m_out.transpose(2, 0, 1, 3), d_out.transpose(2, 0, 1, 3)


def solution(mesh):
    placed = (
        P(None, "lat", "lon", None),
        P("lon", None),
        P("lon", None),
        P(),
        P(),
        P(None, "lat", "lon", None),
    )
    return jax.shard_map(
        functools.partial(per_device, mesh.shape["lat"], mesh.shape["lon"]),
        mesh=mesh,
        in_specs=placed,
        out_specs=(P(None, "lat", "lon", None), P(None, "lat", "lon", None)),
        check_vma=False,
    )
```

```python
import functools

import jax
import jax.numpy as jnp
from jax import lax
from jax.experimental import pallas as pl
from jax.experimental.pallas import tpu as pltpu
from jax.sharding import PartitionSpec as P

MESH = pl.DeviceIdType.MESH
BF = jnp.bfloat16
F32 = jnp.float32

D = 1024
HEADS = 8
HEAD_DIM = 64
LEV = 2
WIN = 12
INNER = 512
HALF = 6
TOK = LEV * WIN * WIN
QUARTER = TOK // 4
GROUP = 4
GW = GROUP * HEAD_DIM
WIDE = GROUP * TOK
ROWS = 32
EPS = 1e-05

PIECE = 80
HALVES = ((1, 1), (1, 0), (0, 1), (0, 0))
SENT, INSIDE = (64, 144, 208), (0, 8, 0, 8)


def nt(a, b):
    return lax.dot_general(a, b, (((1,), (1,)), ((), ())), preferred_element_type=F32)


def nn(a, b):
    return lax.dot_general(a, b, (((1,), (0,)), ((), ())), preferred_element_type=F32)


def tn(a, b):
    return lax.dot_general(a, b, (((0,), (0,)), ((), ())), preferred_element_type=F32)


def ds(start, size):
    return pl.ds(pl.multiple_of(start, size), size)


def kernel(
    n_lat, n_lon,
    t_ref, g_ref, wq_ref, wo_ref, gain_hbm, bias_hbm,
    m_out, d_out,
    comb_q, comb_o, wqf, wof, gain_ref, bias_ref, land_t, land_g, xw, gw, packed, heads, attn, agrad, hgrad, pgrad,
    scores, pt, dst, qblk, doblk, wide, mixed, tgrad,
    own_sem, zs, zr, ys, yr, xs, xr, ss, sr, hs, hr,
):
    lat, lon = lax.axis_index("lat"), lax.axis_index("lon")
    nz, ny = n_lon // 2, n_lat // 4
    rq, ro = D // n_lon, INNER // n_lon
    core, par, z = lax.rem(lat, 2), lax.rem(lon, 2), lon // 2
    half, y = lat // (2 * ny), lax.rem(lat // 2, ny)
    lat_lo, lat_hi = lax.rem(lat + n_lat - 1, n_lat), lax.rem(lat + 1, n_lat)
    lon_lo, lon_hi = lax.rem(lon + n_lon - 1, n_lon), lax.rem(lon + 1, n_lon)
    sib = (lat + 1 - 2 * core, lon)
    differ = lax.rem(par + core, 2)
    across = lon + 1 - 2 * par
    x_to = (lax.rem(lat + differ * (n_lat // 2), n_lat), across)
    x_from = (lax.rem(lat + (1 - differ) * (n_lat // 2), n_lat), across)
    west, north, diag = (lat, lon_lo), (lat_lo, lon), (lat_lo, lon_lo)
    east, south, far = (lat, lon_hi), (lat_hi, lon), (lat_hi, lon_hi)

    def offset(yy, e):
        far_pair = e // 2
        size = (1 - far_pair) * (yy + 1) + far_pair * (2 * ny - yy)
        return (1 - 2 * lax.rem(e, 2)) * size

    def z_to(e):
        return (lat, 2 * lax.rem(z + offset(y, e) + nz, nz) + par)

    def source(yy, e):
        return lax.rem(z - offset(yy, e) + nz, nz)

    def y_to(way):
        return ((half * ny + lax.rem(y + 1 - 2 * way + ny, ny)) * 2 + core, lon)

    def line(group, c):
        return lax.rem(y + ny + (0, 2 * c - 1, 1 - 2 * c, 2)[group], ny)

    comb, cut = (comb_q, comb_o), (3 * INNER // 2, D // 2)
    own = [
        ((wq_ref, wo_ref)[b].at[:, c * cut[b] : (c + 1) * cut[b]], comb[b].at[c, par, 0])
        for b in range(2) for c in range(2)
    ]
    own = [pltpu.make_async_copy(src, to, own_sem.at[8 + k]) for k, (src, to) in enumerate(own)]
    for copy in own:
        copy.start()

    barrier = pltpu.get_barrier_semaphore()
    met = [z_to(e) for e in range(4)]
    met += [y_to(0), y_to(1), sib, x_to, x_from, west, north, diag, east, south, far]
    for who in met:
        pl.semaphore_signal(barrier, inc=1, device_id=who, device_id_type=MESH)
    for copy in own:
        copy.wait()
    pl.semaphore_wait(barrier, len(met))

    def remote(src, dst, send, recv, who):
        return pltpu.make_async_remote_copy(
            src_ref=src, dst_ref=dst, send_sem=send, recv_sem=recv, device_id=who, device_id_type=MESH
        )

    def halo_in(field, rows, land):
        return [
            remote(rows.at[pl.ds(SENT[k], PIECE)], land.at[k], hs.at[field * 3 + k], hr.at[field * 3 + k], who)
            for k, who in enumerate((west, north, diag))
        ]

    def assemble(rows, land, field):
        row = lax.broadcasted_iota(jnp.int32, (16, D), 0)

        def seam(above, below):
            return jnp.where(row < 8, above.astype(F32), below.astype(F32)).astype(BF)

        field[0:64, :] = rows[0:64, :]
        field[64:80, :] = seam(rows[64:80, :], land[0, 0:16, :])
        field[80:144, :] = land[0, 16:80, :]
        field[144:208, :] = land[1, 0:64, :]
        field[208:224, :] = seam(land[1, 64:80, :], land[2, 0:16, :])
        field[224:288, :] = land[2, 16:80, :]

    in_t = halo_in(0, t_ref, land_t)
    in_g = halo_in(1, g_ref, land_g)
    def slots(wave, group, count=1):
        if wave < 2:
            return pl.ds(1 + wave * 8 + group * 2, count * 2)
        return pl.ds(1 + group * 4, count * 4)

    def z_copy(b, e):
        slot = 1 + e if b else 1 + e // 2 * 8 + e % 2
        i = b * 4 + e
        return remote(comb[b].at[core, par, 0], comb[b].at[core, par, slot], zs.at[i], zr.at[i], z_to(e))

    def y_copy(wave, k):
        src, dst = ((0, 1), (0, 2), (1, 3))[k]
        i, buf = wave * 3 + k, comb[wave // 2]
        return remote(
            buf.at[core, par, slots(wave, src)], buf.at[core, par, slots(wave, dst)], ys.at[i], yr.at[i],
            y_to(1 - core if k == 1 else core),
        )

    def x_copy(wave, k, p):
        ref = comb[wave // 2].at[core, p, slots(wave, (0, 1, 3)[k], (1, 2, 1)[k])]
        i = wave * 3 + k
        return remote(ref, ref, xs.at[i], xr.at[i], x_to)

    def x_own(b, p):
        ref = comb[b].at[core, p, 0]
        return remote(ref, ref, xs.at[9 + b], xr.at[9 + b], x_to)

    def s_copy(wave, c):
        ref = comb[wave // 2].at[c, :, slots(wave, 0, 4)]
        return remote(ref, ref, ss.at[wave], sr.at[wave], sib)

    def s_own(b, c):
        ref = comb[b].at[c, 1 - par, 0]
        return remote(ref, ref, ss.at[3 + b], sr.at[3 + b], sib)

    def place(wave):
        b = wave // 2
        full, size = ((wqf, rq), (wof, ro))[b]
        for c in range(2):
            found = [] if wave == 1 else [(0, z)]
            for j in range(4):
                for i in range(4 if b else 2):
                    e = i if b else 2 * wave + i
                    found.append((slots(wave, j).start + i, source(line(j, c), e)))
            for slot, zq in found:
                for p in range(2):
                    full[ds((zq * 2 + p) * size, size), c * cut[b] : (c + 1) * cut[b]] = comb[b][c, p, slot]

    local = [
        pltpu.make_async_copy(gain_hbm, gain_ref, own_sem.at[2]),
        pltpu.make_async_copy(bias_hbm, bias_ref, own_sem.at[3]),
    ]

    z_copies = [[z_copy(b, e) for e in range(4)] for b in range(2)]
    for copy in z_copies[0][:2]:
        copy.start()
    x_own(0, par).start()
    for copy in local:
        copy.start()

    def from_z(wave):
        b = wave // 2
        for copy in z_copies[1] if b else z_copies[0][2 * wave : 2 * wave + 2]:
            copy.wait_recv()
        if wave == 0:
            for copy in z_copies[0][2:]:
                copy.start()
        y_copy(wave, 0).start()
        y_copy(wave, 1).start()
        x_copy(wave, 0, par).start()
        if wave == 0:
            for copy in in_t:
                copy.start()
        if wave == 1:
            for copy in z_copies[1]:
                copy.start()
            x_own(1, par).start()

    def from_y(wave):
        y_copy(wave, 0).wait_recv()
        y_copy(wave, 2).start()
        y_copy(wave, 1).wait_recv()
        x_copy(wave, 1, par).start()

    def from_y2(wave):
        y_copy(wave, 2).wait_recv()
        x_copy(wave, 2, par).start()

    def from_x(wave):
        if wave != 1:
            x_own(wave // 2, 1 - par).wait_recv()
            s_own(wave // 2, core).start()
        for k in range(3):
            x_copy(wave, k, 1 - par).wait_recv()
        s_copy(wave, core).start()

    def from_s(wave):
        if wave != 1:
            s_own(wave // 2, 1 - core).wait_recv()
        s_copy(wave, 1 - core).wait_recv()
        place(wave)

    from_z(0)
    from_y(0)
    from_y2(0)
    from_z(1)
    from_x(0)
    from_y(1)
    from_y2(1)
    for copy in in_t:
        copy.wait_recv()
    for copy in local:
        copy.wait()
    assemble(t_ref, land_t, xw)
    from_s(0)
    from_x(1)
    from_z(2)
    for copy in in_g:
        copy.start()
    from_s(1)
    from_y(2)

    for n in range(3 * INNER // 256):
        cols = slice(n * 256, n * 256 + 256)
        packed[:, cols] = nn(xw[...], wqf[:, cols]).astype(BF)
    from_y2(2)

    lane_head = lax.broadcasted_iota(jnp.int32, (TOK, GW), 1) // HEAD_DIM
    banned = jnp.where(lat == n_lat - 1, -1e30, 0.0).astype(F32)

    def spread(rows):
        return [rows * (lane_head[0:1] == h).astype(F32).astype(BF) for h in range(GROUP)]

    def columns(g):
        return [ds(n * INNER + g * GW, GW) for n in range(3)]

    def turned(block):
        return block.astype(F32).T.astype(BF)

    def narrow(right, left):
        for c in range(0, WIDE, 384):
            wide[:, c : c + 384] = nn(right, left(slice(c, c + 384)))
        blocks = [wide[h * HEAD_DIM : (h + 1) * HEAD_DIM, h * TOK : (h + 1) * TOK] for h in range(GROUP)]
        return jnp.concatenate(blocks, axis=0).T.astype(BF)

    def forward(g, carry):
        q_at, k_at, v_at = columns(g)
        for h, rows in enumerate(spread(packed[:, q_at])):
            qblk[g, h * TOK : (h + 1) * TOK, :] = rows

        for c in range(0, WIDE, 384):
            scores[:, c : c + 384] = nt(packed[:, k_at], qblk[g, c : c + 384, :])
        for c in range(0, WIDE, 128):
            cols = slice(c, c + 128)
            query = lax.rem(c + lax.broadcasted_iota(jnp.int32, (1, 128), 1), TOK)
            side = (query >= TOK // 2).astype(F32)
            s = jnp.concatenate(
                [scores[: TOK // 2, cols] + side * banned, scores[TOK // 2 :, cols] + (1.0 - side) * banned], axis=0
            )
            top = jnp.max(s, axis=0, keepdims=True)
            e = jnp.exp((s - top) * (HEAD_DIM ** -0.5))
            pt[g, :, cols] = (e * (1.0 / jnp.sum(e, axis=0, keepdims=True))).astype(BF)
        heads[:, q_at] = narrow(turned(packed[:, v_at]), lambda cols: pt[g, :, cols])

        @pl.when(g == 0)
        def _():
            from_x(2)

        return carry

    lax.fori_loop(0, HEADS // GROUP, forward, 0)
    from_s(2)

    for n in range(0, D, 256):
        attn[:, n : n + 256] = nn(heads[...], wof[:, n : n + 256]).astype(BF)

    for copy in in_g:
        copy.wait_recv()
    assemble(g_ref, land_g, gw)

    def norm(c, carry):
        rows = ds(c * ROWS, ROWS)
        a = attn[rows, :].astype(F32)
        gain = gain_ref[...]
        scaled = gw[rows, :].astype(F32) * gain
        centered = a - jnp.mean(a, axis=-1, keepdims=True)
        level = scaled - jnp.mean(scaled, axis=-1, keepdims=True)
        inverse = lax.rsqrt(jnp.mean(centered * centered, axis=-1, keepdims=True) + EPS)
        along = jnp.mean(scaled * centered, axis=-1, keepdims=True) * inverse
        normed = centered * inverse
        mixed[rows, :] = (xw[rows, :].astype(F32) + normed * gain + bias_ref[...]).astype(BF)
        agrad[rows, :] = ((level - normed * along) * inverse).astype(BF)
        return carry

    lax.fori_loop(0, TOK // ROWS, norm, 0, unroll=3)

    def halo_out(field, rows, out):
        copies = [
            remote(
                rows.at[pl.ds(SENT[k], PIECE)], out.at[k + 1],
                hs.at[(field + 2) * 3 + k], hr.at[(field + 2) * 3 + k], who,
            )
            for k, who in enumerate((east, south, far))
        ]
        keep = pltpu.make_async_copy(rows.at[pl.ds(0, PIECE)], out.at[0], own_sem.at[6 + field])
        for copy in copies:
            copy.start()
        keep.start()
        return copies, keep

    out_m = halo_out(0, mixed, m_out)

    for n in range(0, INNER, 256):
        hgrad[:, n : n + 256] = nt(agrad[...], wof[n : n + 256, :]).astype(BF)

    def backward(g, carry):
        q_at, k_at, v_at = columns(g)
        for h, rows in enumerate(spread(hgrad[:, q_at])):
            doblk[h * TOK : (h + 1) * TOK, :] = rows

        for c in range(0, WIDE, 384):
            scores[:, c : c + 384] = nt(packed[:, v_at], doblk[c : c + 384, :])
        for c in range(0, WIDE, 128):
            cols = slice(c, c + 128)
            p, dp = pt[g, :, cols].astype(F32), scores[:, cols]
            total = jnp.sum(p * dp, axis=0, keepdims=True)
            dst[:, cols] = (p * (dp - total) * (HEAD_DIM ** -0.5)).astype(BF)
        pgrad[:, q_at] = narrow(turned(packed[:, k_at]), lambda cols: dst[:, cols])
        pgrad[:, v_at] = nn(pt[g], doblk[...]).astype(BF)
        pgrad[:, k_at] = nn(dst[...], qblk[g]).astype(BF)
        return carry

    lax.fori_loop(0, HEADS // GROUP, backward, 0)

    for n in range(0, D, 256):
        cols = slice(n, n + 256)
        sg = nt(pgrad[...], wqf[cols, :]).astype(BF).astype(F32)
        tgrad[:, cols] = (gw[:, cols].astype(F32) + sg).astype(BF)
    out_d = halo_out(1, tgrad, d_out)

    for copy in z_copies[0] + z_copies[1]:
        copy.wait_send()
    for wave in range(3):
        for k in range(3):
            y_copy(wave, k).wait_send()
            x_copy(wave, k, par).wait_send()
        s_copy(wave, core).wait_send()
    for b in range(2):
        x_own(b, par).wait_send()
        s_own(b, core).wait_send()
    for copy in in_t + in_g:
        copy.wait_send()
    for copies, keep in (out_m, out_d):
        keep.wait()
        for copy in copies:
            copy.wait()


def per_device(n_lat, n_lon, tokens, qkv_weight, out_weight, norm_gain, norm_bias, mixed_grad):
    hbm = pl.BlockSpec(memory_space=pltpu.HBM)
    vmem = pl.BlockSpec(memory_space=pltpu.VMEM)

    def rows_of(field):
        cut = field.transpose(1, 2, 0, 3).reshape(2, HALF, 2, HALF, LEV, D)
        return jnp.concatenate([cut[i, :, j].reshape(QUARTER, D) for i, j in HALVES], axis=0)

    def join(pieces):
        own, left, above, corner = (
            pieces[k, INSIDE[k] : INSIDE[k] + QUARTER].reshape(HALF, HALF, LEV, D) for k in range(4)
        )
        cells = jnp.concatenate(
            [jnp.concatenate([corner, above], axis=1), jnp.concatenate([left, own], axis=1)], axis=0
        )
        return cells.transpose(2, 0, 1, 3)

    m_out, d_out = pl.pallas_call(
        functools.partial(kernel, n_lat, n_lon),
        out_shape=[jax.ShapeDtypeStruct((4, PIECE, D), BF)] * 2,
        in_specs=[vmem, vmem, hbm, hbm, hbm, hbm],
        out_specs=[pl.BlockSpec(memory_space=pl.ANY)] * 2,
        scratch_shapes=[
            pltpu.VMEM((2, 2, 17, D // n_lon, 3 * INNER // 2), BF),
            pltpu.VMEM((2, 2, 17, INNER // n_lon, D // 2), BF),
            pltpu.VMEM((D, 3 * INNER), BF),
            pltpu.VMEM((INNER, D), BF),
            pltpu.VMEM((1, D), F32),
            pltpu.VMEM((1, D), F32),
            pltpu.VMEM((3, PIECE, D), BF),
            pltpu.VMEM((3, PIECE, D), BF),
            pltpu.VMEM((TOK, D), BF),
            pltpu.VMEM((TOK, D), BF),
            pltpu.VMEM((TOK, 3 * INNER), BF),
            pltpu.VMEM((TOK, INNER), BF),
            pltpu.VMEM((TOK, D), BF),
            pltpu.VMEM((TOK, D), BF),
            pltpu.VMEM((TOK, INNER), BF),
            pltpu.VMEM((TOK, 3 * INNER), BF),
            pltpu.VMEM((TOK, WIDE), F32),
            pltpu.VMEM((2, TOK, WIDE), BF),
            pltpu.VMEM((TOK, WIDE), BF),
            pltpu.VMEM((2, WIDE, GW), BF),
            pltpu.VMEM((WIDE, GW), BF),
            pltpu.VMEM((GW, WIDE), F32),
            pltpu.VMEM((TOK, D), BF),
            pltpu.VMEM((TOK, D), BF),
            pltpu.SemaphoreType.DMA((12,)),
            pltpu.SemaphoreType.DMA((8,)),
            pltpu.SemaphoreType.DMA((8,)),
            pltpu.SemaphoreType.DMA((9,)),
            pltpu.SemaphoreType.DMA((9,)),
            pltpu.SemaphoreType.DMA((11,)),
            pltpu.SemaphoreType.DMA((11,)),
            pltpu.SemaphoreType.DMA((5,)),
            pltpu.SemaphoreType.DMA((5,)),
            pltpu.SemaphoreType.DMA((16,)),
            pltpu.SemaphoreType.DMA((16,)),
        ],
        compiler_params=pltpu.CompilerParams(
            collective_id=0, has_side_effects=True, vmem_limit_bytes=40 * 1024 * 1024
        ),
    )(
        rows_of(tokens), rows_of(mixed_grad), qkv_weight, out_weight,
        norm_gain.reshape(1, D), norm_bias.reshape(1, D),
    )
    return join(m_out), join(d_out)


def solution(mesh):
    placed = (
        P(None, "lat", "lon", None),
        P("lon", None),
        P("lon", None),
        P(),
        P(),
        P(None, "lat", "lon", None),
    )
    return jax.shard_map(
        functools.partial(per_device, mesh.shape["lat"], mesh.shape["lon"]),
        mesh=mesh,
        in_specs=placed,
        out_specs=(P(None, "lat", "lon", None), P(None, "lat", "lon", None)),
        check_vma=False,
    )
```

```python
import functools

import jax
import jax.numpy as jnp
from jax import lax
from jax.experimental import pallas as pl
from jax.experimental.pallas import tpu as pltpu
from jax.sharding import PartitionSpec as P

MESH = pl.DeviceIdType.MESH
BF = jnp.bfloat16
F32 = jnp.float32

D = 1024
HEADS = 8
HEAD_DIM = 64
LEV = 2
WIN = 12
INNER = 512
HALF = 6
TOK = LEV * WIN * WIN
QUARTER = TOK // 4
GROUP = 4
GW = GROUP * HEAD_DIM
WIDE = GROUP * TOK
ROWS = 32
EPS = 1e-05

HALVES = ((1, 1), (1, 0), (0, 1), (0, 0))


def nt(a, b):
    return lax.dot_general(a, b, (((1,), (1,)), ((), ())), preferred_element_type=F32)


def nn(a, b):
    return lax.dot_general(a, b, (((1,), (0,)), ((), ())), preferred_element_type=F32)


def tn(a, b):
    return lax.dot_general(a, b, (((0,), (0,)), ((), ())), preferred_element_type=F32)


def ds(start, size):
    return pl.ds(pl.multiple_of(start, size), size)


def kernel(
    n_lat, n_lon,
    t_ref, g_ref, wq_ref, wo_ref, gain_hbm, bias_hbm,
    m_out, d_out,
    comb_q, comb_o, wqf, wof, gain_ref, bias_ref, land_t, land_g, xw, gw, packed, heads, attn, agrad, hgrad, pgrad,
    scores, pt, dst, qblk, doblk, wide, mixed, tgrad,
    own_sem, zs, zr, ys, yr, xs, xr, ss, sr, hs, hr,
):
    lat, lon = lax.axis_index("lat"), lax.axis_index("lon")
    nz, ny = n_lon // 2, n_lat // 4
    rq, ro = D // n_lon, INNER // n_lon
    core, par, z = lax.rem(lat, 2), lax.rem(lon, 2), lon // 2
    half, y = lat // (2 * ny), lax.rem(lat // 2, ny)
    lat_lo, lat_hi = lax.rem(lat + n_lat - 1, n_lat), lax.rem(lat + 1, n_lat)
    lon_lo, lon_hi = lax.rem(lon + n_lon - 1, n_lon), lax.rem(lon + 1, n_lon)
    sib = (lat + 1 - 2 * core, lon)
    differ = lax.rem(par + core, 2)
    across = lon + 1 - 2 * par
    x_to = (lax.rem(lat + differ * (n_lat // 2), n_lat), across)
    x_from = (lax.rem(lat + (1 - differ) * (n_lat // 2), n_lat), across)
    west, north, diag = (lat, lon_lo), (lat_lo, lon), (lat_lo, lon_lo)
    east, south, far = (lat, lon_hi), (lat_hi, lon), (lat_hi, lon_hi)

    def offset(yy, e):
        far_pair = e // 2
        size = (1 - far_pair) * (yy + 1) + far_pair * (2 * ny - yy)
        return (1 - 2 * lax.rem(e, 2)) * size

    def z_to(e):
        return (lat, 2 * lax.rem(z + offset(y, e) + nz, nz) + par)

    def source(yy, e):
        return lax.rem(z - offset(yy, e) + nz, nz)

    def y_to(way):
        return ((half * ny + lax.rem(y + 1 - 2 * way + ny, ny)) * 2 + core, lon)

    def line(group, c):
        return lax.rem(y + ny + (0, 2 * c - 1, 1 - 2 * c, 2)[group], ny)

    comb, cut = (comb_q, comb_o), (3 * INNER // 2, D // 2)
    own = [
        ((wq_ref, wo_ref)[b].at[:, c * cut[b] : (c + 1) * cut[b]], comb[b].at[c, par, 0])
        for b in range(2) for c in range(2)
    ]
    own = [pltpu.make_async_copy(src, to, own_sem.at[8 + k]) for k, (src, to) in enumerate(own)]
    for copy in own:
        copy.start()

    barrier = pltpu.get_barrier_semaphore()
    met = [z_to(e) for e in range(4)]
    met += [y_to(0), y_to(1), sib, x_to, x_from, west, north, diag, east, south, far]
    for who in met:
        pl.semaphore_signal(barrier, inc=1, device_id=who, device_id_type=MESH)
    for copy in own:
        copy.wait()
    pl.semaphore_wait(barrier, len(met))

    def remote(src, dst, send, recv, who):
        return pltpu.make_async_remote_copy(
            src_ref=src, dst_ref=dst, send_sem=send, recv_sem=recv, device_id=who, device_id_type=MESH
        )

    def quarter(ref, k):
        i, j = HALVES[k]
        return ref.at[pl.ds(i * HALF, HALF), pl.ds(j * HALF, HALF)]

    def halo_in(field, src, land):
        copies = [
            remote(quarter(src, k), land.at[k], hs.at[field * 4 + k], hr.at[field * 4 + k], who)
            for k, who in ((1, west), (2, north), (3, diag))
        ]
        return copies, pltpu.make_async_copy(quarter(src, 0), land.at[0], own_sem.at[4 + field])

    in_t = halo_in(0, t_ref, land_t)
    in_g = halo_in(1, g_ref, land_g)
    def slots(wave, group, count=1):
        if wave < 2:
            return pl.ds(1 + wave * 8 + group * 2, count * 2)
        return pl.ds(1 + group * 4, count * 4)

    def z_copy(b, e):
        slot = 1 + e if b else 1 + e // 2 * 8 + e % 2
        i = b * 4 + e
        return remote(comb[b].at[core, par, 0], comb[b].at[core, par, slot], zs.at[i], zr.at[i], z_to(e))

    def y_copy(wave, k):
        src, dst = ((0, 1), (0, 2), (1, 3))[k]
        i, buf = wave * 3 + k, comb[wave // 2]
        return remote(
            buf.at[core, par, slots(wave, src)], buf.at[core, par, slots(wave, dst)], ys.at[i], yr.at[i],
            y_to(1 - core if k == 1 else core),
        )

    def x_copy(wave, k, p):
        ref = comb[wave // 2].at[core, p, slots(wave, (0, 1, 3)[k], (1, 2, 1)[k])]
        i = wave * 3 + k
        return remote(ref, ref, xs.at[i], xr.at[i], x_to)

    def x_own(b, p):
        ref = comb[b].at[core, p, 0]
        return remote(ref, ref, xs.at[9 + b], xr.at[9 + b], x_to)

    def s_copy(wave, other, c):
        ref = comb[wave // 2].at[c, lax.rem(par + other, 2), slots(wave, 0, 4)]
        i = wave * 2 + other
        return remote(ref, ref, ss.at[i], sr.at[i], sib)

    def s_own(b, c):
        ref = comb[b].at[c, 1 - par, 0]
        return remote(ref, ref, ss.at[6 + b], sr.at[6 + b], sib)

    def place(wave):
        b = wave // 2
        full, size = ((wqf, rq), (wof, ro))[b]
        for c in range(2):
            found = [] if wave == 1 else [(0, z)]
            for j in range(4):
                for i in range(4 if b else 2):
                    e = i if b else 2 * wave + i
                    found.append((slots(wave, j).start + i, source(line(j, c), e)))
            for slot, zq in found:
                for p in range(2):
                    full[ds((zq * 2 + p) * size, size), c * cut[b] : (c + 1) * cut[b]] = comb[b][c, p, slot]

    local = [
        pltpu.make_async_copy(gain_hbm, gain_ref, own_sem.at[2]),
        pltpu.make_async_copy(bias_hbm, bias_ref, own_sem.at[3]),
        in_t[1],
        in_g[1],
    ]

    def rows_of(land, field):
        def step(t, carry):
            k, i = 2 * (t // 3), 2 * lax.rem(t, 3)
            two = [land[k + n, pl.ds(i, 2)].reshape(24, D) for n in (0, 1)]
            field[ds(t * 48, 48), :] = jnp.concatenate(two, axis=0)
            return carry

        lax.fori_loop(0, 6, step, 0)

    z_copies = [[z_copy(b, e) for e in range(4)] for b in range(2)]
    for copy in z_copies[0]:
        copy.start()
    x_own(0, par).start()
    for copy in local:
        copy.start()

    def from_z(wave):
        b = wave // 2
        for copy in z_copies[1] if b else z_copies[0][2 * wave : 2 * wave + 2]:
            copy.wait_recv()
        for k in range(2):
            y_copy(wave, k).start()
        x_copy(wave, 0, par).start()
        if wave == 0:
            for copy in in_t[0]:
                copy.start()
        if wave == 1:
            for copy in z_copies[1]:
                copy.start()
            x_own(1, par).start()

    def from_y(wave):
        y_copy(wave, 0).wait_recv()
        y_copy(wave, 2).start()
        y_copy(wave, 1).wait_recv()
        x_copy(wave, 1, par).start()

    def from_y2(wave):
        y_copy(wave, 2).wait_recv()
        x_copy(wave, 2, par).start()
        s_copy(wave, 0, core).start()

    def from_x(wave):
        if wave != 1:
            x_own(wave // 2, 1 - par).wait_recv()
            s_own(wave // 2, core).start()
        for k in range(3):
            x_copy(wave, k, 1 - par).wait_recv()
        s_copy(wave, 1, core).start()

    def from_s(wave):
        if wave != 1:
            s_own(wave // 2, 1 - core).wait_recv()
        for other in range(2):
            s_copy(wave, other, 1 - core).wait_recv()
        place(wave)

    from_z(0)
    from_y(0)
    from_z(1)
    from_y2(0)
    from_x(0)
    from_y(1)
    from_y2(1)
    for copy in in_t[0]:
        copy.wait_recv()
    for copy in local:
        copy.wait()
    rows_of(land_t, xw)
    from_s(0)
    from_x(1)
    from_z(2)
    for copy in in_g[0]:
        copy.start()
    from_s(1)
    from_y(2)

    for n in range(3 * INNER // 256):
        cols = slice(n * 256, n * 256 + 256)
        packed[:, cols] = nn(xw[...], wqf[:, cols]).astype(BF)
    from_y2(2)

    lane_head = lax.broadcasted_iota(jnp.int32, (TOK, GW), 1) // HEAD_DIM
    banned = jnp.where(lat == n_lat - 1, -1e30, 0.0).astype(F32)

    def spread(rows):
        return [rows * (lane_head[0:1] == h).astype(F32).astype(BF) for h in range(GROUP)]

    def columns(g):
        return [ds(n * INNER + g * GW, GW) for n in range(3)]

    def turned(block):
        return block.astype(F32).T.astype(BF)

    def narrow(right, left):
        for c in range(0, WIDE, 384):
            wide[:, c : c + 384] = nn(right, left(slice(c, c + 384)))
        blocks = [wide[h * HEAD_DIM : (h + 1) * HEAD_DIM, h * TOK : (h + 1) * TOK] for h in range(GROUP)]
        return jnp.concatenate(blocks, axis=0).T.astype(BF)

    def forward(g, carry):
        q_at, k_at, v_at = columns(g)
        for h, rows in enumerate(spread(packed[:, q_at])):
            qblk[g, h * TOK : (h + 1) * TOK, :] = rows

        for c in range(0, WIDE, 384):
            scores[:, c : c + 384] = nt(packed[:, k_at], qblk[g, c : c + 384, :])
        for c in range(0, WIDE, 128):
            cols = slice(c, c + 128)
            query = lax.rem(c + lax.broadcasted_iota(jnp.int32, (1, 128), 1), TOK)
            side = (query >= TOK // 2).astype(F32)
            s = jnp.concatenate(
                [scores[: TOK // 2, cols] + side * banned, scores[TOK // 2 :, cols] + (1.0 - side) * banned], axis=0
            )
            top = jnp.max(s, axis=0, keepdims=True)
            e = jnp.exp((s - top) * (HEAD_DIM ** -0.5))
            pt[g, :, cols] = (e * (1.0 / jnp.sum(e, axis=0, keepdims=True))).astype(BF)
        heads[:, q_at] = narrow(turned(packed[:, v_at]), lambda cols: pt[g, :, cols])

        @pl.when(g == 0)
        def _():
            from_x(2)

        return carry

    lax.fori_loop(0, HEADS // GROUP, forward, 0)
    from_s(2)

    for n in range(0, D, 256):
        attn[:, n : n + 256] = nn(heads[...], wof[:, n : n + 256]).astype(BF)

    for copy in in_g[0]:
        copy.wait_recv()
    rows_of(land_g, gw)

    def norm(c, carry):
        rows = ds(c * ROWS, ROWS)
        a = attn[rows, :].astype(F32)
        gain = gain_ref[...]
        scaled = gw[rows, :].astype(F32) * gain
        centered = a - jnp.mean(a, axis=-1, keepdims=True)
        level = scaled - jnp.mean(scaled, axis=-1, keepdims=True)
        inverse = lax.rsqrt(jnp.mean(centered * centered, axis=-1, keepdims=True) + EPS)
        along = jnp.mean(scaled * centered, axis=-1, keepdims=True) * inverse
        normed = centered * inverse
        mixed[rows, :] = (xw[rows, :].astype(F32) + normed * gain + bias_ref[...]).astype(BF)
        agrad[rows, :] = ((level - normed * along) * inverse).astype(BF)
        return carry

    lax.fori_loop(0, TOK // ROWS, norm, 0, unroll=3)

    def halo_out(field, rows, land, out):
        def step(t, carry):
            k, i = 2 * (t // 3), 2 * lax.rem(t, 3)
            block = rows[ds(t * 48, 48), :]
            for n in (0, 1):
                land[k + n, pl.ds(i, 2)] = block[n * 24 : (n + 1) * 24].reshape(2, HALF, LEV, D)
            return carry

        lax.fori_loop(0, 6, step, 0)
        copies = [
            remote(land.at[k], quarter(out, k), hs.at[(field + 2) * 4 + k], hr.at[(field + 2) * 4 + k], who)
            for k, who in ((1, east), (2, south), (3, far))
        ]
        keep = pltpu.make_async_copy(land.at[0], quarter(out, 0), own_sem.at[6 + field])
        for copy in copies:
            copy.start()
        keep.start()
        return copies, keep

    out_m = halo_out(0, mixed, land_t, m_out)

    for n in range(0, INNER, 256):
        hgrad[:, n : n + 256] = nt(agrad[...], wof[n : n + 256, :]).astype(BF)

    def backward(g, carry):
        q_at, k_at, v_at = columns(g)
        for h, rows in enumerate(spread(hgrad[:, q_at])):
            doblk[h * TOK : (h + 1) * TOK, :] = rows

        for c in range(0, WIDE, 384):
            scores[:, c : c + 384] = nt(packed[:, v_at], doblk[c : c + 384, :])
        for c in range(0, WIDE, 128):
            cols = slice(c, c + 128)
            p, dp = pt[g, :, cols].astype(F32), scores[:, cols]
            total = jnp.sum(p * dp, axis=0, keepdims=True)
            dst[:, cols] = (p * (dp - total) * (HEAD_DIM ** -0.5)).astype(BF)
        pgrad[:, q_at] = narrow(turned(packed[:, k_at]), lambda cols: dst[:, cols])
        pgrad[:, v_at] = nn(pt[g], doblk[...]).astype(BF)
        pgrad[:, k_at] = nn(dst[...], qblk[g]).astype(BF)
        return carry

    lax.fori_loop(0, HEADS // GROUP, backward, 0)

    for n in range(0, D, 256):
        cols = slice(n, n + 256)
        sg = nt(pgrad[...], wqf[cols, :]).astype(BF).astype(F32)
        tgrad[:, cols] = (gw[:, cols].astype(F32) + sg).astype(BF)
    out_d = halo_out(1, tgrad, land_g, d_out)

    for copy in z_copies[0] + z_copies[1]:
        copy.wait_send()
    for wave in range(3):
        for k in range(3):
            y_copy(wave, k).wait_send()
            x_copy(wave, k, par).wait_send()
        for other in range(2):
            s_copy(wave, other, core).wait_send()
    for b in range(2):
        x_own(b, par).wait_send()
        s_own(b, core).wait_send()
    for copy in in_t[0] + in_g[0]:
        copy.wait_send()
    for copies, keep in (out_m, out_d):
        keep.wait()
        for copy in copies:
            copy.wait()


def per_device(n_lat, n_lon, tokens, qkv_weight, out_weight, norm_gain, norm_bias, mixed_grad):
    hbm = pl.BlockSpec(memory_space=pltpu.HBM)
    cells = (WIN, WIN, LEV, D)
    m_out, d_out = pl.pallas_call(
        functools.partial(kernel, n_lat, n_lon),
        out_shape=[jax.ShapeDtypeStruct(cells, BF)] * 2,
        in_specs=[hbm] * 6,
        out_specs=[pl.BlockSpec(memory_space=pl.ANY)] * 2,
        scratch_shapes=[
            pltpu.VMEM((2, 2, 17, D // n_lon, 3 * INNER // 2), BF),
            pltpu.VMEM((2, 2, 17, INNER // n_lon, D // 2), BF),
            pltpu.VMEM((D, 3 * INNER), BF),
            pltpu.VMEM((INNER, D), BF),
            pltpu.VMEM((1, D), F32),
            pltpu.VMEM((1, D), F32),
            pltpu.VMEM((4, HALF, HALF, LEV, D), BF),
            pltpu.VMEM((4, HALF, HALF, LEV, D), BF),
            pltpu.VMEM((TOK, D), BF),
            pltpu.VMEM((TOK, D), BF),
            pltpu.VMEM((TOK, 3 * INNER), BF),
            pltpu.VMEM((TOK, INNER), BF),
            pltpu.VMEM((TOK, D), BF),
            pltpu.VMEM((TOK, D), BF),
            pltpu.VMEM((TOK, INNER), BF),
            pltpu.VMEM((TOK, 3 * INNER), BF),
            pltpu.VMEM((TOK, WIDE), F32),
            pltpu.VMEM((2, TOK, WIDE), BF),
            pltpu.VMEM((TOK, WIDE), BF),
            pltpu.VMEM((2, WIDE, GW), BF),
            pltpu.VMEM((WIDE, GW), BF),
            pltpu.VMEM((GW, WIDE), F32),
            pltpu.VMEM((TOK, D), BF),
            pltpu.VMEM((TOK, D), BF),
            pltpu.SemaphoreType.DMA((12,)),
            pltpu.SemaphoreType.DMA((8,)),
            pltpu.SemaphoreType.DMA((8,)),
            pltpu.SemaphoreType.DMA((9,)),
            pltpu.SemaphoreType.DMA((9,)),
            pltpu.SemaphoreType.DMA((11,)),
            pltpu.SemaphoreType.DMA((11,)),
            pltpu.SemaphoreType.DMA((8,)),
            pltpu.SemaphoreType.DMA((8,)),
            pltpu.SemaphoreType.DMA((16,)),
            pltpu.SemaphoreType.DMA((16,)),
        ],
        compiler_params=pltpu.CompilerParams(
            collective_id=0, has_side_effects=True, vmem_limit_bytes=63 * 1024 * 1024
        ),
    )(
        tokens.transpose(1, 2, 0, 3), mixed_grad.transpose(1, 2, 0, 3), qkv_weight, out_weight,
        norm_gain.reshape(1, D), norm_bias.reshape(1, D),
    )
    return m_out.transpose(2, 0, 1, 3), d_out.transpose(2, 0, 1, 3)


def solution(mesh):
    placed = (
        P(None, "lat", "lon", None),
        P("lon", None),
        P("lon", None),
        P(),
        P(),
        P(None, "lat", "lon", None),
    )
    return jax.shard_map(
        functools.partial(per_device, mesh.shape["lat"], mesh.shape["lon"]),
        mesh=mesh,
        in_specs=placed,
        out_specs=(P(None, "lat", "lon", None), P(None, "lat", "lon", None)),
        check_vma=False,
    )
```

```python
import functools

import jax
import jax.numpy as jnp
from jax import lax
from jax.experimental import pallas as pl
from jax.experimental.pallas import tpu as pltpu
from jax.sharding import PartitionSpec as P

MESH = pl.DeviceIdType.MESH
BF = jnp.bfloat16
F32 = jnp.float32

D = 1024
HEADS = 8
HEAD_DIM = 64
LEV = 2
WIN = 12
INNER = 512
HALF = 6
TOK = LEV * WIN * WIN
QUARTER = TOK // 4
GROUP = 4
GW = GROUP * HEAD_DIM
WIDE = GROUP * TOK
ROWS = 32
EPS = 1e-05

HALVES = ((1, 1), (1, 0), (0, 1), (0, 0))


def nt(a, b):
    return lax.dot_general(a, b, (((1,), (1,)), ((), ())), preferred_element_type=F32)


def nn(a, b):
    return lax.dot_general(a, b, (((1,), (0,)), ((), ())), preferred_element_type=F32)


def tn(a, b):
    return lax.dot_general(a, b, (((0,), (0,)), ((), ())), preferred_element_type=F32)


def ds(start, size):
    return pl.ds(pl.multiple_of(start, size), size)


def kernel(
    n_lat, n_lon,
    t_ref, g_ref, wq_ref, wo_ref, gain_hbm, bias_hbm,
    m_out, d_out,
    comb_q, comb_o, wqf, wof, gain_ref, bias_ref, land_t, land_g, xw, gw, packed, heads, attn, agrad, hgrad, pgrad,
    scores, pt, dst, qblk, doblk, wide, mixed, tgrad,
    own_sem, zs, zr, ys, yr, xs, xr, ss, sr, hs, hr,
):
    lat, lon = lax.axis_index("lat"), lax.axis_index("lon")
    nz, ny = n_lon // 2, n_lat // 4
    rq, ro = D // n_lon, INNER // n_lon
    core, par, z = lax.rem(lat, 2), lax.rem(lon, 2), lon // 2
    half, y = lat // (2 * ny), lax.rem(lat // 2, ny)
    lat_lo, lat_hi = lax.rem(lat + n_lat - 1, n_lat), lax.rem(lat + 1, n_lat)
    lon_lo, lon_hi = lax.rem(lon + n_lon - 1, n_lon), lax.rem(lon + 1, n_lon)
    sib = (lat + 1 - 2 * core, lon)
    differ = lax.rem(par + core, 2)
    across = lon + 1 - 2 * par
    x_to = (lax.rem(lat + differ * (n_lat // 2), n_lat), across)
    x_from = (lax.rem(lat + (1 - differ) * (n_lat // 2), n_lat), across)
    west, north, diag = (lat, lon_lo), (lat_lo, lon), (lat_lo, lon_lo)
    east, south, far = (lat, lon_hi), (lat_hi, lon), (lat_hi, lon_hi)

    def offset(yy, e):
        far_pair = e // 2
        size = (1 - far_pair) * (yy + 1) + far_pair * (2 * ny - yy)
        return (1 - 2 * lax.rem(e, 2)) * size

    def z_to(e):
        return (lat, 2 * lax.rem(z + offset(y, e) + nz, nz) + par)

    def source(yy, e):
        return lax.rem(z - offset(yy, e) + nz, nz)

    def y_to(way):
        return ((half * ny + lax.rem(y + 1 - 2 * way + ny, ny)) * 2 + core, lon)

    def line(group, c):
        return lax.rem(y + ny + (0, 2 * c - 1, 1 - 2 * c, 2)[group], ny)

    comb, cut = (comb_q, comb_o), (3 * INNER // 2, D // 2)
    own = [
        ((wq_ref, wo_ref)[b].at[:, c * cut[b] : (c + 1) * cut[b]], comb[b].at[c, par, 0])
        for b in range(2) for c in range(2)
    ]
    own = [pltpu.make_async_copy(src, to, own_sem.at[8 + k]) for k, (src, to) in enumerate(own)]
    for copy in own:
        copy.start()

    barrier = pltpu.get_barrier_semaphore()
    met = [z_to(e) for e in range(4)]
    met += [y_to(0), y_to(1), sib, x_to, x_from, west, north, diag, east, south, far]
    for who in met:
        pl.semaphore_signal(barrier, inc=1, device_id=who, device_id_type=MESH)
    for copy in own:
        copy.wait()
    pl.semaphore_wait(barrier, len(met))

    def remote(src, dst, send, recv, who):
        return pltpu.make_async_remote_copy(
            src_ref=src, dst_ref=dst, send_sem=send, recv_sem=recv, device_id=who, device_id_type=MESH
        )

    def quarter(ref, k):
        i, j = HALVES[k]
        return ref.at[pl.ds(i * HALF, HALF), pl.ds(j * HALF, HALF)]

    def halo_in(field, src, land):
        copies = [
            remote(quarter(src, k), land.at[k], hs.at[field * 4 + k], hr.at[field * 4 + k], who)
            for k, who in ((1, west), (2, north), (3, diag))
        ]
        return copies, pltpu.make_async_copy(quarter(src, 0), land.at[0], own_sem.at[4 + field])

    in_t = halo_in(0, t_ref, land_t)
    in_g = halo_in(1, g_ref, land_g)
    def slots(wave, group, count=1):
        if wave < 2:
            return pl.ds(1 + wave * 8 + group * 2, count * 2)
        return pl.ds(1 + group * 4, count * 4)

    def z_copy(b, e):
        slot = 1 + e if b else 1 + e // 2 * 8 + e % 2
        i = b * 4 + e
        return remote(comb[b].at[core, par, 0], comb[b].at[core, par, slot], zs.at[i], zr.at[i], z_to(e))

    def y_copy(wave, k):
        src, dst = ((0, 1), (0, 2), (1, 3))[k]
        i, buf = wave * 3 + k, comb[wave // 2]
        return remote(
            buf.at[core, par, slots(wave, src)], buf.at[core, par, slots(wave, dst)], ys.at[i], yr.at[i],
            y_to(1 - core if k == 1 else core),
        )

    def x_copy(wave, k, p):
        ref = comb[wave // 2].at[core, p, slots(wave, (0, 1, 3)[k], (1, 2, 1)[k])]
        i = wave * 3 + k
        return remote(ref, ref, xs.at[i], xr.at[i], x_to)

    def x_own(b, p):
        ref = comb[b].at[core, p, 0]
        return remote(ref, ref, xs.at[9 + b], xr.at[9 + b], x_to)

    def s_copy(wave, c):
        ref = comb[wave // 2].at[c, :, slots(wave, 0, 4)]
        return remote(ref, ref, ss.at[wave], sr.at[wave], sib)

    def s_own(b, c):
        ref = comb[b].at[c, 1 - par, 0]
        return remote(ref, ref, ss.at[3 + b], sr.at[3 + b], sib)

    def place(wave):
        b = wave // 2
        full, size = ((wqf, rq), (wof, ro))[b]
        for c in range(2):
            found = [] if wave == 1 else [(0, z)]
            for j in range(4):
                for i in range(4 if b else 2):
                    e = i if b else 2 * wave + i
                    found.append((slots(wave, j).start + i, source(line(j, c), e)))
            for slot, zq in found:
                for p in range(2):
                    full[ds((zq * 2 + p) * size, size), c * cut[b] : (c + 1) * cut[b]] = comb[b][c, p, slot]

    local = [
        pltpu.make_async_copy(gain_hbm, gain_ref, own_sem.at[2]),
        pltpu.make_async_copy(bias_hbm, bias_ref, own_sem.at[3]),
        in_t[1],
        in_g[1],
    ]

    def rows_of(land, field):
        def step(t, carry):
            k, i = 2 * (t // 3), 2 * lax.rem(t, 3)
            two = [land[k + n, pl.ds(i, 2)].reshape(24, D) for n in (0, 1)]
            field[ds(t * 48, 48), :] = jnp.concatenate(two, axis=0)
            return carry

        lax.fori_loop(0, 6, step, 0)

    z_copies = [[z_copy(b, e) for e in range(4)] for b in range(2)]
    for copy in z_copies[0][:2]:
        copy.start()
    x_own(0, par).start()
    for copy in local:
        copy.start()

    def from_z(wave):
        b = wave // 2
        for copy in z_copies[1] if b else z_copies[0][2 * wave : 2 * wave + 2]:
            copy.wait_recv()
        if wave == 0:
            for copy in z_copies[0][2:]:
                copy.start()
        y_copy(wave, 0).start()
        y_copy(wave, 1).start()
        x_copy(wave, 0, par).start()
        if wave == 0:
            for copy in in_t[0]:
                copy.start()
        if wave == 1:
            for copy in z_copies[1]:
                copy.start()
            x_own(1, par).start()

    def from_y(wave):
        y_copy(wave, 0).wait_recv()
        y_copy(wave, 2).start()
        y_copy(wave, 1).wait_recv()
        x_copy(wave, 1, par).start()

    def from_y2(wave):
        y_copy(wave, 2).wait_recv()
        x_copy(wave, 2, par).start()

    def from_x(wave):
        if wave != 1:
            x_own(wave // 2, 1 - par).wait_recv()
            s_own(wave // 2, core).start()
        for k in range(3):
            x_copy(wave, k, 1 - par).wait_recv()
        s_copy(wave, core).start()

    def from_s(wave):
        if wave != 1:
            s_own(wave // 2, 1 - core).wait_recv()
        s_copy(wave, 1 - core).wait_recv()
        place(wave)

    from_z(0)
    from_y(0)
    from_y2(0)
    from_z(1)
    from_x(0)
    from_y(1)
    from_y2(1)
    for copy in in_t[0]:
        copy.wait_recv()
    for copy in local:
        copy.wait()
    rows_of(land_t, xw)
    from_s(0)
    from_x(1)
    from_z(2)
    for copy in in_g[0]:
        copy.start()
    from_s(1)
    from_y(2)

    for n in range(3 * INNER // 256):
        cols = slice(n * 256, n * 256 + 256)
        packed[:, cols] = nn(xw[...], wqf[:, cols]).astype(BF)
    from_y2(2)

    lane_head = lax.broadcasted_iota(jnp.int32, (TOK, GW), 1) // HEAD_DIM
    banned = jnp.where(lat == n_lat - 1, -1e30, 0.0).astype(F32)

    def spread(rows):
        return [rows * (lane_head[0:1] == h).astype(F32).astype(BF) for h in range(GROUP)]

    def columns(g):
        return [ds(n * INNER + g * GW, GW) for n in range(3)]

    def turned(block):
        return block.astype(F32).T.astype(BF)

    def narrow(right, left):
        for c in range(0, WIDE, 384):
            wide[:, c : c + 384] = nn(right, left(slice(c, c + 384)))
        blocks = [wide[h * HEAD_DIM : (h + 1) * HEAD_DIM, h * TOK : (h + 1) * TOK] for h in range(GROUP)]
        return jnp.concatenate(blocks, axis=0).T.astype(BF)

    def forward(g, carry):
        q_at, k_at, v_at = columns(g)
        for h, rows in enumerate(spread(packed[:, q_at])):
            qblk[g, h * TOK : (h + 1) * TOK, :] = rows

        for c in range(0, WIDE, 384):
            scores[:, c : c + 384] = nt(packed[:, k_at], qblk[g, c : c + 384, :])
        for c in range(0, WIDE, 128):
            cols = slice(c, c + 128)
            query = lax.rem(c + lax.broadcasted_iota(jnp.int32, (1, 128), 1), TOK)
            side = (query >= TOK // 2).astype(F32)
            s = jnp.concatenate(
                [scores[: TOK // 2, cols] + side * banned, scores[TOK // 2 :, cols] + (1.0 - side) * banned], axis=0
            )
            top = jnp.max(s, axis=0, keepdims=True)
            e = jnp.exp((s - top) * (HEAD_DIM ** -0.5))
            pt[g, :, cols] = (e * (1.0 / jnp.sum(e, axis=0, keepdims=True))).astype(BF)
        heads[:, q_at] = narrow(turned(packed[:, v_at]), lambda cols: pt[g, :, cols])

        @pl.when(g == 0)
        def _():
            from_x(2)

        return carry

    lax.fori_loop(0, HEADS // GROUP, forward, 0)
    from_s(2)

    for n in range(0, D, 256):
        attn[:, n : n + 256] = nn(heads[...], wof[:, n : n + 256]).astype(BF)

    for copy in in_g[0]:
        copy.wait_recv()
    rows_of(land_g, gw)

    def norm(c, carry):
        rows = ds(c * ROWS, ROWS)
        a = attn[rows, :].astype(F32)
        gain = gain_ref[...]
        scaled = gw[rows, :].astype(F32) * gain
        centered = a - jnp.mean(a, axis=-1, keepdims=True)
        level = scaled - jnp.mean(scaled, axis=-1, keepdims=True)
        inverse = lax.rsqrt(jnp.mean(centered * centered, axis=-1, keepdims=True) + EPS)
        along = jnp.mean(scaled * centered, axis=-1, keepdims=True) * inverse
        normed = centered * inverse
        mixed[rows, :] = (xw[rows, :].astype(F32) + normed * gain + bias_ref[...]).astype(BF)
        agrad[rows, :] = ((level - normed * along) * inverse).astype(BF)
        return carry

    lax.fori_loop(0, TOK // ROWS, norm, 0, unroll=3)

    def halo_out(field, rows, land, out):
        def step(t, carry):
            k, i = 2 * (t // 3), 2 * lax.rem(t, 3)
            block = rows[ds(t * 48, 48), :]
            for n in (0, 1):
                land[k + n, pl.ds(i, 2)] = block[n * 24 : (n + 1) * 24].reshape(2, HALF, LEV, D)
            return carry

        lax.fori_loop(0, 6, step, 0)
        copies = [
            remote(land.at[k], quarter(out, k), hs.at[(field + 2) * 4 + k], hr.at[(field + 2) * 4 + k], who)
            for k, who in ((1, east), (2, south), (3, far))
        ]
        keep = pltpu.make_async_copy(land.at[0], quarter(out, 0), own_sem.at[6 + field])
        for copy in copies:
            copy.start()
        keep.start()
        return copies, keep

    out_m = halo_out(0, mixed, land_t, m_out)

    for n in range(0, INNER, 256):
        hgrad[:, n : n + 256] = nt(agrad[...], wof[n : n + 256, :]).astype(BF)

    def backward(g, carry):
        q_at, k_at, v_at = columns(g)
        for h, rows in enumerate(spread(hgrad[:, q_at])):
            doblk[h * TOK : (h + 1) * TOK, :] = rows

        for c in range(0, WIDE, 384):
            scores[:, c : c + 384] = nt(packed[:, v_at], doblk[c : c + 384, :])
        for c in range(0, WIDE, 128):
            cols = slice(c, c + 128)
            p, dp = pt[g, :, cols].astype(F32), scores[:, cols]
            total = jnp.sum(p * dp, axis=0, keepdims=True)
            dst[:, cols] = (p * (dp - total) * (HEAD_DIM ** -0.5)).astype(BF)
        pgrad[:, q_at] = narrow(turned(packed[:, k_at]), lambda cols: dst[:, cols])
        pgrad[:, v_at] = nn(pt[g], doblk[...]).astype(BF)
        pgrad[:, k_at] = nn(dst[...], qblk[g]).astype(BF)
        return carry

    lax.fori_loop(0, HEADS // GROUP, backward, 0)

    for n in range(0, D, 256):
        cols = slice(n, n + 256)
        sg = nt(pgrad[...], wqf[cols, :]).astype(BF).astype(F32)
        tgrad[:, cols] = (gw[:, cols].astype(F32) + sg).astype(BF)
    out_d = halo_out(1, tgrad, land_g, d_out)

    for copy in z_copies[0] + z_copies[1]:
        copy.wait_send()
    for wave in range(3):
        for k in range(3):
            y_copy(wave, k).wait_send()
            x_copy(wave, k, par).wait_send()
        s_copy(wave, core).wait_send()
    for b in range(2):
        x_own(b, par).wait_send()
        s_own(b, core).wait_send()
    for copy in in_t[0] + in_g[0]:
        copy.wait_send()
    for copies, keep in (out_m, out_d):
        keep.wait()
        for copy in copies:
            copy.wait()


def per_device(n_lat, n_lon, tokens, qkv_weight, out_weight, norm_gain, norm_bias, mixed_grad):
    hbm = pl.BlockSpec(memory_space=pltpu.HBM)
    cells = (WIN, WIN, LEV, D)
    m_out, d_out = pl.pallas_call(
        functools.partial(kernel, n_lat, n_lon),
        out_shape=[jax.ShapeDtypeStruct(cells, BF)] * 2,
        in_specs=[hbm] * 6,
        out_specs=[pl.BlockSpec(memory_space=pl.ANY)] * 2,
        scratch_shapes=[
            pltpu.VMEM((2, 2, 17, D // n_lon, 3 * INNER // 2), BF),
            pltpu.VMEM((2, 2, 17, INNER // n_lon, D // 2), BF),
            pltpu.VMEM((D, 3 * INNER), BF),
            pltpu.VMEM((INNER, D), BF),
            pltpu.VMEM((1, D), F32),
            pltpu.VMEM((1, D), F32),
            pltpu.VMEM((4, HALF, HALF, LEV, D), BF),
            pltpu.VMEM((4, HALF, HALF, LEV, D), BF),
            pltpu.VMEM((TOK, D), BF),
            pltpu.VMEM((TOK, D), BF),
            pltpu.VMEM((TOK, 3 * INNER), BF),
            pltpu.VMEM((TOK, INNER), BF),
            pltpu.VMEM((TOK, D), BF),
            pltpu.VMEM((TOK, D), BF),
            pltpu.VMEM((TOK, INNER), BF),
            pltpu.VMEM((TOK, 3 * INNER), BF),
            pltpu.VMEM((TOK, WIDE), F32),
            pltpu.VMEM((2, TOK, WIDE), BF),
            pltpu.VMEM((TOK, WIDE), BF),
            pltpu.VMEM((2, WIDE, GW), BF),
            pltpu.VMEM((WIDE, GW), BF),
            pltpu.VMEM((GW, WIDE), F32),
            pltpu.VMEM((TOK, D), BF),
            pltpu.VMEM((TOK, D), BF),
            pltpu.SemaphoreType.DMA((12,)),
            pltpu.SemaphoreType.DMA((8,)),
            pltpu.SemaphoreType.DMA((8,)),
            pltpu.SemaphoreType.DMA((9,)),
            pltpu.SemaphoreType.DMA((9,)),
            pltpu.SemaphoreType.DMA((11,)),
            pltpu.SemaphoreType.DMA((11,)),
            pltpu.SemaphoreType.DMA((5,)),
            pltpu.SemaphoreType.DMA((5,)),
            pltpu.SemaphoreType.DMA((16,)),
            pltpu.SemaphoreType.DMA((16,)),
        ],
        compiler_params=pltpu.CompilerParams(
            collective_id=0, has_side_effects=True, vmem_limit_bytes=63 * 1024 * 1024
        ),
    )(
        tokens.transpose(1, 2, 0, 3), mixed_grad.transpose(1, 2, 0, 3), qkv_weight, out_weight,
        norm_gain.reshape(1, D), norm_bias.reshape(1, D),
    )
    return m_out.transpose(2, 0, 1, 3), d_out.transpose(2, 0, 1, 3)


def solution(mesh):
    placed = (
        P(None, "lat", "lon", None),
        P("lon", None),
        P("lon", None),
        P(),
        P(),
        P(None, "lat", "lon", None),
    )
    return jax.shard_map(
        functools.partial(per_device, mesh.shape["lat"], mesh.shape["lon"]),
        mesh=mesh,
        in_specs=placed,
        out_specs=(P(None, "lat", "lon", None), P(None, "lat", "lon", None)),
        check_vma=False,
    )
```
